128 devices in a mesh: sx: 16 (over x, y), sy: 8 (over z, core).
Axes of the slice: x: 4, y: 4, z: 4, core: 2. Of those that a mesh axis runs over, the one named last changes fastest.
Arguments:
- panels: bfloat16 [128, 384, 400], P(('sx', 'sy')), may hold values from -0.3125 to 0.3125
- coupling: bfloat16 [1024, 2, 384, 384], P(('sx', 'sy')), may hold values from -6 to 6
- partner: int32 [1024], P(('sx', 'sy')), may hold values from 0 to 23, as said below
- counts: int32 [1024], P(('sx', 'sy')), may hold values from 48 to 384
Outputs:
- pair_blocks: bfloat16 [1024, 2, 400, 400], P(('sx', 'sy'))
- partner_blocks: float32 [128, 2, 400, 400], P(('sx', 'sy'))
The draws below stay inside these ranges and needn't reach their ends.
Inputs may be any that keep to these rules, and one draw needn't show every extreme that they name: `partner`: A code below 16 names the substructure with that sx index in the first substructure's sy column; a code c of 16 or more names the one with sy index c - 16 in its sx row; a pair never names its own first substructure.
All inputs are finite; a program needn't handle non-finite values.
Results may differ from the reference program's by a relative error of at most 0.014.
Values may be sent and summed in bfloat16 or wider, within the bound.
No kernel may reach another device: no remote copies, remote signals or barrier semaphores. Data moves between devices by JAX's collectives and lax.ppermute only.
A program may use at most 192 MiB of HBM per device.

```python
import jax
import jax.numpy as jnp
from jax import lax

M = 400
B = 384
P_DEV = 8
SPAN_X = 16
SPAN_Y = 8
SUBS = 128
PAIRS = 1024


def draw_partner(key, part):
    index = jnp.arange(PAIRS, dtype=jnp.int32)
    host = index // P_DEV
    own_x = host // SPAN_Y
    own_y = host % SPAN_Y
    value = jax.random.randint(key, (PAIRS,), 0, SPAN_X + SPAN_Y - 2, dtype=jnp.int32)
    along_x = value < SPAN_X - 1
    code_x = value + (value >= own_x).astype(jnp.int32)
    shifted = value - (SPAN_X - 1)
    code_y = SPAN_X + shifted + (shifted >= own_y).astype(jnp.int32)
    return jnp.where(along_x, code_x, code_y).astype(jnp.int32)


def plant(entries, stream_key, low, top_value):
    extent = entries.shape
    place = [jax.random.randint(jax.random.fold_in(stream_key, axis), (), 0, extent[axis]) for axis in range(len(extent))]
    entries = entries.at[tuple(place)].set(low)
    longest = extent.index(max(extent))
    place[longest] = (place[longest] + 1) % extent[longest]
    return entries.at[tuple(place)].set(top_value)


def steps_of(rng, dims, cuts, least, top_value):
    def one(axis_at, parts):
        draws = jax.random.uniform(jax.random.fold_in(jax.random.fold_in(rng, 6), axis_at), (parts,), jnp.float32, least / len(cuts), top_value / len(cuts))
        return jnp.repeat(jnp.exp(draws), dims[axis_at] // parts).reshape((-1,) + (1,) * (len(dims) - axis_at - 1))

    loudness = one(*cuts[0])
    for cut in cuts[1:]:
        loudness = loudness * one(*cut)
    return loudness


def bell_draw(rng, shape, scale, limit, pieces=(), kind=jnp.bfloat16):
    values = jax.random.normal(rng, shape, jnp.float32) * scale
    if len(pieces) > 0:
        values = steps_of(rng, shape, pieces, -0.22, 0.18) * values
    return jnp.clip(values, min=-limit, max=limit).astype(kind)


def setup_inputs(seed: int = 0) -> dict:
    seeds = jax.random.split(jax.random.key(seed), 5)
    return {
        "panels": bell_draw(seeds[0], (SUBS, B, M), B ** -0.5, 0.3125, ((0, 128),)),
        "coupling": bell_draw(seeds[1], (PAIRS, 2, B, B), 1.0, 6.0, ((0, 128),)),
        "partner": draw_partner(jax.random.fold_in(seeds[4], 71), 0),
        "counts": plant(jax.random.randint(seeds[3], (PAIRS,), B // 8, B + 1), jax.random.fold_in(seeds[3], 1), B // 8, B).astype(jnp.int32),
    }


def reference(panels, coupling, partner, counts):
    subs = panels.shape[0]
    npairs = partner.shape[0]
    per_host = npairs // subs
    width = coupling.shape[2]
    modes = panels.shape[2]
    index = jnp.arange(npairs, dtype=jnp.int32)
    left = (index // per_host).astype(jnp.int32)
    left_x = left // SPAN_Y
    left_y = left % SPAN_Y
    right = jnp.where(partner < SPAN_X, partner * SPAN_Y + left_y, left_x * SPAN_Y + (partner - SPAN_X)).astype(jnp.int32)
    rowpos = jnp.arange(width, dtype=jnp.int32)

    def step(total, item):
        block, count, first, second = item
        keep = (rowpos[:, None] < count) & (rowpos[None, :] < count)
        masked = jnp.where(keep[None], block, jnp.zeros_like(block))
        own = lax.dynamic_index_in_dim(panels, first, 0, keepdims=False)
        other = lax.dynamic_index_in_dim(panels, second, 0, keepdims=False)
        left_product = jnp.einsum("bm,tbk->tmk", own.astype(jnp.float32), masked.astype(jnp.float32)).astype(jnp.bfloat16)
        full = jnp.einsum("tmb,bn->tmn", left_product.astype(jnp.float32), other.astype(jnp.float32))
        total = total.at[second].add(jnp.transpose(full, (0, 2, 1)))
        return total, full.astype(jnp.bfloat16)

    start = jnp.zeros((subs, 2, modes, modes), jnp.float32)
    total, blocks = lax.scan(step, start, (coupling, counts, left, right))
    return blocks, total
```

```python
import functools

import jax
import jax.numpy as jnp
from jax import lax
from jax.experimental import pallas as pl
from jax.experimental.pallas import tpu as pltpu
from jax.sharding import PartitionSpec as P


def left_kernel(along_ref, slot_ref, first_ref, used_x_ref, used_y_ref, counts_ref,
                own_ref, coupling_ref, left_ref, slots_x_ref, slots_y_ref):
    p = pl.program_id(0)
    span_x, span_y = slots_x_ref.shape[0], slots_y_ref.shape[0]

    @pl.when(p == 0)
    def _():
        for ref, used, span in ((slots_x_ref, used_x_ref, span_x), (slots_y_ref, used_y_ref, span_y)):
            @pl.loop(0, span)
            def _(k):
                @pl.when(used[k] == 0)
                def _():
                    ref[k] = jnp.zeros(ref.shape[1:], ref.dtype)

    count = counts_ref[p]
    width = coupling_ref.shape[-1]
    rows = lax.broadcasted_iota(jnp.int32, (width, width), 0)
    cols = lax.broadcasted_iota(jnp.int32, (width, width), 1)
    keep = (rows < count) & (cols < count)
    slot = slot_ref[p]
    for t in range(2):
        block = jnp.where(keep, coupling_ref[0, t], jnp.zeros((width, width), coupling_ref.dtype))
        product = jnp.dot(own_ref[...], block, preferred_element_type=jnp.float32).astype(jnp.bfloat16)
        left_ref[0, t] = product
        for ref, mine in ((slots_x_ref, 1), (slots_y_ref, 0)):
            @pl.when((along_ref[p] == mine) & (first_ref[p] == 1))
            def _():
                ref[slot, t] = product

            @pl.when((along_ref[p] == mine) & (first_ref[p] == 0))
            def _():
                ref[slot, t] = (
                    ref[slot, t].astype(jnp.float32) + product.astype(jnp.float32)
                ).astype(jnp.bfloat16)


def left_products(own, coupling, along, slot, first, used_x, used_y, counts):
    pairs, blocks, width, _ = coupling.shape
    modes = own.shape[0]
    span_x, span_y = used_x.shape[0], used_y.shape[0]
    return pl.pallas_call(
        left_kernel,
        grid_spec=pltpu.PrefetchScalarGridSpec(
            num_scalar_prefetch=6,
            grid=(pairs,),
            in_specs=[
                pl.BlockSpec((modes, width), lambda p, *_: (0, 0)),
                pl.BlockSpec((1, blocks, width, width), lambda p, *_: (p, 0, 0, 0)),
            ],
            out_specs=[
                pl.BlockSpec((1, blocks, modes, width), lambda p, *_: (p, 0, 0, 0)),
                pl.BlockSpec((span_x, blocks, modes, width), lambda p, *_: (0, 0, 0, 0),
                             pipeline_mode=pl.Buffered(1)),
                pl.BlockSpec((span_y, blocks, modes, width), lambda p, *_: (0, 0, 0, 0),
                             pipeline_mode=pl.Buffered(1)),
            ],
        ),
        out_shape=[
            jax.ShapeDtypeStruct((pairs, blocks, modes, width), jnp.bfloat16),
            jax.ShapeDtypeStruct((span_x, blocks, modes, width), jnp.bfloat16),
            jax.ShapeDtypeStruct((span_y, blocks, modes, width), jnp.bfloat16),
        ],
        compiler_params=pltpu.CompilerParams(vmem_limit_bytes=40 * 2**20),
        cost_estimate=pl.CostEstimate(flops=2 * pairs * blocks * modes * width * width,
                                      bytes_accessed=30 * 10**6, transcendentals=0),
    )(along, slot, first, used_x, used_y, counts, own, coupling)


def nt(a, b):
    return lax.dot_general(a, b, (((1,), (1,)), ((), ())), preferred_element_type=jnp.float32)


def pair_kernel(along_ref, ix_ref, iy_ref, left_ref, rx_ref, ry_ref, out_ref):
    p = pl.program_id(0)
    for mine, ref in ((1, rx_ref), (0, ry_ref)):
        @pl.when(along_ref[p] == mine)
        def _():
            for t in range(2):
                out_ref[0, t] = nt(left_ref[0, t], ref[0]).astype(jnp.bfloat16)


def pair_products(left, rx, ry, along, ix, iy):
    pairs, blocks, modes, width = left.shape
    return pl.pallas_call(
        pair_kernel,
        grid_spec=pltpu.PrefetchScalarGridSpec(
            num_scalar_prefetch=3,
            grid=(pairs,),
            in_specs=[
                pl.BlockSpec((1, blocks, modes, width), lambda p, *_: (p, 0, 0, 0)),
                pl.BlockSpec((1, modes, width), lambda p, a, ix, iy: (ix[p], 0, 0)),
                pl.BlockSpec((1, modes, width), lambda p, a, ix, iy: (iy[p], 0, 0)),
            ],
            out_specs=pl.BlockSpec((1, blocks, modes, modes), lambda p, *_: (p, 0, 0, 0)),
        ),
        out_shape=jax.ShapeDtypeStruct((pairs, blocks, modes, modes), jnp.bfloat16),
        compiler_params=pltpu.CompilerParams(vmem_limit_bytes=24 * 2**20),
        cost_estimate=pl.CostEstimate(flops=2 * pairs * blocks * modes * width * modes,
                                      bytes_accessed=15 * 10**6, transcendentals=0),
    )(along, ix, iy, left, rx, ry)


def partner_kernel(own_ref, gx_ref, gy_ref, out_ref):
    for t in range(2):
        total = (gx_ref[t].astype(jnp.float32) + gy_ref[t].astype(jnp.float32)).astype(jnp.bfloat16)
        out_ref[t] = nt(own_ref[...], total)


def partner_products(own, gx, gy):
    blocks, modes, width = gx.shape
    return pl.pallas_call(
        partner_kernel,
        out_shape=jax.ShapeDtypeStruct((blocks, modes, modes), jnp.float32),
        compiler_params=pltpu.CompilerParams(vmem_limit_bytes=16 * 2**20),
    )(own, gx, gy)


def body(panels, coupling, partner, counts):
    span_x, span_y = lax.axis_size("sx"), lax.axis_size("sy")
    own = jnp.swapaxes(panels[0], 0, 1)
    along = (partner < span_x).astype(jnp.int32)
    slot = jnp.where(along == 1, partner, partner - span_x)
    order = jnp.arange(partner.shape[0])
    first = jnp.all((partner[:, None] != partner[None, :]) | (order[None, :] >= order[:, None]), axis=1).astype(jnp.int32)
    used = jnp.any(partner[None, :] == jnp.arange(span_x + span_y)[:, None], axis=1).astype(jnp.int32)
    left, slots_x, slots_y = left_products(
        own, coupling, along, slot, first, used[:span_x], used[span_x:], counts
    )
    ry = lax.all_gather(own, "sy", axis=0)
    rx = lax.all_gather(own, "sx", axis=0)
    gy = lax.psum_scatter(slots_y, "sy", scatter_dimension=0, tiled=True)
    gx = lax.psum_scatter(slots_x, "sx", scatter_dimension=0, tiled=True)
    pair_blocks = pair_products(
        left, rx, ry, along, jnp.where(along == 1, slot, 0), jnp.where(along == 1, 0, slot)
    )
    partner_blocks = partner_products(own, gx[0], gy[0])
    return (pair_blocks, partner_blocks[None])


def solution(mesh):
    placed = (
        P(("sx", "sy"), None, None),
        P(("sx", "sy"), None, None, None),
        P(("sx", "sy")),
        P(("sx", "sy")),
    )
    return jax.shard_map(
        body,
        mesh=mesh,
        in_specs=placed,
        out_specs=(P(("sx", "sy"), None, None, None), P(("sx", "sy"), None, None, None)),
        check_vma=False,
    )
```

```python
import jax
import jax.numpy as jnp
from jax import lax
from jax.experimental import pallas as pl
from jax.experimental.pallas import tpu as pltpu
from jax.sharding import PartitionSpec as P

SIDE = 4
PARTS = ((0, 4), (4, 4), (8, 2), (10, 2), (12, 4))


def slot_of(d1, d2):
    low = d2 < 2
    return jnp.where(
        d1 == 0, 12 + d2,
        jnp.where(d1 == 1, jnp.where(low, 8 + d2, d2),
                  jnp.where(d1 == 2, jnp.where(low, d2, 2 + d2), jnp.where(low, 6 + d2, 8 + d2))))


def offsets(code):
    me = lax.axis_index("sx")
    dx = (code // SIDE - me // SIDE + SIDE) % SIDE
    dy = (code % SIDE - me % SIDE + SIDE) % SIDE
    return dx, dy


def left_kernel(partner_ref, counts_ref, own_ref, coupling_ref, left_ref, *rest):
    outs, (slots_y_ref, slots, used, sems) = rest[:10], rest[10:]
    t, p = pl.program_id(0), pl.program_id(1)
    last = pl.num_programs(1) - 1
    span = SIDE * SIDE
    span_y = slots.shape[0] - span

    @pl.when(p == 0)
    def _():
        @pl.loop(0, span + span_y)
        def _(k):
            used[k] = 0

    modes, width = own_ref.shape
    keep = lax.broadcasted_iota(jnp.int32, (1, width), 1) < counts_ref[p]
    own = jnp.where(keep, own_ref[...], jnp.zeros((modes, width), own_ref.dtype))
    product = jnp.dot(own, coupling_ref[0, 0], preferred_element_type=jnp.float32)
    product = jnp.where(keep, product, 0.0).astype(jnp.bfloat16)
    left_ref[0, 0] = product

    code = partner_ref[p]
    dx, dy = offsets(code)
    slot = jnp.where(code < span, jnp.where(t == 0, slot_of(dx, dy), slot_of(dy, dx)), code)
    fresh = used[slot] == 0

    @pl.when(fresh)
    def _():
        slots[slot, t] = product
        used[slot] = 1

    @pl.when(jnp.logical_not(fresh))
    def _():
        slots[slot, t] = (slots[slot, t].astype(jnp.float32) + product.astype(jnp.float32)).astype(jnp.bfloat16)

    def copies(b):
        return [
            pltpu.make_async_copy(slots.at[pl.ds(at, size), b], outs[5 * b + i], sems.at[5 * b + i])
            for i, (at, size) in enumerate(PARTS)
        ]

    copy_y = pltpu.make_async_copy(slots.at[pl.ds(span, span_y)], slots_y_ref, sems.at[10])

    @pl.when(p == last)
    def _():
        @pl.loop(0, span + span_y)
        def _(k):
            @pl.when(used[k] == 0)
            def _():
                slots[k, t] = jnp.zeros((modes, width), slots.dtype)

        @pl.when(t == 0)
        def _():
            for c in copies(0):
                c.start()

        @pl.when(t == 1)
        def _():
            copy_y.start()
            for c in copies(1):
                c.start()
            for c in copies(0) + copies(1) + [copy_y]:
                c.wait()


def left_products(own, coupling, partner, counts, span_y):
    pairs, blocks, width, _ = coupling.shape
    modes = own.shape[0]
    piece = [jax.ShapeDtypeStruct((size, modes, width), jnp.bfloat16) for _, size in PARTS]
    anywhere = pl.BlockSpec(memory_space=pl.ANY)
    out = pl.pallas_call(
        left_kernel,
        grid_spec=pltpu.PrefetchScalarGridSpec(
            num_scalar_prefetch=2,
            grid=(blocks, pairs),
            in_specs=[
                pl.BlockSpec((modes, width), lambda t, p, *_: (0, 0)),
                pl.BlockSpec((1, 1, width, width), lambda t, p, *_: (p, t, 0, 0)),
            ],
            out_specs=[pl.BlockSpec((1, 1, modes, width), lambda t, p, *_: (p, t, 0, 0))] + [anywhere] * 11,
            scratch_shapes=[
                pltpu.VMEM((SIDE * SIDE + span_y, blocks, modes, width), jnp.bfloat16),
                pltpu.SMEM((SIDE * SIDE + span_y,), jnp.int32),
                pltpu.SemaphoreType.DMA((11,)),
            ],
        ),
        out_shape=[jax.ShapeDtypeStruct((pairs, blocks, modes, width), jnp.bfloat16)] + piece + piece
        + [jax.ShapeDtypeStruct((span_y, blocks, modes, width), jnp.bfloat16)],
        compiler_params=pltpu.CompilerParams(vmem_limit_bytes=24 * 2**20),
        cost_estimate=pl.CostEstimate(flops=2 * pairs * blocks * modes * width * width,
                                      bytes_accessed=25 * 10**6, transcendentals=0),
    )(partner, counts, own, coupling)
    return out[0], out[1:6], out[6:11], out[11]


def nt(a, b):
    return lax.dot_general(a, b, (((1,), (1,)), ((), ())), preferred_element_type=jnp.float32)


def pair_kernel(partner_ref, left_ref, *rest):
    halves, (ry_ref, out_ref, panels, sems) = (rest[:5], rest[5:10]), rest[10:]
    p = pl.program_id(0)
    pairs = panels.shape[0]
    span = SIDE * SIDE
    cut = halves[0][0].shape[1]
    rows = ((0, cut), (cut, panels.shape[1] - cut))

    @pl.when(p == 0)
    def _():
        @pl.loop(0, pairs)
        def _(q):
            code = partner_ref[q]
            dx, dy = offsets(code)

            @pl.when(code >= span)
            def _():
                for h, (at, size) in enumerate(rows):
                    pltpu.make_async_copy(ry_ref.at[code - span, pl.ds(at, size)], panels.at[q, pl.ds(at, size)],
                                          sems.at[q, h]).start()

            for h, (at, size) in enumerate(rows):
                d1, d2 = ((dx, dy), (dy, dx))[h]
                kept, near, far, low, high = halves[h]
                for ref, index, chosen in (
                    (kept, d1, d2 == 0), (near, d1, d2 == 1), (far, d1, d2 == 3),
                    (low, d1, (d2 == 2) & (d1 < 2)), (high, d1 - 2, (d2 == 2) & (d1 >= 2)),
                ):
                    @pl.when((code < span) & chosen)
                    def _():
                        pltpu.make_async_copy(ref.at[index], panels.at[q, pl.ds(at, size)], sems.at[q, h]).start()

    for h, (at, size) in enumerate(rows):
        pltpu.make_async_copy(ry_ref.at[0, pl.ds(at, size)], panels.at[p, pl.ds(at, size)], sems.at[p, h]).wait()
    for t in range(2):
        out_ref[0, t] = nt(left_ref[0, t], panels[p]).astype(jnp.bfloat16)


def pair_products(left, half_a, half_b, ry, partner):
    pairs, blocks, modes, width = left.shape
    anywhere = pl.BlockSpec(memory_space=pl.ANY)
    return pl.pallas_call(
        pair_kernel,
        grid_spec=pltpu.PrefetchScalarGridSpec(
            num_scalar_prefetch=1,
            grid=(pairs,),
            in_specs=[pl.BlockSpec((1, blocks, modes, width), lambda p, *_: (p, 0, 0, 0))] + [anywhere] * 11,
            out_specs=pl.BlockSpec((1, blocks, modes, modes), lambda p, *_: (p, 0, 0, 0)),
            scratch_shapes=[
                pltpu.VMEM((pairs, modes, width), jnp.bfloat16),
                pltpu.SemaphoreType.DMA((pairs, 2)),
            ],
        ),
        out_shape=jax.ShapeDtypeStruct((pairs, blocks, modes, modes), jnp.bfloat16),
        compiler_params=pltpu.CompilerParams(vmem_limit_bytes=16 * 2**20),
        cost_estimate=pl.CostEstimate(flops=2 * pairs * blocks * modes * width * modes,
                                      bytes_accessed=15 * 10**6, transcendentals=0),
    )(partner, left, *half_a, *half_b, ry)


def partner_kernel(own_ref, gy_ref, *rest):
    sums, out_ref = rest[:-1], rest[-1]
    each = len(sums) // 2
    for t in range(2):
        total = gy_ref[t].astype(jnp.float32)
        for ref in sums[t * each:(t + 1) * each]:
            total = total + ref[...].astype(jnp.float32)
        out_ref[t] = nt(own_ref[...], total.astype(jnp.bfloat16))


def partner_products(own, gy, sums):
    blocks, modes, width = gy.shape
    return pl.pallas_call(
        partner_kernel,
        out_shape=jax.ShapeDtypeStruct((blocks, modes, modes), jnp.float32),
        compiler_params=pltpu.CompilerParams(vmem_limit_bytes=16 * 2**20),
    )(own, gy, *sums)


def shift(value, axis, by):
    moved = []
    for x in range(SIDE):
        for y in range(SIDE):
            to = ((x + by) % SIDE * SIDE + y) if axis == 0 else (x * SIDE + (y + by) % SIDE)
            moved.append((x * SIDE + y, to))
    return lax.ppermute(value, "sx", moved)


def gather_half(piece, first):
    second = 1 - first
    kept = jnp.stack([piece] + [shift(piece, first, -d) for d in (1, 2, 3)])
    near = shift(kept, second, -1)
    far = shift(kept, second, 1)
    low = shift(near[:2], second, -1)
    high = shift(far[2:], second, 1)
    return kept, near, far, low, high


def added(*terms):
    return sum(v.astype(jnp.float32) for v in terms).astype(jnp.bfloat16)


def scatter_half(parts, first):
    second = 1 - first
    up, down, pass_up, pass_down, kept = parts
    got_up = shift(up, first, 1)
    got_down = shift(down, first, -1)
    last_up = shift(added(pass_up, got_up[:2]), first, 1)
    last_down = shift(added(pass_down, got_down[:2]), first, -1)
    v = [
        added(kept[0], got_down[2], last_up[0]),
        added(kept[1], got_down[3], last_up[1]),
        added(kept[2], got_up[2], last_down[0]),
        added(kept[3], got_up[3], last_down[1]),
    ]
    return [v[0]] + [shift(v[d], second, d) for d in (1, 2, 3)]


def body(panels, coupling, partner, counts):
    own = jnp.swapaxes(panels[0], 0, 1)
    modes = own.shape[0]
    cut = (modes // 2 + 15) // 16 * 16
    left, parts0, parts1, slots_y = left_products(own, coupling, partner, counts, lax.axis_size("sy"))
    ry = lax.all_gather(own, "sy", axis=0)
    half_a = gather_half(own[:cut], 0)
    half_b = gather_half(own[cut:], 1)
    gy = lax.psum_scatter(slots_y, "sy", scatter_dimension=0, tiled=True)
    sums = scatter_half(parts0, 0) + scatter_half(parts1, 1)
    pair_blocks = pair_products(left, half_a, half_b, ry, partner)
    partner_blocks = partner_products(own, gy[0], sums)
    return (pair_blocks, partner_blocks[None])


def solution(mesh):
    placed = (
        P(("sx", "sy"), None, None),
        P(("sx", "sy"), None, None, None),
        P(("sx", "sy")),
        P(("sx", "sy")),
    )
    return jax.shard_map(
        body,
        mesh=mesh,
        in_specs=placed,
        out_specs=(P(("sx", "sy"), None, None, None), P(("sx", "sy"), None, None, None)),
        check_vma=False,
    )
```

```python
import jax
import jax.numpy as jnp
from jax import lax
from jax.experimental import pallas as pl
from jax.experimental.pallas import tpu as pltpu
from jax.sharding import PartitionSpec as P

SIDE = 4
PARTS = ((0, 4), (4, 4), (8, 2), (10, 2), (12, 4))


def slot_of(d1, d2):
    low = d2 < 2
    return jnp.where(
        d1 == 0, 12 + d2,
        jnp.where(d1 == 1, jnp.where(low, 8 + d2, d2),
                  jnp.where(d1 == 2, jnp.where(low, d2, 2 + d2), jnp.where(low, 6 + d2, 8 + d2))))


def offsets(code):
    me = lax.axis_index("sx")
    dx = (code // SIDE - me // SIDE + SIDE) % SIDE
    dy = (code % SIDE - me % SIDE + SIDE) % SIDE
    return dx, dy


def left_kernel(partner_ref, counts_ref, own_ref, coupling_ref, left_ref, *rest):
    outs, (slots_y_ref, slots, used, sems) = rest[:10], rest[10:]
    t, step = pl.program_id(0), pl.program_id(1)
    last = pl.num_programs(1) - 1
    group = coupling_ref.shape[0]
    span = SIDE * SIDE
    span_y = slots.shape[0] - span
    modes, width = own_ref.shape

    @pl.when(step == 0)
    def _():
        for k in range(span + span_y):
            used[k] = 0

    for i in range(group):
        p = step * group + i
        keep = lax.broadcasted_iota(jnp.int32, (1, width), 1) < counts_ref[p]
        own = jnp.where(keep, own_ref[...], jnp.zeros((modes, width), own_ref.dtype))
        product = jnp.dot(own, coupling_ref[i, 0], preferred_element_type=jnp.float32)
        product = jnp.where(keep, product, 0.0).astype(jnp.bfloat16)
        left_ref[i, 0] = product

        code = partner_ref[p]
        dx, dy = offsets(code)
        slot = jnp.where(code < span, jnp.where(t == 0, slot_of(dx, dy), slot_of(dy, dx)), code)
        fresh = used[slot] == 0

        @pl.when(fresh)
        def _():
            slots[slot, t] = product
            used[slot] = 1

        @pl.when(jnp.logical_not(fresh))
        def _():
            slots[slot, t] = (slots[slot, t].astype(jnp.float32) + product.astype(jnp.float32)).astype(jnp.bfloat16)

    def copies(b):
        return [
            pltpu.make_async_copy(slots.at[pl.ds(at, size), b], outs[5 * b + i], sems.at[5 * b + i])
            for i, (at, size) in enumerate(PARTS)
        ]

    copy_y = pltpu.make_async_copy(slots.at[pl.ds(span, span_y)], slots_y_ref, sems.at[10])

    @pl.when(step == last)
    def _():
        @pl.loop(0, span + span_y)
        def _(k):
            @pl.when(used[k] == 0)
            def _():
                slots[k, t] = jnp.zeros((modes, width), slots.dtype)

        @pl.when(t == 0)
        def _():
            for c in copies(0):
                c.start()

        @pl.when(t == 1)
        def _():
            for c in copies(1):
                c.start()
            copy_y.start()
            for c in copies(0) + copies(1) + [copy_y]:
                c.wait()


def in_hbm(value):
    return pltpu.with_memory_space_constraint(value, pltpu.HBM)


def left_products(own, coupling, partner, counts, span_y):
    pairs, blocks, width, _ = coupling.shape
    modes = own.shape[0]
    group = 4
    piece = [pltpu.HBM((size, modes, width), jnp.bfloat16) for _, size in PARTS]
    anywhere = pl.BlockSpec(memory_space=pltpu.HBM)
    out = pl.pallas_call(
        left_kernel,
        grid_spec=pltpu.PrefetchScalarGridSpec(
            num_scalar_prefetch=2,
            grid=(blocks, pairs // group),
            in_specs=[
                pl.BlockSpec((modes, width), lambda t, p, *_: (0, 0)),
                pl.BlockSpec((group, 1, width, width), lambda t, p, *_: (p, t, 0, 0)),
            ],
            out_specs=[pl.BlockSpec((group, 1, modes, width), lambda t, p, *_: (p, t, 0, 0))] + [anywhere] * 11,
            scratch_shapes=[
                pltpu.VMEM((SIDE * SIDE + span_y, blocks, modes, width), jnp.bfloat16),
                pltpu.SMEM((SIDE * SIDE + span_y,), jnp.int32),
                pltpu.SemaphoreType.DMA((11,)),
            ],
        ),
        out_shape=[pltpu.HBM((pairs, blocks, modes, width), jnp.bfloat16)] + piece + piece
        + [pltpu.HBM((span_y, blocks, modes, width), jnp.bfloat16)],
        compiler_params=pltpu.CompilerParams(vmem_limit_bytes=26 * 2**20),
        cost_estimate=pl.CostEstimate(flops=2 * pairs * blocks * modes * width * width,
                                      bytes_accessed=25 * 10**6, transcendentals=0),
    )(partner, counts, in_hbm(own), in_hbm(coupling))
    return out[0], out[1:6], out[6:11], out[11]


def nt(a, b):
    return lax.dot_general(a, b, (((1,), (1,)), ((), ())), preferred_element_type=jnp.float32)


def pair_kernel(partner_ref, left_ref, *rest):
    halves, (ry_ref, out_ref, panels, sems) = (rest[:5], rest[5:10]), rest[10:]
    step = pl.program_id(0)
    group = out_ref.shape[0]
    pairs = panels.shape[0]
    span = SIDE * SIDE
    cut = halves[0][0].shape[1]
    rows = ((0, cut), (cut, panels.shape[1] - cut))

    @pl.when(step == 0)
    def _():
        @pl.loop(0, pairs)
        def _(q):
            code = partner_ref[q]
            dx, dy = offsets(code)

            @pl.when(code >= span)
            def _():
                for h, (at, size) in enumerate(rows):
                    pltpu.make_async_copy(ry_ref.at[code - span, pl.ds(at, size)], panels.at[q, pl.ds(at, size)],
                                          sems.at[q, h]).start()

            for h, (at, size) in enumerate(rows):
                d1, d2 = ((dx, dy), (dy, dx))[h]
                kept, near, far, low, high = halves[h]
                for ref, index, chosen in (
                    (kept, d1, d2 == 0), (near, d1, d2 == 1), (far, d1, d2 == 3),
                    (low, d1, (d2 == 2) & (d1 < 2)), (high, d1 - 2, (d2 == 2) & (d1 >= 2)),
                ):
                    @pl.when((code < span) & chosen)
                    def _():
                        pltpu.make_async_copy(ref.at[index], panels.at[q, pl.ds(at, size)], sems.at[q, h]).start()

    for i in range(group):
        p = step * group + i
        for h, (at, size) in enumerate(rows):
            pltpu.make_async_copy(ry_ref.at[0, pl.ds(at, size)], panels.at[p, pl.ds(at, size)], sems.at[p, h]).wait()
        for t in range(2):
            out_ref[i, t] = nt(left_ref[i, t], panels[p]).astype(jnp.bfloat16)


def pair_products(left, half_a, half_b, ry, partner):
    pairs, blocks, modes, width = left.shape
    group = 2
    anywhere = pl.BlockSpec(memory_space=pl.ANY)
    return pl.pallas_call(
        pair_kernel,
        grid_spec=pltpu.PrefetchScalarGridSpec(
            num_scalar_prefetch=1,
            grid=(pairs // group,),
            in_specs=[pl.BlockSpec((group, blocks, modes, width), lambda p, *_: (p, 0, 0, 0))] + [anywhere] * 10
            + [pl.BlockSpec(memory_space=pltpu.HBM)],
            out_specs=pl.BlockSpec((group, blocks, modes, modes), lambda p, *_: (p, 0, 0, 0)),
            scratch_shapes=[
                pltpu.VMEM((pairs, modes, width), jnp.bfloat16),
                pltpu.SemaphoreType.DMA((pairs, 2)),
            ],
        ),
        out_shape=jax.ShapeDtypeStruct((pairs, blocks, modes, modes), jnp.bfloat16),
        compiler_params=pltpu.CompilerParams(vmem_limit_bytes=16 * 2**20),
        cost_estimate=pl.CostEstimate(flops=2 * pairs * blocks * modes * width * modes,
                                      bytes_accessed=15 * 10**6, transcendentals=0),
    )(partner, in_hbm(left), *map(in_hbm, half_a), *map(in_hbm, half_b), in_hbm(ry))


def partner_kernel(own_ref, gy_ref, *rest):
    sums, out_ref = rest[:-1], rest[-1]
    each = len(sums) // 2
    for t in range(2):
        total = gy_ref[t].astype(jnp.float32)
        for ref in sums[t * each:(t + 1) * each]:
            total = total + ref[...].astype(jnp.float32)
        out_ref[t] = nt(own_ref[...], total.astype(jnp.bfloat16))


def partner_products(own, gy, sums):
    blocks, modes, width = gy.shape
    return pl.pallas_call(
        partner_kernel,
        out_shape=jax.ShapeDtypeStruct((blocks, modes, modes), jnp.float32),
        compiler_params=pltpu.CompilerParams(vmem_limit_bytes=16 * 2**20),
    )(*map(in_hbm, (own, gy, *sums)))


def shift(value, axis, by):
    moved = []
    for x in range(SIDE):
        for y in range(SIDE):
            to = ((x + by) % SIDE * SIDE + y) if axis == 0 else (x * SIDE + (y + by) % SIDE)
            moved.append((x * SIDE + y, to))
    return lax.ppermute(value, "sx", moved)


def after(value, *others):
    return lax.optimization_barrier((value,) + others)[0]


def added(*terms):
    return sum(v.astype(jnp.float32) for v in terms).astype(jnp.bfloat16)


def body(panels, coupling, partner, counts):
    own = jnp.swapaxes(panels[0], 0, 1)
    modes = own.shape[0]
    cut = (modes // 2 + 15) // 16 * 16
    ry = lax.all_gather(own, "sy", axis=0)

    pieces = (own[:cut], own[cut:])
    near = [[shift(pieces[h], h, -1), shift(pieces[h], h, 1)] for h in range(2)]
    opposite = [shift(pieces[h], h, 2) for h in range(2)]
    kept = [jnp.stack([pieces[h], near[h][0], opposite[h], near[h][1]]) for h in range(2)]

    kept = list(lax.optimization_barrier(tuple(kept)))

    ring = [[shift(kept[h], 1 - h, -1), shift(kept[h], 1 - h, 1)] for h in range(2)]
    left, parts0, parts1, slots_y = left_products(
        own, coupling, partner, after(counts, kept[0], kept[1]), lax.axis_size("sy")
    )
    sent, slots_y, ring = lax.optimization_barrier(
        ([[parts0[0], parts0[1]], [parts1[0], parts1[1]]], slots_y, ring)
    )
    gy = lax.psum_scatter(slots_y, "sy", scatter_dimension=0, tiled=True)

    parts = (parts0, parts1)
    got = [[shift(sent[t][0], t, 1), shift(sent[t][1], t, -1)] for t in range(2)]
    passed = []
    for h in range(2):
        low = shift(after(ring[h][0][:2], got[1 - h][1]), 1 - h, -1)
        high = shift(after(ring[h][1][2:], got[1 - h][0]), 1 - h, 1)
        passed.append([low, high])
    final = [
        [shift(added(parts[t][2], got[t][0][:2]), t, 1), shift(added(parts[t][3], got[t][1][:2]), t, -1)]
        for t in range(2)
    ]
    sums = []
    for t in range(2):
        here = parts[t][4]
        v = [
            added(here[0], got[t][1][2], final[t][0][0]),
            added(here[1], got[t][1][3], final[t][0][1]),
            added(here[2], got[t][0][2], final[t][1][0]),
            added(here[3], got[t][0][3], final[t][1][1]),
        ]
        sums.append(v)
    out = [[sums[t][0]] + [shift(sums[t][d], 1 - t, d) for d in (1, 3, 2)] for t in range(2)]

    halves = [[kept[h], *ring[h], *passed[h]] for h in range(2)]
    waits = [sums[t][d] for t in range(2) for d in (1, 2, 3)]
    pair_blocks = pair_products(left, halves[0], halves[1], ry, after(partner, *waits))
    partner_blocks = partner_products(own, gy[0], out[0] + out[1])
    return (pair_blocks, partner_blocks[None])


def solution(mesh):
    placed = (
        P(("sx", "sy"), None, None),
        P(("sx", "sy"), None, None, None),
        P(("sx", "sy")),
        P(("sx", "sy")),
    )
    return jax.shard_map(
        body,
        mesh=mesh,
        in_specs=placed,
        out_specs=(P(("sx", "sy"), None, None, None), P(("sx", "sy"), None, None, None)),
        check_vma=False,
    )
```

```python
import jax
import jax.numpy as jnp
from jax import lax
from jax.experimental import pallas as pl
from jax.experimental.pallas import tpu as pltpu
from jax.sharding import PartitionSpec as P

SIDE = 4
SPAN_X, SPAN_Y = SIDE * SIDE, 2 * SIDE
PARTS = ((0, 4), (4, 4), (8, 2), (10, 2), (12, 4))
CHUNK = 80


def slot_of(d1, d2):
    if isinstance(d1, int):
        return {0: 12 + d2, 1: 8 + d2 if d2 < 2 else d2, 2: d2 if d2 < 2 else 2 + d2, 3: 6 + d2 if d2 < 2 else 8 + d2}[d1]
    low = d2 < 2
    return jnp.where(
        d1 == 0, 12 + d2,
        jnp.where(d1 == 1, jnp.where(low, 8 + d2, d2),
                  jnp.where(d1 == 2, jnp.where(low, d2, 2 + d2), jnp.where(low, 6 + d2, 8 + d2))))


def place_of(slot):
    for n, (at, size) in enumerate(PARTS):
        if at <= slot < at + size:
            return n, slot - at


def offsets(code):
    me = lax.axis_index("sx")
    dx = (code // SIDE - me // SIDE + SIDE) % SIDE
    dy = (code % SIDE - me % SIDE + SIDE) % SIDE
    return dx, dy


def ring_offset(code):
    me = lax.axis_index("sy")
    other = code - SPAN_X
    return (other // 2 - me // 2 + SIDE) % SIDE, other % 2, me % 2


def left_kernel(partner_ref, counts_ref, own_hbm, coupling_hbm, left_hbm, *rest):
    first, second, (z_other, z_mine) = rest[:5], rest[5:10], rest[10:12]
    own_ref, blocks, lefts, slots, used, in_sem, left_sem, out_sem = rest[12:]
    count = blocks.shape[0]
    modes, width = own_ref.shape
    cut = first[0].shape[2]

    def load(i):
        return pltpu.make_async_copy(coupling_hbm.at[i // 2, i % 2], blocks.at[i], in_sem.at[i])

    def save(i):
        return pltpu.make_async_copy(lefts.at[i], left_hbm.at[i // 2, i % 2], left_sem.at[i])

    load_own = pltpu.make_async_copy(own_hbm, own_ref, in_sem.at[count])
    load_own.start()

    @pl.loop(0, count)
    def _(i):
        load(i).start()

    @pl.loop(0, SPAN_X + SPAN_Y)
    def _(k):
        used[k] = 0

    load_own.wait()

    @pl.loop(0, count)
    def _(i):
        p, t = i // 2, i % 2
        load(i).wait()
        keep = lax.broadcasted_iota(jnp.int32, (1, width), 1) < counts_ref[p]
        own = jnp.where(keep, own_ref[...], jnp.zeros((modes, width), own_ref.dtype))
        product = jnp.dot(own, blocks[i], preferred_element_type=jnp.float32)
        lefts[i] = jnp.where(keep, product, 0.0).astype(jnp.bfloat16)
        save(i).start()

        code = partner_ref[p]
        dx, dy = offsets(code)
        dz, core, me = ring_offset(code)
        turn = jnp.where((dz == 1) | (dz == 3), jnp.where((dz == 1) == (core == 0), 1, 2), jnp.where(dz == 2, 3, 0))
        slot = jnp.where(code < SPAN_X, slot_of(dx, dy), SPAN_X + turn + jnp.where(core == me, SIDE, 0))
        fresh = (used[slot] == 0) | (used[slot] == p + 1)

        @pl.when(fresh)
        def _():
            used[slot] = p + 1

        @pl.loop(0, modes // CHUNK)
        def _(r):
            rows = pl.ds(pl.multiple_of(r * CHUNK, CHUNK), CHUNK)
            before = jnp.where(fresh, 0.0, slots[slot, t, rows].astype(jnp.float32))
            slots[slot, t, rows] = (before + lefts[i, rows].astype(jnp.float32)).astype(jnp.bfloat16)

    @pl.loop(0, SPAN_X + SPAN_Y)
    def _(k):
        @pl.when(used[k] == 0)
        def _():
            @pl.loop(0, 2 * (modes // CHUNK))
            def _(r):
                rows = pl.ds(pl.multiple_of(r // 2 * CHUNK, CHUNK), CHUNK)
                slots[k, r % 2, rows] = jnp.zeros((CHUNK, width), slots.dtype)

    copies = [
        pltpu.make_async_copy(slots.at[pl.ds(at, size), :, pl.ds(0, cut)], first[n], out_sem.at[n])
        for n, (at, size) in enumerate(PARTS)
    ]
    copies.append(pltpu.make_async_copy(slots.at[pl.ds(SPAN_X, SIDE)], z_other, out_sem.at[5]))
    copies.append(pltpu.make_async_copy(slots.at[pl.ds(SPAN_X + SIDE, SIDE)], z_mine, out_sem.at[6]))
    for dx in range(SIDE):
        for dy in range(SIDE):
            n, at = place_of(slot_of(dy, dx))
            copies.append(pltpu.make_async_copy(
                slots.at[slot_of(dx, dy), :, pl.ds(cut, modes - cut)], second[n].at[at], out_sem.at[7 + dx * SIDE + dy]))
    for c in copies:
        c.start()

    @pl.loop(0, count)
    def _(i):
        save(i).wait()

    for c in copies:
        c.wait()


def in_hbm(value):
    return pltpu.with_memory_space_constraint(value, pltpu.HBM)


def left_products(own, coupling, partner, counts, cut):
    pairs, blocks, width, _ = coupling.shape
    modes = own.shape[0]
    hbm, smem = pl.BlockSpec(memory_space=pltpu.HBM), pl.BlockSpec(memory_space=pltpu.SMEM)
    shapes = [(pairs, blocks, modes, width)]
    shapes += [(size, blocks, cut, width) for _, size in PARTS]
    shapes += [(size, blocks, modes - cut, width) for _, size in PARTS]
    shapes += [(SIDE, blocks, modes, width)] * 2
    out = pl.pallas_call(
        left_kernel,
        in_specs=[smem, smem, hbm, hbm],
        out_specs=[hbm] * len(shapes),
        out_shape=[pltpu.HBM(s, jnp.bfloat16) for s in shapes],
        scratch_shapes=[
            pltpu.VMEM((modes, width), jnp.bfloat16),
            pltpu.VMEM((pairs * blocks, width, width), jnp.bfloat16),
            pltpu.VMEM((pairs * blocks, modes, width), jnp.bfloat16),
            pltpu.VMEM((SPAN_X + SPAN_Y, blocks, modes, width), jnp.bfloat16),
            pltpu.SMEM((SPAN_X + SPAN_Y,), jnp.int32),
            pltpu.SemaphoreType.DMA((pairs * blocks + 1,)),
            pltpu.SemaphoreType.DMA((pairs * blocks,)),
            pltpu.SemaphoreType.DMA((7 + SPAN_X,)),
        ],
        compiler_params=pltpu.CompilerParams(vmem_limit_bytes=32 * 2**20),
        cost_estimate=pl.CostEstimate(flops=2 * pairs * blocks * modes * width * width,
                                      bytes_accessed=25 * 10**6, transcendentals=0),
    )(partner, counts, in_hbm(own), in_hbm(coupling))
    return out[0], out[1:6], out[6:11], out[11], out[12]


def nt(a, b):
    return lax.dot_general(a, b, (((1,), (1,)), ((), ())), preferred_element_type=jnp.float32)


def pair_kernel(partner_ref, left_hbm, *rest):
    (kept, near, far, low, high, ring_mine, ring_other), out_hbm = rest[:7], rest[7]
    lefts, panels, outs, left_sem, panel_sem, out_sem = rest[8:]
    pairs, count = panels.shape[0], lefts.shape[0]

    def load(i):
        return pltpu.make_async_copy(left_hbm.at[i // 2, i % 2], lefts.at[i], left_sem.at[i])

    def save(i):
        return pltpu.make_async_copy(outs.at[i], out_hbm.at[i // 2, i % 2], out_sem.at[i])

    @pl.loop(0, pairs)
    def _(q):
        load(2 * q).start()
        load(2 * q + 1).start()
        code = partner_ref[q]
        dx, dy = offsets(code)
        dz, core, me = ring_offset(code)
        turn = jnp.where((dz == 1) | (dz == 3), jnp.where((dz == 3) == (core == 0), 1, 2), jnp.where(dz == 2, 3, 0))
        along = code < SPAN_X
        for ref, index, chosen in (
            (kept, dx, along & (dy == 0)),
            (near, dx, along & (dy == 1)),
            (far, dx, along & (dy == 3)),
            (low, dx, along & (dy == 2) & (dx < 2)),
            (high, dx - 2, along & (dy == 2) & (dx >= 2)),
            (ring_mine, turn, (code >= SPAN_X) & (core == me)),
            (ring_other, turn, (code >= SPAN_X) & (core != me)),
        ):
            @pl.when(chosen)
            def _():
                pltpu.make_async_copy(ref.at[index], panels.at[q], panel_sem.at[q]).start()

    @pl.loop(0, count)
    def _(i):
        p = i // 2

        @pl.when(i % 2 == 0)
        def _():
            pltpu.make_async_copy(kept.at[0], panels.at[p], panel_sem.at[p]).wait()

        load(i).wait()
        outs[i] = nt(lefts[i], panels[p]).astype(jnp.bfloat16)
        save(i).start()

    @pl.loop(0, count)
    def _(i):
        save(i).wait()


def pair_products(left, sources, partner):
    pairs, blocks, modes, width = left.shape
    hbm, smem = pl.BlockSpec(memory_space=pltpu.HBM), pl.BlockSpec(memory_space=pltpu.SMEM)
    return pl.pallas_call(
        pair_kernel,
        in_specs=[smem] + [hbm] * 8,
        out_specs=hbm,
        out_shape=jax.ShapeDtypeStruct((pairs, blocks, modes, modes), jnp.bfloat16),
        scratch_shapes=[
            pltpu.VMEM((pairs * blocks, modes, width), jnp.bfloat16),
            pltpu.VMEM((pairs, modes, width), jnp.bfloat16),
            pltpu.VMEM((pairs * blocks, modes, modes), jnp.bfloat16),
            pltpu.SemaphoreType.DMA((pairs * blocks,)),
            pltpu.SemaphoreType.DMA((pairs,)),
            pltpu.SemaphoreType.DMA((pairs * blocks,)),
        ],
        compiler_params=pltpu.CompilerParams(vmem_limit_bytes=20 * 2**20),
        cost_estimate=pl.CostEstimate(flops=2 * pairs * blocks * modes * width * modes,
                                      bytes_accessed=15 * 10**6, transcendentals=0),
    )(partner, in_hbm(left), *map(in_hbm, sources))


def partner_kernel(own_ref, top_ref, bottom_ref, *rest):
    last, out_ref, total = rest[:3], rest[3], rest[4]
    cut = top_ref.shape[1]

    @pl.loop(0, out_ref.shape[0])
    def _(t):
        top = top_ref[t]
        for ref in last:
            top = top + ref[t].astype(jnp.float32)
        total[:cut] = top.astype(jnp.bfloat16)
        total[cut:] = bottom_ref[t].astype(jnp.bfloat16)
        out_ref[t] = nt(own_ref[...], total[...])


def partner_products(own, top, bottom, last):
    modes, width = own.shape
    blocks = top.shape[0]
    return pl.pallas_call(
        partner_kernel,
        out_shape=jax.ShapeDtypeStruct((blocks, modes, modes), jnp.float32),
        scratch_shapes=[pltpu.VMEM((modes, width), jnp.bfloat16)],
        compiler_params=pltpu.CompilerParams(vmem_limit_bytes=16 * 2**20),
    )(own, top, bottom, *last)


def shift(value, axis, by):
    moved = []
    for x in range(SIDE):
        for y in range(SIDE):
            to = ((x + by) % SIDE * SIDE + y) if axis == 0 else (x * SIDE + (y + by) % SIDE)
            moved.append((x * SIDE + y, to))
    return lax.ppermute(value, "sx", moved)


def turn(value, by):
    moved = [(2 * z + c, (z + (by if c == 0 else -by)) % SIDE * 2 + c) for z in range(SIDE) for c in range(2)]
    return lax.ppermute(value, "sy", moved)


def swap(value):
    return lax.ppermute(value, "sy", [(2 * z + c, 2 * z + 1 - c) for z in range(SIDE) for c in range(2)])


def added(*terms):
    return sum(v.astype(jnp.float32) for v in terms)


def rounded(*terms):
    return added(*terms).astype(jnp.bfloat16)


def settled(parts, got, last):
    here = parts[4]
    return [
        rounded(here[0], got[1][2], last[0][0]),
        rounded(here[1], got[1][3], last[0][1]),
        rounded(here[2], got[0][2], last[1][0]),
        rounded(here[3], got[0][3], last[1][1]),
    ]


def body(panels, coupling, partner, counts):
    own = jnp.swapaxes(panels[0], 0, 1)
    cut = -(-own.shape[0] * 3 // 64) * 16
    barrier = lax.optimization_barrier

    x1, x3, x2 = shift(own, 0, -1), shift(own, 0, 1), shift(own, 0, 2)
    ring = jnp.stack([own, turn(own, 1), turn(own, -1), turn(own, 2)])
    kept = jnp.stack([own, x1, x2, x3])
    left, top, bottom, z_other, z_mine = left_products(own, coupling, partner, counts, cut)

    kept, up, down = barrier((kept, top[0], top[1]))
    near, far = shift(kept, 1, -1), shift(kept, 1, 1)
    got = [shift(up, 0, 1), shift(down, 0, -1)]

    z_other, ring = barrier((z_other, ring))
    ring_other = swap(ring)
    pair_sum = swap(z_other)
    w = [rounded(z_mine[k], pair_sum[k]) for k in range(SIDE)]
    z_sum = added(w[0], turn(w[1], 1), turn(w[2], -1), turn(w[3], 2))

    near, far, up, down = barrier((near, far, bottom[0], bottom[1]))
    got_b = [shift(up, 1, 1), shift(down, 1, -1)]
    near, far, got_b = barrier((near, far, got_b))
    low, high = shift(near[:2], 1, -1), shift(far[2:], 1, 1)
    pass_b = [rounded(bottom[2], got_b[0][:2]), rounded(bottom[3], got_b[1][:2])]
    pass_b, low, high = barrier((pass_b, low, high))
    last_b = [shift(pass_b[0], 1, 1), shift(pass_b[1], 1, -1)]

    last = [shift(rounded(top[2], got[0][:2]), 0, 1), shift(rounded(top[3], got[1][:2]), 0, -1)]
    v = settled(top, got, last)
    v_b = settled(bottom, got_b, last_b)
    ends = [shift(v[1], 1, 1), shift(v[3], 1, -1), shift(v[2], 1, 2)]
    ends_b = [shift(v_b[1], 0, 1), shift(v_b[3], 0, -1), shift(v_b[2], 0, 2)]

    sources = [kept, near, far, low, high, ring, ring_other]
    pair_blocks = pair_products(left, sources, barrier((partner, v))[0])
    partner_blocks = partner_products(
        own, added(v[0], z_sum[:, :cut]), added(v_b[0], *ends_b, z_sum[:, cut:]), ends
    )
    return (pair_blocks, partner_blocks[None])


def solution(mesh):
    placed = (
        P(("sx", "sy"), None, None),
        P(("sx", "sy"), None, None, None),
        P(("sx", "sy")),
        P(("sx", "sy")),
    )
    return jax.shard_map(
        body,
        mesh=mesh,
        in_specs=placed,
        out_specs=(P(("sx", "sy"), None, None, None), P(("sx", "sy"), None, None, None)),
        check_vma=False,
    )
```

```python
import jax
import jax.numpy as jnp
from jax import lax
from jax.experimental import pallas as pl
from jax.experimental.pallas import tpu as pltpu
from jax.sharding import PartitionSpec as P

SIDE = 4
SPAN_X, SPAN_Y = SIDE * SIDE, 2 * SIDE
PARTS = ((0, 4), (4, 4), (8, 2), (10, 2), (12, 4))
CHUNK = 80


def slot_of(d1, d2):
    low = d2 < 2
    return jnp.where(
        d1 == 0, 12 + d2,
        jnp.where(d1 == 1, jnp.where(low, 8 + d2, d2),
                  jnp.where(d1 == 2, jnp.where(low, d2, 2 + d2), jnp.where(low, 6 + d2, 8 + d2))))


def offsets(code):
    me = lax.axis_index("sx")
    dx = (code // SIDE - me // SIDE + SIDE) % SIDE
    dy = (code % SIDE - me % SIDE + SIDE) % SIDE
    swapped = lax.axis_index("sy") % 2 == 1
    return jnp.where(swapped, dy, dx), jnp.where(swapped, dx, dy)


def ring_offset(code):
    me = lax.axis_index("sy")
    other = code - SPAN_X
    return (other // 2 - me // 2 + SIDE) % SIDE, other % 2, me % 2


def left_kernel(partner_ref, counts_ref, own_hbm, coupling_hbm, left_hbm, *rest):
    outs = rest[:7]
    own_ref, blocks, lefts, zero, sums, keys, number, seen, at_sum, in_sem, left_sem, out_sem = rest[7:]
    count, pairs = blocks.shape[0], keys.shape[0]
    modes, width = own_ref.shape
    slots = SPAN_X + SPAN_Y

    def load(i):
        return pltpu.make_async_copy(coupling_hbm.at[i // 2, i % 2], blocks.at[i], in_sem.at[i])

    def save(i):
        return pltpu.make_async_copy(lefts.at[i], left_hbm.at[i // 2, i % 2], left_sem.at[i])

    load_own = pltpu.make_async_copy(own_hbm, own_ref, in_sem.at[count])
    load_own.start()

    @pl.loop(0, count)
    def _(i):
        load(i).start()

    @pl.loop(0, slots)
    def _(k):
        number[k] = 0
        seen[k] = 0

    at_sum[slots] = 0

    @pl.loop(0, pairs)
    def _(p):
        code = partner_ref[p]
        d1, d2 = offsets(code)
        dz, core, me = ring_offset(code)
        step = jnp.where((dz == 1) | (dz == 3), jnp.where((dz == 1) == (core == 0), 1, 2), jnp.where(dz == 2, 3, 0))
        key = jnp.where(code < SPAN_X, slot_of(d1, d2), SPAN_X + step + jnp.where(core == me, SIDE, 0))
        keys[p] = key
        number[key] = number[key] + 1

    @pl.loop(0, 2 * (modes // CHUNK))
    def _(r):
        rows = pl.ds(pl.multiple_of(r // 2 * CHUNK, CHUNK), CHUNK)
        zero[r % 2, rows] = jnp.zeros((CHUNK, width), zero.dtype)

    def send(source, key):
        for out, (at, size) in zip(outs, PARTS + ((SPAN_X, SIDE), (SPAN_X + SIDE, SIDE)), strict=True):
            @pl.when((key >= at) & (key < at + size))
            def _():
                pltpu.make_async_copy(source, out.at[key - at], out_sem.at[key]).start()

    @pl.loop(0, slots)
    def _(k):
        @pl.when(number[k] == 0)
        def _():
            send(zero, k)

    load_own.wait()

    @pl.loop(0, count)
    def _(i):
        p = i // 2
        load(i).wait()
        keep = lax.broadcasted_iota(jnp.int32, (1, width), 1) < counts_ref[p]
        own = jnp.where(keep, own_ref[...], jnp.zeros((modes, width), own_ref.dtype))
        product = jnp.dot(own, blocks[i], preferred_element_type=jnp.float32)
        lefts[i] = jnp.where(keep, product, 0.0).astype(jnp.bfloat16)
        save(i).start()
        key = keys[p]
        single = number[key] == 1

        @pl.when((i % 2 == 1) & single)
        def _():
            send(lefts.at[pl.ds(i - 1, 2)], key)

        @pl.when((i % 2 == 1) & jnp.logical_not(single))
        def _():
            fresh = seen[key] == 0

            @pl.when(fresh)
            def _():
                at_sum[key] = at_sum[slots]
                at_sum[slots] = at_sum[slots] + 1

            seen[key] = seen[key] + 1
            place = at_sum[key]

            @pl.loop(0, 2 * (modes // CHUNK))
            def _(r):
                t, rows = r % 2, pl.ds(pl.multiple_of(r // 2 * CHUNK, CHUNK), CHUNK)
                before = jnp.where(fresh, 0.0, sums[place, t, rows].astype(jnp.float32))
                sums[place, t, rows] = (before + lefts[i - 1 + t, rows].astype(jnp.float32)).astype(jnp.bfloat16)

            @pl.when(seen[key] == number[key])
            def _():
                send(sums.at[place], key)

    @pl.loop(0, count)
    def _(i):
        save(i).wait()

    @pl.loop(0, slots)
    def _(k):
        pltpu.make_async_copy(zero, outs[0].at[0], out_sem.at[k]).wait()


def in_hbm(value):
    return pltpu.with_memory_space_constraint(value, pltpu.HBM)


def left_products(own, coupling, partner, counts):
    pairs, blocks, width, _ = coupling.shape
    modes = own.shape[0]
    hbm, smem = pl.BlockSpec(memory_space=pltpu.HBM), pl.BlockSpec(memory_space=pltpu.SMEM)
    slots = SPAN_X + SPAN_Y
    sizes = [pairs] + [size for _, size in PARTS] + [SIDE] * 2
    out = pl.pallas_call(
        left_kernel,
        in_specs=[smem, smem, hbm, hbm],
        out_specs=[hbm] * len(sizes),
        out_shape=[pltpu.HBM((n, blocks, modes, width), jnp.bfloat16) for n in sizes],
        scratch_shapes=[
            pltpu.VMEM((modes, width), jnp.bfloat16),
            pltpu.VMEM((pairs * blocks, width, width), jnp.bfloat16),
            pltpu.VMEM((pairs * blocks, modes, width), jnp.bfloat16),
            pltpu.VMEM((blocks, modes, width), jnp.bfloat16),
            pltpu.VMEM((pairs // 2, blocks, modes, width), jnp.bfloat16),
            pltpu.SMEM((pairs,), jnp.int32),
            pltpu.SMEM((slots,), jnp.int32),
            pltpu.SMEM((slots,), jnp.int32),
            pltpu.SMEM((slots + 1,), jnp.int32),
            pltpu.SemaphoreType.DMA((pairs * blocks + 1,)),
            pltpu.SemaphoreType.DMA((pairs * blocks,)),
            pltpu.SemaphoreType.DMA((slots,)),
        ],
        compiler_params=pltpu.CompilerParams(vmem_limit_bytes=20 * 2**20),
        cost_estimate=pl.CostEstimate(flops=2 * pairs * blocks * modes * width * width,
                                      bytes_accessed=25 * 10**6, transcendentals=0),
    )(partner, counts, in_hbm(own), in_hbm(coupling))
    return out[0], out[1:6], out[6], out[7]


def nt(a, b):
    return lax.dot_general(a, b, (((1,), (1,)), ((), ())), preferred_element_type=jnp.float32)


def pair_kernel(partner_ref, left_hbm, *rest):
    (kept, near, far, low, high, ring_mine, ring_other), out_hbm = rest[:7], rest[7]
    lefts, panels, outs, left_sem, panel_sem, out_sem = rest[8:]
    pairs, count = panels.shape[0], lefts.shape[0]

    def load(i):
        return pltpu.make_async_copy(left_hbm.at[i // 2, i % 2], lefts.at[i], left_sem.at[i])

    def save(i):
        return pltpu.make_async_copy(outs.at[i], out_hbm.at[i // 2, i % 2], out_sem.at[i])

    @pl.loop(0, pairs)
    def _(q):
        load(2 * q).start()
        load(2 * q + 1).start()
        code = partner_ref[q]
        d1, d2 = offsets(code)
        dz, core, me = ring_offset(code)
        step = jnp.where((dz == 1) | (dz == 3), jnp.where((dz == 3) == (core == 0), 1, 2), jnp.where(dz == 2, 3, 0))
        along = code < SPAN_X
        for ref, index, chosen in (
            (kept, d1, along & (d2 == 0)),
            (near, d1, along & (d2 == 1)),
            (far, d1, along & (d2 == 3)),
            (low, d1, along & (d2 == 2) & (d1 < 2)),
            (high, d1 - 2, along & (d2 == 2) & (d1 >= 2)),
            (ring_mine, step, (code >= SPAN_X) & (core == me)),
            (ring_other, step, (code >= SPAN_X) & (core != me)),
        ):
            @pl.when(chosen)
            def _():
                pltpu.make_async_copy(ref.at[index], panels.at[q], panel_sem.at[q]).start()

    @pl.loop(0, count)
    def _(i):
        p = i // 2

        @pl.when(i % 2 == 0)
        def _():
            pltpu.make_async_copy(kept.at[0], panels.at[p], panel_sem.at[p]).wait()

        load(i).wait()
        outs[i] = nt(lefts[i], panels[p]).astype(jnp.bfloat16)
        save(i).start()

    @pl.loop(0, count)
    def _(i):
        save(i).wait()


def pair_products(left, sources, partner):
    pairs, blocks, modes, width = left.shape
    hbm, smem = pl.BlockSpec(memory_space=pltpu.HBM), pl.BlockSpec(memory_space=pltpu.SMEM)
    return pl.pallas_call(
        pair_kernel,
        in_specs=[smem] + [hbm] * 8,
        out_specs=hbm,
        out_shape=jax.ShapeDtypeStruct((pairs, blocks, modes, modes), jnp.bfloat16),
        scratch_shapes=[
            pltpu.VMEM((pairs * blocks, modes, width), jnp.bfloat16),
            pltpu.VMEM((pairs, modes, width), jnp.bfloat16),
            pltpu.VMEM((pairs * blocks, modes, modes), jnp.bfloat16),
            pltpu.SemaphoreType.DMA((pairs * blocks,)),
            pltpu.SemaphoreType.DMA((pairs,)),
            pltpu.SemaphoreType.DMA((pairs * blocks,)),
        ],
        compiler_params=pltpu.CompilerParams(vmem_limit_bytes=20 * 2**20),
        cost_estimate=pl.CostEstimate(flops=2 * pairs * blocks * modes * width * modes,
                                      bytes_accessed=15 * 10**6, transcendentals=0),
    )(partner, in_hbm(left), *map(in_hbm, sources))


def partner_kernel(own_ref, sum_ref, *rest):
    last, out_ref = rest[:-1], rest[-1]

    @pl.loop(0, out_ref.shape[0])
    def _(t):
        total = sum_ref[t]
        for ref in last:
            total = total + ref[t].astype(jnp.float32)
        out_ref[t] = nt(own_ref[...], total.astype(jnp.bfloat16))


def partner_products(own, start, last):
    modes, _ = own.shape
    blocks = start.shape[0]
    return pl.pallas_call(
        partner_kernel,
        out_shape=jax.ShapeDtypeStruct((blocks, modes, modes), jnp.float32),
        compiler_params=pltpu.CompilerParams(vmem_limit_bytes=16 * 2**20),
    )(own, start, *last)


def permuted(value, move):
    pairs = []
    for n in range(SPAN_X * SPAN_Y):
        here = (n // SPAN_Y // SIDE, n // SPAN_Y % SIDE, n % SPAN_Y // 2, n % 2)
        x, y, z, c = move(*here)
        pairs.append((n, ((x % SIDE) * SIDE + y % SIDE) * SPAN_Y + (z % SIDE) * 2 + c))
    return lax.ppermute(value, ("sx", "sy"), pairs)


def first(value, by):
    return permuted(value, lambda x, y, z, c: (x + by, y, z, c) if c == 0 else (x, y + by, z, c))


def second(value, by):
    return permuted(value, lambda x, y, z, c: (x, y + by, z, c) if c == 0 else (x + by, y, z, c))


def turn(value, by):
    return permuted(value, lambda x, y, z, c: (x, y, z + (by if c == 0 else -by), c))


def swap(value):
    return permuted(value, lambda x, y, z, c: (x, y, z, 1 - c))


def added(*terms):
    return sum(v.astype(jnp.float32) for v in terms)


def rounded(*terms):
    return added(*terms).astype(jnp.bfloat16)


def after(value, *others):
    return lax.optimization_barrier((value,) + others)[0]


def body(panels, coupling, partner, counts):
    own = jnp.swapaxes(panels[0], 0, 1)
    barrier = lax.optimization_barrier

    kept = [own, first(own, -1), first(own, 2), first(own, 1)]
    kept = jnp.stack([kept[0], kept[1], kept[2], kept[3]])
    ring1 = turn(own, 1)
    left, (up, down, pass_up, pass_down, here), z_other, z_mine = left_products(own, coupling, partner, counts)

    kept, up, down = barrier((kept, up, down))
    got_up, got_down = first(up, 1), first(down, -1)
    near, far = second(kept, -1), second(kept, 1)
    ring2 = turn(after(own, ring1, up), -1)
    ring3 = turn(after(own, ring2), 2)
    ring = jnp.stack([own, ring1, ring2, ring3])
    ring_other = swap(ring)
    near, far, ring_other = barrier((near, far, ring_other))
    low, high = second(near[:2], -1), second(far[2:], 1)

    pair_sum = swap(after(z_other, ring_other))
    w = [rounded(z_mine[k], pair_sum[k]) for k in range(SIDE)]
    z1 = turn(w[1], 1)
    z2 = turn(after(w[2], z1), -1)
    z3 = turn(after(w[3], z2), 2)

    b_up, b_down = rounded(pass_up, got_up[:2]), rounded(pass_down, got_down[:2])
    b_up, b_down = barrier((b_up, b_down, w))[:2]
    last_up, last_down = first(b_up, 1), first(b_down, -1)

    v = [
        rounded(here[0], got_down[2], last_up[0]),
        rounded(here[1], got_down[3], last_up[1]),
        rounded(here[2], got_up[2], last_down[0]),
        rounded(here[3], got_up[3], last_down[1]),
    ]
    v = barrier((v, z1))[0]
    ends = [second(v[1], 1), second(v[3], -1), second(v[2], 2)]

    sources = [kept, near, far, low, high, ring, ring_other]
    pair_blocks = pair_products(left, sources, after(partner, *v))
    partner_blocks = partner_products(own, added(v[0], w[0], z1, z2, z3), ends)
    return (pair_blocks, partner_blocks[None])


def solution(mesh):
    placed = (
        P(("sx", "sy"), None, None),
        P(("sx", "sy"), None, None, None),
        P(("sx", "sy")),
        P(("sx", "sy")),
    )
    return jax.shard_map(
        body,
        mesh=mesh,
        in_specs=placed,
        out_specs=(P(("sx", "sy"), None, None, None), P(("sx", "sy"), None, None, None)),
        check_vma=False,
    )
```

```python
import jax
import jax.numpy as jnp
from jax import lax
from jax.experimental import pallas as pl
from jax.experimental.pallas import tpu as pltpu
from jax.sharding import PartitionSpec as P

SIDE = 4
SPAN_X, SPAN_Y = SIDE * SIDE, 2 * SIDE
PARTS = ((0, 4), (4, 4), (8, 2), (10, 2), (12, 4))
CHUNK = 80


def slot_of(d1, d2):
    low = d2 < 2
    return jnp.where(
        d1 == 0, 12 + d2,
        jnp.where(d1 == 1, jnp.where(low, 8 + d2, d2),
                  jnp.where(d1 == 2, jnp.where(low, d2, 2 + d2), jnp.where(low, 6 + d2, 8 + d2))))


def offsets(code):
    me = lax.axis_index("sx")
    dx = (code // SIDE - me // SIDE + SIDE) % SIDE
    dy = (code % SIDE - me % SIDE + SIDE) % SIDE
    swapped = lax.axis_index("sy") % 2 == 1
    return jnp.where(swapped, dy, dx), jnp.where(swapped, dx, dy)


def ring_offset(code):
    me = lax.axis_index("sy")
    other = code - SPAN_X
    return (other // 2 - me // 2 + SIDE) % SIDE, other % 2, me % 2


def left_kernel(partner_hbm, counts_hbm, own_hbm, coupling_hbm, left_hbm, *rest):
    outs = rest[:7]
    partner_ref, counts_ref, own_ref, blocks, lefts, zero, sums = rest[7:14]
    keys, number, seen, at_sum, in_sem, left_sem, out_sem = rest[14:]
    count, pairs = blocks.shape[0], keys.shape[0]
    modes, width = own_ref.shape
    slots = SPAN_X + SPAN_Y

    def load(i):
        return pltpu.make_async_copy(coupling_hbm.at[i // 2, i % 2], blocks.at[i], in_sem.at[i])

    def save(i):
        return pltpu.make_async_copy(lefts.at[i], left_hbm.at[i // 2, i % 2], left_sem.at[i])

    load_partner = pltpu.make_async_copy(partner_hbm, partner_ref, in_sem.at[count + 1])
    load_partner.start()
    load_counts = pltpu.make_async_copy(counts_hbm, counts_ref, in_sem.at[count + 2])
    load_counts.start()
    load_own = pltpu.make_async_copy(own_hbm, own_ref, in_sem.at[count])
    load_own.start()

    @pl.loop(0, count)
    def _(i):
        load(i).start()

    @pl.loop(0, slots)
    def _(k):
        number[k] = 0
        seen[k] = 0

    at_sum[slots] = 0
    load_partner.wait()
    load_counts.wait()

    @pl.loop(0, pairs)
    def _(p):
        code = partner_ref[p]
        d1, d2 = offsets(code)
        dz, core, me = ring_offset(code)
        step = jnp.where((dz == 1) | (dz == 3), jnp.where((dz == 1) == (core == 0), 1, 2), jnp.where(dz == 2, 3, 0))
        key = jnp.where(code < SPAN_X, slot_of(d1, d2), SPAN_X + step + jnp.where(core == me, SIDE, 0))
        keys[p] = key
        number[key] = number[key] + 1

    @pl.loop(0, 2 * (modes // CHUNK))
    def _(r):
        rows = pl.ds(pl.multiple_of(r // 2 * CHUNK, CHUNK), CHUNK)
        zero[r % 2, rows] = jnp.zeros((CHUNK, width), zero.dtype)

    def send(source, key):
        for out, (at, size) in zip(outs, PARTS + ((SPAN_X, SIDE), (SPAN_X + SIDE, SIDE)), strict=True):
            @pl.when((key >= at) & (key < at + size))
            def _():
                pltpu.make_async_copy(source, out.at[key - at], out_sem.at[key]).start()

    @pl.loop(0, slots)
    def _(k):
        @pl.when(number[k] == 0)
        def _():
            send(zero, k)

    load_own.wait()

    @pl.loop(0, count)
    def _(i):
        p = i // 2
        load(i).wait()
        keep = lax.broadcasted_iota(jnp.int32, (1, width), 1) < counts_ref[p]
        own = jnp.where(keep, own_ref[...], jnp.zeros((modes, width), own_ref.dtype))
        product = jnp.dot(own, blocks[i], preferred_element_type=jnp.float32)
        lefts[i] = jnp.where(keep, product, 0.0).astype(jnp.bfloat16)
        save(i).start()
        key = keys[p]
        single = number[key] == 1

        @pl.when((i % 2 == 1) & single)
        def _():
            send(lefts.at[pl.ds(i - 1, 2)], key)

        @pl.when((i % 2 == 1) & jnp.logical_not(single))
        def _():
            fresh = seen[key] == 0

            @pl.when(fresh)
            def _():
                at_sum[key] = at_sum[slots]
                at_sum[slots] = at_sum[slots] + 1

            seen[key] = seen[key] + 1
            place = at_sum[key]

            @pl.loop(0, 2 * (modes // CHUNK))
            def _(r):
                t, rows = r % 2, pl.ds(pl.multiple_of(r // 2 * CHUNK, CHUNK), CHUNK)
                before = jnp.where(fresh, 0.0, sums[place, t, rows].astype(jnp.float32))
                sums[place, t, rows] = (before + lefts[i - 1 + t, rows].astype(jnp.float32)).astype(jnp.bfloat16)

            @pl.when(seen[key] == number[key])
            def _():
                send(sums.at[place], key)

    @pl.loop(0, count)
    def _(i):
        save(i).wait()

    @pl.loop(0, slots)
    def _(k):
        pltpu.make_async_copy(zero, outs[0].at[0], out_sem.at[k]).wait()


def in_hbm(value):
    return pltpu.with_memory_space_constraint(value, pltpu.HBM)


def left_products(own, coupling, partner, counts):
    pairs, blocks, width, _ = coupling.shape
    modes = own.shape[0]
    hbm = pl.BlockSpec(memory_space=pltpu.HBM)
    slots = SPAN_X + SPAN_Y
    sizes = [pairs] + [size for _, size in PARTS] + [SIDE] * 2
    out = pl.pallas_call(
        left_kernel,
        in_specs=[hbm] * 4,
        out_specs=[hbm] * len(sizes),
        out_shape=[pltpu.HBM((n, blocks, modes, width), jnp.bfloat16) for n in sizes],
        scratch_shapes=[
            pltpu.SMEM((pairs,), jnp.int32),
            pltpu.SMEM((pairs,), jnp.int32),
            pltpu.VMEM((modes, width), jnp.bfloat16),
            pltpu.VMEM((pairs * blocks, width, width), jnp.bfloat16),
            pltpu.VMEM((pairs * blocks, modes, width), jnp.bfloat16),
            pltpu.VMEM((blocks, modes, width), jnp.bfloat16),
            pltpu.VMEM((pairs // 2, blocks, modes, width), jnp.bfloat16),
            pltpu.SMEM((pairs,), jnp.int32),
            pltpu.SMEM((slots,), jnp.int32),
            pltpu.SMEM((slots,), jnp.int32),
            pltpu.SMEM((slots + 1,), jnp.int32),
            pltpu.SemaphoreType.DMA((pairs * blocks + 3,)),
            pltpu.SemaphoreType.DMA((pairs * blocks,)),
            pltpu.SemaphoreType.DMA((slots,)),
        ],
        compiler_params=pltpu.CompilerParams(vmem_limit_bytes=20 * 2**20),
        cost_estimate=pl.CostEstimate(flops=2 * pairs * blocks * modes * width * width,
                                      bytes_accessed=25 * 10**6, transcendentals=0),
    )(*map(in_hbm, (partner, counts, own, coupling)))
    return out[0], out[1:6], out[6], out[7]


def nt(a, b):
    return lax.dot_general(a, b, (((1,), (1,)), ((), ())), preferred_element_type=jnp.float32)


def pair_kernel(partner_ref, left_hbm, *rest):
    (kept, near, far, low, high, ring_mine, ring_other), out_hbm = rest[:7], rest[7]
    lefts, panels, outs, left_sem, panel_sem, out_sem = rest[8:]
    pairs, count = panels.shape[0], lefts.shape[0]

    def load(i):
        return pltpu.make_async_copy(left_hbm.at[i // 2, i % 2], lefts.at[i], left_sem.at[i])

    def save(i):
        return pltpu.make_async_copy(outs.at[i], out_hbm.at[i // 2, i % 2], out_sem.at[i])

    @pl.loop(0, pairs)
    def _(q):
        load(2 * q).start()
        load(2 * q + 1).start()
        code = partner_ref[q]
        d1, d2 = offsets(code)
        dz, core, me = ring_offset(code)
        step = jnp.where((dz == 1) | (dz == 3), jnp.where((dz == 3) == (core == 0), 1, 2), jnp.where(dz == 2, 3, 0))
        along = code < SPAN_X
        for ref, index, chosen in (
            (kept, d1, along & (d2 == 0)),
            (near, d1, along & (d2 == 1)),
            (far, d1, along & (d2 == 3)),
            (low, d1, along & (d2 == 2) & (d1 < 2)),
            (high, d1 - 2, along & (d2 == 2) & (d1 >= 2)),
            (ring_mine, step, (code >= SPAN_X) & (core == me)),
            (ring_other, step, (code >= SPAN_X) & (core != me)),
        ):
            @pl.when(chosen)
            def _():
                pltpu.make_async_copy(ref.at[index], panels.at[q], panel_sem.at[q]).start()

    @pl.loop(0, count)
    def _(i):
        p = i // 2

        @pl.when(i % 2 == 0)
        def _():
            pltpu.make_async_copy(kept.at[0], panels.at[p], panel_sem.at[p]).wait()

        load(i).wait()
        outs[i] = nt(lefts[i], panels[p]).astype(jnp.bfloat16)
        save(i).start()

    @pl.loop(0, count)
    def _(i):
        save(i).wait()


def pair_products(left, sources, partner):
    pairs, blocks, modes, width = left.shape
    hbm, smem = pl.BlockSpec(memory_space=pltpu.HBM), pl.BlockSpec(memory_space=pltpu.SMEM)
    return pl.pallas_call(
        pair_kernel,
        in_specs=[smem] + [hbm] * 8,
        out_specs=hbm,
        out_shape=jax.ShapeDtypeStruct((pairs, blocks, modes, modes), jnp.bfloat16),
        scratch_shapes=[
            pltpu.VMEM((pairs * blocks, modes, width), jnp.bfloat16),
            pltpu.VMEM((pairs, modes, width), jnp.bfloat16),
            pltpu.VMEM((pairs * blocks, modes, modes), jnp.bfloat16),
            pltpu.SemaphoreType.DMA((pairs * blocks,)),
            pltpu.SemaphoreType.DMA((pairs,)),
            pltpu.SemaphoreType.DMA((pairs * blocks,)),
        ],
        compiler_params=pltpu.CompilerParams(vmem_limit_bytes=20 * 2**20),
        cost_estimate=pl.CostEstimate(flops=2 * pairs * blocks * modes * width * modes,
                                      bytes_accessed=15 * 10**6, transcendentals=0),
    )(partner, in_hbm(left), *map(in_hbm, sources))


def partner_kernel(own_ref, sum_ref, *rest):
    last, out_ref = rest[:-1], rest[-1]

    @pl.loop(0, out_ref.shape[0])
    def _(t):
        total = sum_ref[t]
        for ref in last:
            total = total + ref[t].astype(jnp.float32)
        out_ref[t] = nt(own_ref[...], total.astype(jnp.bfloat16))


def partner_products(own, start, last):
    modes, _ = own.shape
    blocks = start.shape[0]
    return pl.pallas_call(
        partner_kernel,
        out_shape=jax.ShapeDtypeStruct((blocks, modes, modes), jnp.float32),
        compiler_params=pltpu.CompilerParams(vmem_limit_bytes=16 * 2**20),
    )(own, start, *last)


def permuted(value, move):
    pairs = []
    for n in range(SPAN_X * SPAN_Y):
        here = (n // SPAN_Y // SIDE, n // SPAN_Y % SIDE, n % SPAN_Y // 2, n % 2)
        x, y, z, c = move(*here)
        pairs.append((n, ((x % SIDE) * SIDE + y % SIDE) * SPAN_Y + (z % SIDE) * 2 + c))
    return lax.ppermute(value, ("sx", "sy"), pairs)


def first(value, by):
    return permuted(value, lambda x, y, z, c: (x + by, y, z, c) if c == 0 else (x, y + by, z, c))


def second(value, by):
    return permuted(value, lambda x, y, z, c: (x, y + by, z, c) if c == 0 else (x + by, y, z, c))


def turn(value, by):
    return permuted(value, lambda x, y, z, c: (x, y, z + (by if c == 0 else -by), c))


def swap(value):
    return permuted(value, lambda x, y, z, c: (x, y, z, 1 - c))


def added(*terms):
    return sum(v.astype(jnp.float32) for v in terms)


def rounded(*terms):
    return added(*terms).astype(jnp.bfloat16)


def after(value, *others):
    return lax.optimization_barrier((value,) + others)[0]


def body(panels, coupling, partner, counts):
    own = jnp.swapaxes(panels[0], 0, 1)
    barrier = lax.optimization_barrier

    moved = [first(own, -1), first(own, 2), first(own, 1)]
    kept = jnp.stack([own] + moved)
    left, (up, down, pass_up, pass_down, here), z_other, z_mine = left_products(own, coupling, partner, counts)
    kept, up, down, z_other, own_z = barrier((kept, up, down, z_other, own))

    got = [first(up, 1), first(down, -1)]
    ring = [second(kept, -1), second(kept, 1)]
    ring1 = turn(own_z, 1)
    ring2 = turn(after(own_z, ring1), -1)
    ring3 = turn(after(own_z, ring2), 2)
    ring_mine = jnp.stack([own, ring1, ring2, ring3])
    ring_other = swap(ring_mine)
    got, ring, ring_other, z_other = barrier((got, ring, ring_other, z_other))
    (got_up, got_down), (near, far) = got, ring

    last = [first(rounded(pass_up, got_up[:2]), 1), first(rounded(pass_down, got_down[:2]), -1)]
    relay = [second(near[:2], -1), second(far[2:], 1)]
    pair_sum = swap(z_other)
    w = [rounded(z_mine[k], pair_sum[k]) for k in range(SIDE)]
    z1 = turn(w[1], 1)
    last, relay, w, z1 = barrier((last, relay, w, z1))
    (last_up, last_down), (low, high) = last, relay

    v = [
        rounded(here[0], got_down[2], last_up[0]),
        rounded(here[1], got_down[3], last_up[1]),
        rounded(here[2], got_up[2], last_down[0]),
        rounded(here[3], got_up[3], last_down[1]),
    ]
    ends = [second(v[1], 1), second(v[3], -1), second(v[2], 2)]
    z2, z3 = turn(w[2], -1), turn(w[3], 2)

    sources = [kept, near, far, low, high, ring_mine, ring_other]
    pair_blocks = pair_products(left, sources, after(partner, *v))
    partner_blocks = partner_products(own, added(v[0], w[0], z1, z2, z3), ends)
    return (pair_blocks, partner_blocks[None])


def solution(mesh):
    placed = (
        P(("sx", "sy"), None, None),
        P(("sx", "sy"), None, None, None),
        P(("sx", "sy")),
        P(("sx", "sy")),
    )
    return jax.shard_map(
        body,
        mesh=mesh,
        in_specs=placed,
        out_specs=(P(("sx", "sy"), None, None, None), P(("sx", "sy"), None, None, None)),
        check_vma=False,
    )
```

```python
import jax
import jax.numpy as jnp
from jax import lax
from jax.experimental import pallas as pl
from jax.experimental.pallas import tpu as pltpu
from jax.sharding import PartitionSpec as P

SIDE = 4
SPAN_X, SPAN_Y = SIDE * SIDE, 2 * SIDE
PARTS = ((0, 4), (4, 4), (8, 2), (10, 2), (12, 4))
CHUNK = 80


def slot_of(d1, d2):
    low = d2 < 2
    return jnp.where(
        d1 == 0, 12 + d2,
        jnp.where(d1 == 1, jnp.where(low, 8 + d2, d2),
                  jnp.where(d1 == 2, jnp.where(low, d2, 2 + d2), jnp.where(low, 6 + d2, 8 + d2))))


def offsets(code):
    me = lax.axis_index("sx")
    dx = (code // SIDE - me // SIDE + SIDE) % SIDE
    dy = (code % SIDE - me % SIDE + SIDE) % SIDE
    swapped = lax.axis_index("sy") % 2 == 1
    return jnp.where(swapped, dy, dx), jnp.where(swapped, dx, dy)


def ring_offset(code):
    me = lax.axis_index("sy")
    other = code - SPAN_X
    return (other // 2 - me // 2 + SIDE) % SIDE, other % 2, me % 2


def left_kernel(partner_hbm, counts_hbm, own_hbm, coupling_hbm, left_hbm, *rest):
    outs = rest[:7]
    partner_ref, counts_ref, own_ref, blocks, lefts, zero, sums = rest[7:14]
    keys, number, seen, at_sum, in_sem, left_sem, out_sem = rest[14:]
    count, pairs = blocks.shape[0], keys.shape[0]
    modes, width = own_ref.shape
    slots = SPAN_X + SPAN_Y

    def load(i):
        return pltpu.make_async_copy(coupling_hbm.at[i // 2, i % 2], blocks.at[i], in_sem.at[i])

    def save(i):
        return pltpu.make_async_copy(lefts.at[i], left_hbm.at[i // 2, i % 2], left_sem.at[i])

    load_partner = pltpu.make_async_copy(partner_hbm, partner_ref, in_sem.at[count + 1])
    load_partner.start()
    load_counts = pltpu.make_async_copy(counts_hbm, counts_ref, in_sem.at[count + 2])
    load_counts.start()
    load_own = pltpu.make_async_copy(own_hbm, own_ref, in_sem.at[count])
    load_own.start()

    @pl.loop(0, count)
    def _(i):
        load(i).start()

    @pl.loop(0, slots)
    def _(k):
        number[k] = 0
        seen[k] = 0

    at_sum[slots] = 0
    load_partner.wait()
    load_counts.wait()

    @pl.loop(0, pairs)
    def _(p):
        code = partner_ref[p]
        d1, d2 = offsets(code)
        dz, core, me = ring_offset(code)
        step = jnp.where((dz == 1) | (dz == 3), jnp.where((dz == 1) == (core == 0), 1, 2), jnp.where(dz == 2, 3, 0))
        key = jnp.where(code < SPAN_X, slot_of(d1, d2), SPAN_X + step + jnp.where(core == me, SIDE, 0))
        keys[p] = key
        number[key] = number[key] + 1

    @pl.loop(0, 2 * (modes // CHUNK))
    def _(r):
        rows = pl.ds(pl.multiple_of(r // 2 * CHUNK, CHUNK), CHUNK)
        zero[r % 2, rows] = jnp.zeros((CHUNK, width), zero.dtype)

    def send(source, key):
        for out, (at, size) in zip(outs, PARTS + ((SPAN_X, SIDE), (SPAN_X + SIDE, SIDE)), strict=True):
            @pl.when((key >= at) & (key < at + size))
            def _():
                pltpu.make_async_copy(source, out.at[key - at], out_sem.at[key]).start()

    @pl.loop(0, slots)
    def _(k):
        @pl.when(number[k] == 0)
        def _():
            send(zero, k)

    load_own.wait()

    @pl.loop(0, count)
    def _(i):
        p = i // 2
        load(i).wait()
        keep = lax.broadcasted_iota(jnp.int32, (1, width), 1) < counts_ref[p]
        own = jnp.where(keep, own_ref[...], jnp.zeros((modes, width), own_ref.dtype))
        product = jnp.dot(own, blocks[i], preferred_element_type=jnp.float32)
        lefts[i] = jnp.where(keep, product, 0.0).astype(jnp.bfloat16)
        save(i).start()
        key = keys[p]
        single = number[key] == 1

        @pl.when((i % 2 == 1) & single)
        def _():
            send(lefts.at[pl.ds(i - 1, 2)], key)

        @pl.when((i % 2 == 1) & jnp.logical_not(single))
        def _():
            fresh = seen[key] == 0

            @pl.when(fresh)
            def _():
                at_sum[key] = at_sum[slots]
                at_sum[slots] = at_sum[slots] + 1

            seen[key] = seen[key] + 1
            place = at_sum[key]

            @pl.loop(0, 2 * (modes // CHUNK))
            def _(r):
                t, rows = r % 2, pl.ds(pl.multiple_of(r // 2 * CHUNK, CHUNK), CHUNK)
                before = jnp.where(fresh, 0.0, sums[place, t, rows].astype(jnp.float32))
                sums[place, t, rows] = (before + lefts[i - 1 + t, rows].astype(jnp.float32)).astype(jnp.bfloat16)

            @pl.when(seen[key] == number[key])
            def _():
                send(sums.at[place], key)

    @pl.loop(0, count)
    def _(i):
        save(i).wait()

    @pl.loop(0, slots)
    def _(k):
        pltpu.make_async_copy(zero, outs[0].at[0], out_sem.at[k]).wait()


def in_hbm(value):
    return pltpu.with_memory_space_constraint(value, pltpu.HBM)


def left_products(own, coupling, partner, counts):
    pairs, blocks, width, _ = coupling.shape
    modes = own.shape[0]
    hbm = pl.BlockSpec(memory_space=pltpu.HBM)
    slots = SPAN_X + SPAN_Y
    sizes = [pairs] + [size for _, size in PARTS] + [SIDE] * 2
    out = pl.pallas_call(
        left_kernel,
        in_specs=[hbm] * 4,
        out_specs=[hbm] * len(sizes),
        out_shape=[pltpu.HBM((n, blocks, modes, width), jnp.bfloat16) for n in sizes],
        scratch_shapes=[
            pltpu.SMEM((pairs,), jnp.int32),
            pltpu.SMEM((pairs,), jnp.int32),
            pltpu.VMEM((modes, width), jnp.bfloat16),
            pltpu.VMEM((pairs * blocks, width, width), jnp.bfloat16),
            pltpu.VMEM((pairs * blocks, modes, width), jnp.bfloat16),
            pltpu.VMEM((blocks, modes, width), jnp.bfloat16),
            pltpu.VMEM((pairs // 2, blocks, modes, width), jnp.bfloat16),
            pltpu.SMEM((pairs,), jnp.int32),
            pltpu.SMEM((slots,), jnp.int32),
            pltpu.SMEM((slots,), jnp.int32),
            pltpu.SMEM((slots + 1,), jnp.int32),
            pltpu.SemaphoreType.DMA((pairs * blocks + 3,)),
            pltpu.SemaphoreType.DMA((pairs * blocks,)),
            pltpu.SemaphoreType.DMA((slots,)),
        ],
        compiler_params=pltpu.CompilerParams(vmem_limit_bytes=20 * 2**20),
        cost_estimate=pl.CostEstimate(flops=2 * pairs * blocks * modes * width * width,
                                      bytes_accessed=25 * 10**6, transcendentals=0),
    )(*map(in_hbm, (partner, counts, own, coupling)))
    return out[0], out[1:6], out[6], out[7]


def nt(a, b):
    return lax.dot_general(a, b, (((1,), (1,)), ((), ())), preferred_element_type=jnp.float32)


def pair_kernel(partner_ref, left_hbm, *rest):
    (kept, near, far, low, high, ring_mine, ring_other), out_hbm = rest[:7], rest[7]
    lefts, panels, outs, left_sem, panel_sem, out_sem = rest[8:]
    pairs, count = panels.shape[0], lefts.shape[0]

    def load(i):
        return pltpu.make_async_copy(left_hbm.at[i // 2, i % 2], lefts.at[i], left_sem.at[i])

    def save(i):
        return pltpu.make_async_copy(outs.at[i], out_hbm.at[i // 2, i % 2], out_sem.at[i])

    @pl.loop(0, pairs)
    def _(q):
        load(2 * q).start()
        load(2 * q + 1).start()
        code = partner_ref[q]
        d1, d2 = offsets(code)
        dz, core, me = ring_offset(code)
        step = jnp.where((dz == 1) | (dz == 3), jnp.where((dz == 3) == (core == 0), 1, 2), jnp.where(dz == 2, 3, 0))
        along = code < SPAN_X
        for ref, index, chosen in (
            (kept, d1, along & (d2 == 0)),
            (near, d1, along & (d2 == 1)),
            (far, d1, along & (d2 == 3)),
            (low, d1, along & (d2 == 2) & (d1 < 2)),
            (high, d1 - 2, along & (d2 == 2) & (d1 >= 2)),
            (ring_mine, step, (code >= SPAN_X) & (core == me)),
            (ring_other, step, (code >= SPAN_X) & (core != me)),
        ):
            @pl.when(chosen)
            def _():
                pltpu.make_async_copy(ref.at[index], panels.at[q], panel_sem.at[q]).start()

    @pl.loop(0, count)
    def _(i):
        p = i // 2

        @pl.when(i % 2 == 0)
        def _():
            pltpu.make_async_copy(kept.at[0], panels.at[p], panel_sem.at[p]).wait()

        load(i).wait()
        outs[i] = nt(lefts[i], panels[p]).astype(jnp.bfloat16)
        save(i).start()

    @pl.loop(0, count)
    def _(i):
        save(i).wait()


def pair_products(left, sources, partner):
    pairs, blocks, modes, width = left.shape
    hbm, smem = pl.BlockSpec(memory_space=pltpu.HBM), pl.BlockSpec(memory_space=pltpu.SMEM)
    return pl.pallas_call(
        pair_kernel,
        in_specs=[smem] + [hbm] * 8,
        out_specs=hbm,
        out_shape=jax.ShapeDtypeStruct((pairs, blocks, modes, modes), jnp.bfloat16),
        scratch_shapes=[
            pltpu.VMEM((pairs * blocks, modes, width), jnp.bfloat16),
            pltpu.VMEM((pairs, modes, width), jnp.bfloat16),
            pltpu.VMEM((pairs * blocks, modes, modes), jnp.bfloat16),
            pltpu.SemaphoreType.DMA((pairs * blocks,)),
            pltpu.SemaphoreType.DMA((pairs,)),
            pltpu.SemaphoreType.DMA((pairs * blocks,)),
        ],
        compiler_params=pltpu.CompilerParams(vmem_limit_bytes=20 * 2**20),
        cost_estimate=pl.CostEstimate(flops=2 * pairs * blocks * modes * width * modes,
                                      bytes_accessed=15 * 10**6, transcendentals=0),
    )(partner, in_hbm(left), *map(in_hbm, sources))


def partner_kernel(own_ref, sum_ref, *rest):
    last, out_ref = rest[:-1], rest[-1]

    @pl.loop(0, out_ref.shape[0])
    def _(t):
        total = sum_ref[t]
        for ref in last:
            total = total + ref[t].astype(jnp.float32)
        out_ref[t] = nt(own_ref[...], total.astype(jnp.bfloat16))


def partner_products(own, start, last):
    modes, _ = own.shape
    blocks = start.shape[0]
    return pl.pallas_call(
        partner_kernel,
        out_shape=jax.ShapeDtypeStruct((blocks, modes, modes), jnp.float32),
        compiler_params=pltpu.CompilerParams(vmem_limit_bytes=16 * 2**20),
    )(own, start, *last)


def permuted(value, move):
    pairs = []
    for n in range(SPAN_X * SPAN_Y):
        here = (n // SPAN_Y // SIDE, n // SPAN_Y % SIDE, n % SPAN_Y // 2, n % 2)
        x, y, z, c = move(*here)
        pairs.append((n, ((x % SIDE) * SIDE + y % SIDE) * SPAN_Y + (z % SIDE) * 2 + c))
    return lax.ppermute(value, ("sx", "sy"), pairs)


def first(value, by):
    return permuted(value, lambda x, y, z, c: (x + by, y, z, c) if c == 0 else (x, y + by, z, c))


def second(value, by):
    return permuted(value, lambda x, y, z, c: (x, y + by, z, c) if c == 0 else (x + by, y, z, c))


def turn(value, by):
    return permuted(value, lambda x, y, z, c: (x, y, z + (by if c == 0 else -by), c))


def swap(value):
    return permuted(value, lambda x, y, z, c: (x, y, z, 1 - c))


def added(*terms):
    return sum(v.astype(jnp.float32) for v in terms)


def rounded(*terms):
    return added(*terms).astype(jnp.bfloat16)


def after(value, *others):
    return lax.optimization_barrier((value,) + others)[0]


def body(panels, coupling, partner, counts):
    own = jnp.swapaxes(panels[0], 0, 1)
    barrier = lax.optimization_barrier

    moved = [first(own, -1), first(own, 2), first(own, 1)]
    ring1, ring2 = turn(own, 1), turn(own, -1)
    kept = jnp.stack([own] + moved)
    left, (up, down, pass_up, pass_down, here), z_other, z_mine = left_products(own, coupling, partner, counts)
    kept, ring1, ring2, up, down, z_other, own_z = barrier((kept, ring1, ring2, up, down, z_other, own))

    got = [first(up, 1), first(down, -1)]
    near, far = second(kept, -1), second(kept, 1)
    ring3 = turn(own_z, 2)
    ring_mine = jnp.stack([own, ring1, ring2, ring3])
    pair_sum = swap(z_other)
    got, near, far, ring_mine, pair_sum = barrier((got, near, far, ring_mine, pair_sum))
    got_up, got_down = got

    last = [first(rounded(pass_up, got_up[:2]), 1), first(rounded(pass_down, got_down[:2]), -1)]
    low, high = second(near[:2], -1), second(far[2:], 1)
    ring_other = swap(ring_mine)
    w = [rounded(z_mine[k], pair_sum[k]) for k in range(SIDE)]
    z1 = turn(w[1], 1)
    last, low, high, ring_other, w, z1 = barrier((last, low, high, ring_other, w, z1))
    last_up, last_down = last

    v = [
        rounded(here[0], got_down[2], last_up[0]),
        rounded(here[1], got_down[3], last_up[1]),
        rounded(here[2], got_up[2], last_down[0]),
        rounded(here[3], got_up[3], last_down[1]),
    ]
    v, w = barrier((v, w))
    z3, z2 = turn(w[3], 2), turn(w[2], -1)
    ends = [second(v[1], 1), second(v[3], -1), second(v[2], 2)]

    sources = [kept, near, far, low, high, ring_mine, ring_other]
    pair_blocks = pair_products(left, sources, after(partner, *v))
    pair_blocks, z2, z3, ends = barrier((pair_blocks, z2, z3, ends))
    partner_blocks = partner_products(own, added(v[0], w[0], z1, z2, z3), ends)
    return (pair_blocks, partner_blocks[None])


def solution(mesh):
    placed = (
        P(("sx", "sy"), None, None),
        P(("sx", "sy"), None, None, None),
        P(("sx", "sy")),
        P(("sx", "sy")),
    )
    return jax.shard_map(
        body,
        mesh=mesh,
        in_specs=placed,
        out_specs=(P(("sx", "sy"), None, None, None), P(("sx", "sy"), None, None, None)),
        check_vma=False,
    )
```

```python
import jax
import jax.numpy as jnp
from jax import lax
from jax.experimental import pallas as pl
from jax.experimental.pallas import tpu as pltpu
from jax.sharding import PartitionSpec as P

SIDE = 4
SPAN_X, SPAN_Y = SIDE * SIDE, 2 * SIDE
PARTS = ((0, 4), (4, 4), (8, 2), (10, 2), (12, 4))
CHUNK = 80


def slot_of(d1, d2):
    low = d2 < 2
    return jnp.where(
        d1 == 0, 12 + d2,
        jnp.where(d1 == 1, jnp.where(low, 8 + d2, d2),
                  jnp.where(d1 == 2, jnp.where(low, d2, 2 + d2), jnp.where(low, 6 + d2, 8 + d2))))


def offsets(code):
    me = lax.axis_index("sx")
    dx = (code // SIDE - me // SIDE + SIDE) % SIDE
    dy = (code % SIDE - me % SIDE + SIDE) % SIDE
    swapped = lax.axis_index("sy") % 2 == 1
    return jnp.where(swapped, dy, dx), jnp.where(swapped, dx, dy)


def ring_offset(code):
    me = lax.axis_index("sy")
    other = code - SPAN_X
    return (other // 2 - me // 2 + SIDE) % SIDE, other % 2, me % 2


def left_kernel(partner_hbm, counts_hbm, own_hbm, coupling_hbm, left_hbm, *rest):
    outs = rest[:7]
    partner_ref, counts_ref, own_ref, blocks, lefts, zero, sums = rest[7:14]
    keys, number, seen, at_sum, in_sem, left_sem, out_sem = rest[14:]
    count, pairs = blocks.shape[0], keys.shape[0]
    modes, width = own_ref.shape
    slots = SPAN_X + SPAN_Y

    def load(i):
        return pltpu.make_async_copy(coupling_hbm.at[i // 2, i % 2], blocks.at[i], in_sem.at[i])

    def save(i):
        return pltpu.make_async_copy(lefts.at[i], left_hbm.at[i // 2, i % 2], left_sem.at[i])

    load_partner = pltpu.make_async_copy(partner_hbm, partner_ref, in_sem.at[count + 1])
    load_partner.start()
    load_counts = pltpu.make_async_copy(counts_hbm, counts_ref, in_sem.at[count + 2])
    load_counts.start()
    load_own = pltpu.make_async_copy(own_hbm, own_ref, in_sem.at[count])
    load_own.start()

    @pl.loop(0, count)
    def _(i):
        load(i).start()

    @pl.loop(0, slots)
    def _(k):
        number[k] = 0
        seen[k] = 0

    at_sum[slots] = 0
    load_partner.wait()
    load_counts.wait()

    @pl.loop(0, pairs)
    def _(p):
        code = partner_ref[p]
        d1, d2 = offsets(code)
        dz, core, me = ring_offset(code)
        step = jnp.where((dz == 1) | (dz == 3), jnp.where((dz == 1) == (core == 0), 1, 2), jnp.where(dz == 2, 3, 0))
        key = jnp.where(code < SPAN_X, slot_of(d1, d2), SPAN_X + step + jnp.where(core == me, SIDE, 0))
        keys[p] = key
        number[key] = number[key] + 1

    @pl.loop(0, 2 * (modes // CHUNK))
    def _(r):
        rows = pl.ds(pl.multiple_of(r // 2 * CHUNK, CHUNK), CHUNK)
        zero[r % 2, rows] = jnp.zeros((CHUNK, width), zero.dtype)

    def send(source, key):
        for out, (at, size) in zip(outs, PARTS + ((SPAN_X, SIDE), (SPAN_X + SIDE, SIDE)), strict=True):
            @pl.when((key >= at) & (key < at + size))
            def _():
                pltpu.make_async_copy(source, out.at[key - at], out_sem.at[key]).start()

    @pl.loop(0, slots)
    def _(k):
        @pl.when(number[k] == 0)
        def _():
            send(zero, k)

    load_own.wait()

    @pl.loop(0, count)
    def _(i):
        p = i // 2
        load(i).wait()
        keep = lax.broadcasted_iota(jnp.int32, (1, width), 1) < counts_ref[p]
        own = jnp.where(keep, own_ref[...], jnp.zeros((modes, width), own_ref.dtype))
        product = jnp.dot(own, blocks[i], preferred_element_type=jnp.float32)
        lefts[i] = jnp.where(keep, product, 0.0).astype(jnp.bfloat16)
        save(i).start()
        key = keys[p]
        single = number[key] == 1

        @pl.when((i % 2 == 1) & single)
        def _():
            send(lefts.at[pl.ds(i - 1, 2)], key)

        @pl.when((i % 2 == 1) & jnp.logical_not(single))
        def _():
            fresh = seen[key] == 0

            @pl.when(fresh)
            def _():
                at_sum[key] = at_sum[slots]
                at_sum[slots] = at_sum[slots] + 1

            seen[key] = seen[key] + 1
            place = at_sum[key]

            @pl.loop(0, 2 * (modes // CHUNK))
            def _(r):
                t, rows = r % 2, pl.ds(pl.multiple_of(r // 2 * CHUNK, CHUNK), CHUNK)
                before = jnp.where(fresh, 0.0, sums[place, t, rows].astype(jnp.float32))
                sums[place, t, rows] = (before + lefts[i - 1 + t, rows].astype(jnp.float32)).astype(jnp.bfloat16)

            @pl.when(seen[key] == number[key])
            def _():
                send(sums.at[place], key)

    @pl.loop(0, count)
    def _(i):
        save(i).wait()

    @pl.loop(0, slots)
    def _(k):
        pltpu.make_async_copy(zero, outs[0].at[0], out_sem.at[k]).wait()


def in_hbm(value):
    return pltpu.with_memory_space_constraint(value, pltpu.HBM)


def left_products(own, coupling, partner, counts):
    pairs, blocks, width, _ = coupling.shape
    modes = own.shape[0]
    hbm = pl.BlockSpec(memory_space=pltpu.HBM)
    slots = SPAN_X + SPAN_Y
    sizes = [pairs] + [size for _, size in PARTS] + [SIDE] * 2
    out = pl.pallas_call(
        left_kernel,
        in_specs=[hbm] * 4,
        out_specs=[hbm] * len(sizes),
        out_shape=[pltpu.HBM((n, blocks, modes, width), jnp.bfloat16) for n in sizes],
        scratch_shapes=[
            pltpu.SMEM((pairs,), jnp.int32),
            pltpu.SMEM((pairs,), jnp.int32),
            pltpu.VMEM((modes, width), jnp.bfloat16),
            pltpu.VMEM((pairs * blocks, width, width), jnp.bfloat16),
            pltpu.VMEM((pairs * blocks, modes, width), jnp.bfloat16),
            pltpu.VMEM((blocks, modes, width), jnp.bfloat16),
            pltpu.VMEM((pairs // 2, blocks, modes, width), jnp.bfloat16),
            pltpu.SMEM((pairs,), jnp.int32),
            pltpu.SMEM((slots,), jnp.int32),
            pltpu.SMEM((slots,), jnp.int32),
            pltpu.SMEM((slots + 1,), jnp.int32),
            pltpu.SemaphoreType.DMA((pairs * blocks + 3,)),
            pltpu.SemaphoreType.DMA((pairs * blocks,)),
            pltpu.SemaphoreType.DMA((slots,)),
        ],
        compiler_params=pltpu.CompilerParams(vmem_limit_bytes=20 * 2**20),
        cost_estimate=pl.CostEstimate(flops=2 * pairs * blocks * modes * width * width,
                                      bytes_accessed=25 * 10**6, transcendentals=0),
    )(*map(in_hbm, (partner, counts, own, coupling)))
    return out[0], out[1:6], out[6], out[7]


def nt(a, b):
    return lax.dot_general(a, b, (((1,), (1,)), ((), ())), preferred_element_type=jnp.float32)


def pair_kernel(partner_ref, left_hbm, *rest):
    (kept, near, far, low, high, ring_mine, ring_other), out_hbm = rest[:7], rest[7]
    lefts, panels, outs, left_sem, panel_sem, out_sem = rest[8:]
    pairs, count = panels.shape[0], lefts.shape[0]

    def load(i):
        return pltpu.make_async_copy(left_hbm.at[i // 2, i % 2], lefts.at[i], left_sem.at[i])

    def save(i):
        return pltpu.make_async_copy(outs.at[i], out_hbm.at[i // 2, i % 2], out_sem.at[i])

    @pl.loop(0, pairs)
    def _(q):
        load(2 * q).start()
        load(2 * q + 1).start()
        code = partner_ref[q]
        d1, d2 = offsets(code)
        dz, core, me = ring_offset(code)
        step = jnp.where((dz == 1) | (dz == 3), jnp.where((dz == 3) == (core == 0), 1, 2), jnp.where(dz == 2, 3, 0))
        along = code < SPAN_X
        for ref, index, chosen in (
            (kept, d1, along & (d2 == 0)),
            (near, d1, along & (d2 == 1)),
            (far, d1, along & (d2 == 3)),
            (low, d1, along & (d2 == 2) & (d1 < 2)),
            (high, d1 - 2, along & (d2 == 2) & (d1 >= 2)),
            (ring_mine, step, (code >= SPAN_X) & (core == me)),
            (ring_other, step, (code >= SPAN_X) & (core != me)),
        ):
            @pl.when(chosen)
            def _():
                pltpu.make_async_copy(ref.at[index], panels.at[q], panel_sem.at[q]).start()

    @pl.loop(0, count)
    def _(i):
        p = i // 2

        @pl.when(i % 2 == 0)
        def _():
            pltpu.make_async_copy(kept.at[0], panels.at[p], panel_sem.at[p]).wait()

        load(i).wait()
        outs[i] = nt(lefts[i], panels[p]).astype(jnp.bfloat16)
        save(i).start()

    @pl.loop(0, count)
    def _(i):
        save(i).wait()


def pair_products(left, sources, partner):
    pairs, blocks, modes, width = left.shape
    hbm, smem = pl.BlockSpec(memory_space=pltpu.HBM), pl.BlockSpec(memory_space=pltpu.SMEM)
    return pl.pallas_call(
        pair_kernel,
        in_specs=[smem] + [hbm] * 8,
        out_specs=hbm,
        out_shape=jax.ShapeDtypeStruct((pairs, blocks, modes, modes), jnp.bfloat16),
        scratch_shapes=[
            pltpu.VMEM((pairs * blocks, modes, width), jnp.bfloat16),
            pltpu.VMEM((pairs, modes, width), jnp.bfloat16),
            pltpu.VMEM((pairs * blocks, modes, modes), jnp.bfloat16),
            pltpu.SemaphoreType.DMA((pairs * blocks,)),
            pltpu.SemaphoreType.DMA((pairs,)),
            pltpu.SemaphoreType.DMA((pairs * blocks,)),
        ],
        compiler_params=pltpu.CompilerParams(vmem_limit_bytes=20 * 2**20),
        cost_estimate=pl.CostEstimate(flops=2 * pairs * blocks * modes * width * modes,
                                      bytes_accessed=15 * 10**6, transcendentals=0),
    )(partner, in_hbm(left), *map(in_hbm, sources))


def partner_kernel(own_ref, sum_ref, *rest):
    last, out_ref = rest[:-1], rest[-1]

    @pl.loop(0, out_ref.shape[0])
    def _(t):
        total = sum_ref[t]
        for ref in last:
            total = total + ref[t].astype(jnp.float32)
        out_ref[t] = nt(own_ref[...], total.astype(jnp.bfloat16))


def partner_products(own, start, last):
    modes, _ = own.shape
    blocks = start.shape[0]
    return pl.pallas_call(
        partner_kernel,
        out_shape=jax.ShapeDtypeStruct((blocks, modes, modes), jnp.float32),
        compiler_params=pltpu.CompilerParams(vmem_limit_bytes=16 * 2**20),
    )(own, start, *last)


def permuted(value, move):
    pairs = []
    for n in range(SPAN_X * SPAN_Y):
        here = (n // SPAN_Y // SIDE, n // SPAN_Y % SIDE, n % SPAN_Y // 2, n % 2)
        x, y, z, c = move(*here)
        pairs.append((n, ((x % SIDE) * SIDE + y % SIDE) * SPAN_Y + (z % SIDE) * 2 + c))
    return lax.ppermute(value, ("sx", "sy"), pairs)


def first(value, by):
    return permuted(value, lambda x, y, z, c: (x + by, y, z, c) if c == 0 else (x, y + by, z, c))


def second(value, by):
    return permuted(value, lambda x, y, z, c: (x, y + by, z, c) if c == 0 else (x + by, y, z, c))


def turn(value, by):
    return permuted(value, lambda x, y, z, c: (x, y, z + (by if c == 0 else -by), c))


def swap(value):
    return permuted(value, lambda x, y, z, c: (x, y, z, 1 - c))


def added(*terms):
    return sum(v.astype(jnp.float32) for v in terms)


def rounded(*terms):
    return added(*terms).astype(jnp.bfloat16)


def after(value, *others):
    return lax.optimization_barrier((value,) + others)[0]


def body(panels, coupling, partner, counts):
    own = jnp.swapaxes(panels[0], 0, 1)
    barrier = lax.optimization_barrier

    moved = [first(own, -1), first(own, 2), first(own, 1)]
    ring1, ring2 = turn(own, 1), turn(own, -1)
    kept = jnp.stack([own] + moved)
    left, (up, down, pass_up, pass_down, here), z_other, z_mine = left_products(own, coupling, partner, counts)
    kept, ring1, ring2, up, down, z_other, own_z = barrier((kept, ring1, ring2, up, down, z_other, own))

    got = [first(up, 1), first(down, -1)]
    near, far = second(kept, -1), second(kept, 1)
    ring3 = turn(own_z, 2)
    ring_mine = jnp.stack([own, ring1, ring2, ring3])
    pair_sum = swap(z_other)
    w = [rounded(z_mine[k], pair_sum[k]) for k in range(SIDE)]
    z1 = turn(w[1], 1)
    got, near, far, ring_mine, w, z1 = barrier((got, near, far, ring_mine, w, z1))
    got_up, got_down = got

    b_up, b_down = rounded(pass_up, got_up[:2]), rounded(pass_down, got_down[:2])
    b_up, b_down, near, far, ring_mine, w = barrier((b_up, b_down, near, far, ring_mine, w))
    last = [first(b_up, 1), first(b_down, -1)]
    low, high = second(near[:2], -1), second(far[2:], 1)
    ring_other = swap(ring_mine)
    z2 = turn(w[2], -1)
    z3 = turn(after(w[3], z2), 2)
    last, low, high, ring_other, z2, z3 = barrier((last, low, high, ring_other, z2, z3))
    last_up, last_down = last

    v = [
        rounded(here[0], got_down[2], last_up[0]),
        rounded(here[1], got_down[3], last_up[1]),
        rounded(here[2], got_up[2], last_down[0]),
        rounded(here[3], got_up[3], last_down[1]),
    ]
    ends = [second(v[1], 1), second(v[3], -1), second(v[2], 2)]

    sources = [kept, near, far, low, high, ring_mine, ring_other]
    pair_blocks = pair_products(left, sources, after(partner, *v))
    pair_blocks, ends = barrier((pair_blocks, ends))
    partner_blocks = partner_products(own, added(v[0], w[0], z1, z2, z3), ends)
    return (pair_blocks, partner_blocks[None])


def solution(mesh):
    placed = (
        P(("sx", "sy"), None, None),
        P(("sx", "sy"), None, None, None),
        P(("sx", "sy")),
        P(("sx", "sy")),
    )
    return jax.shard_map(
        body,
        mesh=mesh,
        in_specs=placed,
        out_specs=(P(("sx", "sy"), None, None, None), P(("sx", "sy"), None, None, None)),
        check_vma=False,
    )
```

```python
import jax
import jax.numpy as jnp
from jax import lax
from jax.experimental import pallas as pl
from jax.experimental.pallas import tpu as pltpu
from jax.sharding import PartitionSpec as P

SIDE = 4
SPAN_X, SPAN_Y = SIDE * SIDE, 2 * SIDE
PARTS = ((0, 4), (4, 4), (8, 2), (10, 2), (12, 4))
CHUNK = 80


def slot_of(d1, d2):
    low = d2 < 2
    return jnp.where(
        d1 == 0, 12 + d2,
        jnp.where(d1 == 1, jnp.where(low, 8 + d2, d2),
                  jnp.where(d1 == 2, jnp.where(low, d2, 2 + d2), jnp.where(low, 6 + d2, 8 + d2))))


def offsets(code):
    me = lax.axis_index("sx")
    dx = (code // SIDE - me // SIDE + SIDE) % SIDE
    dy = (code % SIDE - me % SIDE + SIDE) % SIDE
    swapped = lax.axis_index("sy") % 2 == 1
    return jnp.where(swapped, dy, dx), jnp.where(swapped, dx, dy)


def ring_offset(code):
    me = lax.axis_index("sy")
    other = code - SPAN_X
    return (other // 2 - me // 2 + SIDE) % SIDE, other % 2, me % 2


def left_kernel(partner_hbm, counts_hbm, own_hbm, coupling_hbm, left_ref, *rest):
    outs = rest[:7]
    partner_ref, counts_ref, own_ref, blocks, used, in_sem = rest[7:]
    count, pairs = blocks.shape[0], left_ref.shape[0]
    modes, width = own_ref.shape
    places = PARTS + ((SPAN_X, SIDE), (SPAN_X + SIDE, SIDE))
    chunks = modes // CHUNK

    def load(i):
        return pltpu.make_async_copy(coupling_hbm.at[i // 2, i % 2], blocks.at[i], in_sem.at[i])

    load_partner = pltpu.make_async_copy(partner_hbm, partner_ref, in_sem.at[count + 1])
    load_partner.start()
    load_counts = pltpu.make_async_copy(counts_hbm, counts_ref, in_sem.at[count + 2])
    load_counts.start()
    load_own = pltpu.make_async_copy(own_hbm, own_ref, in_sem.at[count])
    load_own.start()

    @pl.loop(0, count)
    def _(i):
        load(i).start()

    @pl.loop(0, SPAN_X + SPAN_Y)
    def _(k):
        used[k] = 0

    def key_of(p):
        code = partner_ref[p]
        d1, d2 = offsets(code)
        dz, core, me = ring_offset(code)
        step = jnp.where((dz == 1) | (dz == 3), jnp.where((dz == 1) == (core == 0), 1, 2), jnp.where(dz == 2, 3, 0))
        return jnp.where(code < SPAN_X, slot_of(d1, d2), SPAN_X + step + jnp.where(core == me, SIDE, 0))

    def rows(r):
        return r % 2, pl.ds(pl.multiple_of(r // 2 * CHUNK, CHUNK), CHUNK)

    load_partner.wait()
    load_counts.wait()
    load_own.wait()

    @pl.loop(0, count)
    def _(i):
        p, t = i // 2, i % 2
        load(i).wait()
        keep = lax.broadcasted_iota(jnp.int32, (1, width), 1) < counts_ref[p]
        own = jnp.where(keep, own_ref[...], jnp.zeros((modes, width), own_ref.dtype))
        product = jnp.dot(own, blocks[i], preferred_element_type=jnp.float32)
        left_ref[p, t] = jnp.where(keep, product, 0.0).astype(jnp.bfloat16)

        @pl.when(t == 1)
        def _():
            key = key_of(p)
            fresh = used[key] == 0
            used[key] = 1
            for out, (at, size) in zip(outs, places, strict=True):
                here = (key >= at) & (key < at + size)

                @pl.when(here & fresh)
                def _():
                    @pl.loop(0, 2 * chunks)
                    def _(r):
                        b, some = rows(r)
                        out[key - at, b, some] = left_ref[p, b, some]

                @pl.when(here & jnp.logical_not(fresh))
                def _():
                    @pl.loop(0, 2 * chunks)
                    def _(r):
                        b, some = rows(r)
                        total = out[key - at, b, some].astype(jnp.float32) + left_ref[p, b, some].astype(jnp.float32)
                        out[key - at, b, some] = total.astype(jnp.bfloat16)

    for out, (at, size) in zip(outs, places, strict=True):
        @pl.loop(0, size)
        def _(k):
            @pl.when(used[at + k] == 0)
            def _():
                @pl.loop(0, 2 * chunks)
                def _(r):
                    b, some = rows(r)
                    out[k, b, some] = jnp.zeros((CHUNK, width), out.dtype)


def in_hbm(value):
    return pltpu.with_memory_space_constraint(value, pltpu.HBM)


def left_products(own, coupling, partner, counts):
    pairs, blocks, width, _ = coupling.shape
    modes = own.shape[0]
    slots = SPAN_X + SPAN_Y
    sizes = [pairs] + [size for _, size in PARTS] + [SIDE] * 2
    out = pl.pallas_call(
        left_kernel,
        in_specs=[pl.BlockSpec(memory_space=pltpu.HBM)] * 4,
        out_specs=[pl.BlockSpec(memory_space=pltpu.VMEM)] * len(sizes),
        out_shape=[pltpu.VMEM((n, blocks, modes, width), jnp.bfloat16) for n in sizes],
        scratch_shapes=[
            pltpu.SMEM((pairs,), jnp.int32),
            pltpu.SMEM((pairs,), jnp.int32),
            pltpu.VMEM((modes, width), jnp.bfloat16),
            pltpu.VMEM((pairs * blocks, width, width), jnp.bfloat16),
            pltpu.SMEM((slots,), jnp.int32),
            pltpu.SemaphoreType.DMA((pairs * blocks + 3,)),
        ],
        compiler_params=pltpu.CompilerParams(vmem_limit_bytes=8 * 2**20),
        cost_estimate=pl.CostEstimate(flops=2 * pairs * blocks * modes * width * width,
                                      bytes_accessed=25 * 10**6, transcendentals=0),
    )(*map(in_hbm, (partner, counts, own, coupling)))
    return out[0], out[1:6], out[6], out[7]


def nt(a, b):
    return lax.dot_general(a, b, (((1,), (1,)), ((), ())), preferred_element_type=jnp.float32)


def pair_kernel(partner_ref, left_ref, *rest):
    (kept, near, far, low, high, ring_mine, ring_other), out_hbm = rest[:7], rest[7]
    panels, outs, panel_sem, out_sem = rest[8:]
    pairs, count = panels.shape[0], outs.shape[0]

    def save(i):
        return pltpu.make_async_copy(outs.at[i], out_hbm.at[i // 2, i % 2], out_sem.at[i])

    @pl.loop(0, pairs)
    def _(q):
        code = partner_ref[q]
        d1, d2 = offsets(code)
        dz, core, me = ring_offset(code)
        step = jnp.where((dz == 1) | (dz == 3), jnp.where((dz == 3) == (core == 0), 1, 2), jnp.where(dz == 2, 3, 0))
        along = code < SPAN_X
        for ref, index, chosen in (
            (kept, d1, along & (d2 == 0)),
            (near, d1, along & (d2 == 1)),
            (far, d1, along & (d2 == 3)),
            (low, d1, along & (d2 == 2) & (d1 < 2)),
            (high, d1 - 2, along & (d2 == 2) & (d1 >= 2)),
            (ring_mine, step, (code >= SPAN_X) & (core == me)),
            (ring_other, step, (code >= SPAN_X) & (core != me)),
        ):
            @pl.when(chosen)
            def _():
                pltpu.make_async_copy(ref.at[index], panels.at[q], panel_sem.at[q]).start()

    @pl.loop(0, count)
    def _(i):
        p = i // 2

        @pl.when(i % 2 == 0)
        def _():
            pltpu.make_async_copy(kept.at[0], panels.at[p], panel_sem.at[p]).wait()

        outs[i] = nt(left_ref[p, i % 2], panels[p]).astype(jnp.bfloat16)
        save(i).start()

    @pl.loop(0, count)
    def _(i):
        save(i).wait()


def pair_products(left, sources, partner):
    pairs, blocks, modes, width = left.shape
    hbm, smem = pl.BlockSpec(memory_space=pltpu.HBM), pl.BlockSpec(memory_space=pltpu.SMEM)
    return pl.pallas_call(
        pair_kernel,
        in_specs=[smem, pl.BlockSpec(memory_space=pltpu.VMEM)] + [pl.BlockSpec(memory_space=pl.ANY)] * 7,
        out_specs=hbm,
        out_shape=jax.ShapeDtypeStruct((pairs, blocks, modes, modes), jnp.bfloat16),
        scratch_shapes=[
            pltpu.VMEM((pairs, modes, width), jnp.bfloat16),
            pltpu.VMEM((pairs * blocks, modes, modes), jnp.bfloat16),
            pltpu.SemaphoreType.DMA((pairs,)),
            pltpu.SemaphoreType.DMA((pairs * blocks,)),
        ],
        compiler_params=pltpu.CompilerParams(vmem_limit_bytes=14 * 2**20),
        cost_estimate=pl.CostEstimate(flops=2 * pairs * blocks * modes * width * modes,
                                      bytes_accessed=15 * 10**6, transcendentals=0),
    )(partner, left, *sources)


def partner_kernel(own_ref, sum_ref, *rest):
    last, out_ref = rest[:-1], rest[-1]

    @pl.loop(0, out_ref.shape[0])
    def _(t):
        total = sum_ref[t]
        for ref in last:
            total = total + ref[t].astype(jnp.float32)
        out_ref[t] = nt(own_ref[...], total.astype(jnp.bfloat16))


def partner_products(own, start, last):
    modes, _ = own.shape
    blocks = start.shape[0]
    return pl.pallas_call(
        partner_kernel,
        out_shape=jax.ShapeDtypeStruct((blocks, modes, modes), jnp.float32),
        compiler_params=pltpu.CompilerParams(vmem_limit_bytes=16 * 2**20),
    )(own, start, *last)


def permuted(value, move):
    pairs = []
    for n in range(SPAN_X * SPAN_Y):
        here = (n // SPAN_Y // SIDE, n // SPAN_Y % SIDE, n % SPAN_Y // 2, n % 2)
        x, y, z, c = move(*here)
        pairs.append((n, ((x % SIDE) * SIDE + y % SIDE) * SPAN_Y + (z % SIDE) * 2 + c))
    return lax.ppermute(value, ("sx", "sy"), pairs)


def first(value, by):
    return permuted(value, lambda x, y, z, c: (x + by, y, z, c) if c == 0 else (x, y + by, z, c))


def second(value, by):
    return permuted(value, lambda x, y, z, c: (x, y + by, z, c) if c == 0 else (x + by, y, z, c))


def turn(value, by):
    return permuted(value, lambda x, y, z, c: (x, y, z + (by if c == 0 else -by), c))


def swap(value):
    return permuted(value, lambda x, y, z, c: (x, y, z, 1 - c))


def added(*terms):
    return sum(v.astype(jnp.float32) for v in terms)


def rounded(*terms):
    return added(*terms).astype(jnp.bfloat16)


def after(value, *others):
    return lax.optimization_barrier((value,) + others)[0]


def body(panels, coupling, partner, counts):
    own = jnp.swapaxes(panels[0], 0, 1)
    barrier = lax.optimization_barrier

    moved = [first(own, -1), first(own, 2), first(own, 1)]
    ring1, ring2 = turn(own, 1), turn(own, -1)
    kept = jnp.stack([own] + moved)
    left, (up, down, pass_up, pass_down, here), z_other, z_mine = left_products(own, coupling, partner, counts)
    kept, ring1, ring2, up, down, z_other, own_z = barrier((kept, ring1, ring2, up, down, z_other, own))

    got = [first(up, 1), first(down, -1)]
    near, far = second(kept, -1), second(kept, 1)
    ring3 = turn(own_z, 2)
    ring_mine = jnp.stack([own, ring1, ring2, ring3])
    pair_sum = swap(z_other)
    w = [rounded(z_mine[k], pair_sum[k]) for k in range(SIDE)]
    z1, z2, z3 = turn(w[1], 1), turn(w[2], -1), turn(w[3], 2)
    got, near, far, ring_mine, w, z1, z2, z3 = barrier((got, near, far, ring_mine, w, z1, z2, z3))
    got_up, got_down = got

    b_up, b_down = rounded(pass_up, got_up[:2]), rounded(pass_down, got_down[:2])
    b_up, b_down, near, far, ring_mine = barrier((b_up, b_down, near, far, ring_mine))
    low, high = second(near[:2], -1), second(far[2:], 1)
    ring_other = swap(ring_mine)
    last = [first(b_up, 1), first(b_down, -1)]
    last, low, high, ring_other = barrier((last, low, high, ring_other))
    last_up, last_down = last

    v = [
        rounded(here[0], got_down[2], last_up[0]),
        rounded(here[1], got_down[3], last_up[1]),
        rounded(here[2], got_up[2], last_down[0]),
        rounded(here[3], got_up[3], last_down[1]),
    ]
    ends = [second(v[1], 1), second(v[3], -1), second(v[2], 2)]

    sources = [kept, near, far, low, high, ring_mine, ring_other]
    pair_blocks = pair_products(left, sources, after(partner, *v))
    pair_blocks, ends = barrier((pair_blocks, ends))
    partner_blocks = partner_products(own, added(v[0], w[0], z1, z2, z3), ends)
    return (pair_blocks, partner_blocks[None])


def solution(mesh):
    placed = (
        P(("sx", "sy"), None, None),
        P(("sx", "sy"), None, None, None),
        P(("sx", "sy")),
        P(("sx", "sy")),
    )
    return jax.shard_map(
        body,
        mesh=mesh,
        in_specs=placed,
        out_specs=(P(("sx", "sy"), None, None, None), P(("sx", "sy"), None, None, None)),
        check_vma=False,
    )
```

```python
import jax
import jax.numpy as jnp
from jax import lax
from jax.experimental import pallas as pl
from jax.experimental.pallas import tpu as pltpu
from jax.sharding import PartitionSpec as P

SIDE = 4
SPAN_X, SPAN_Y = SIDE * SIDE, 2 * SIDE
PARTS = ((0, 4), (4, 4), (8, 2), (10, 2), (12, 4))
CHUNK = 80


def slot_of(d1, d2):
    low = d2 < 2
    return jnp.where(
        d1 == 0, 12 + d2,
        jnp.where(d1 == 1, jnp.where(low, 8 + d2, d2),
                  jnp.where(d1 == 2, jnp.where(low, d2, 2 + d2), jnp.where(low, 6 + d2, 8 + d2))))


def offsets(code):
    me = lax.axis_index("sx")
    dx = (code // SIDE - me // SIDE + SIDE) % SIDE
    dy = (code % SIDE - me % SIDE + SIDE) % SIDE
    swapped = lax.axis_index("sy") % 2 == 1
    return jnp.where(swapped, dy, dx), jnp.where(swapped, dx, dy)


def ring_offset(code):
    me = lax.axis_index("sy")
    other = code - SPAN_X
    return (other // 2 - me // 2 + SIDE) % SIDE, other % 2, me % 2


def left_kernel(partner_hbm, counts_hbm, own_hbm, coupling_hbm, left_ref, *rest):
    outs = rest[:7]
    partner_ref, counts_ref, own_ref, blocks, zero, sums = rest[7:13]
    keys, number, seen, at_sum, in_sem, out_sem = rest[13:]
    count, pairs = blocks.shape[0], keys.shape[0]
    modes, width = own_ref.shape
    slots = SPAN_X + SPAN_Y

    def load(i):
        return pltpu.make_async_copy(coupling_hbm.at[i // 2, i % 2], blocks.at[i], in_sem.at[i])

    load_partner = pltpu.make_async_copy(partner_hbm, partner_ref, in_sem.at[count + 1])
    load_partner.start()
    load_counts = pltpu.make_async_copy(counts_hbm, counts_ref, in_sem.at[count + 2])
    load_counts.start()
    load_own = pltpu.make_async_copy(own_hbm, own_ref, in_sem.at[count])
    load_own.start()

    @pl.loop(0, count)
    def _(i):
        load(i).start()

    @pl.loop(0, slots)
    def _(k):
        number[k] = 0
        seen[k] = 0

    at_sum[slots] = 0
    load_partner.wait()
    load_counts.wait()

    @pl.loop(0, pairs)
    def _(p):
        code = partner_ref[p]
        d1, d2 = offsets(code)
        dz, core, me = ring_offset(code)
        step = jnp.where((dz == 1) | (dz == 3), jnp.where((dz == 1) == (core == 0), 1, 2), jnp.where(dz == 2, 3, 0))
        key = jnp.where(code < SPAN_X, slot_of(d1, d2), SPAN_X + step + jnp.where(core == me, SIDE, 0))
        keys[p] = key
        number[key] = number[key] + 1

    @pl.loop(0, 2 * (modes // CHUNK))
    def _(r):
        rows = pl.ds(pl.multiple_of(r // 2 * CHUNK, CHUNK), CHUNK)
        zero[r % 2, rows] = jnp.zeros((CHUNK, width), zero.dtype)

    def send(source, key):
        for out, (at, size) in zip(outs, PARTS + ((SPAN_X, SIDE), (SPAN_X + SIDE, SIDE)), strict=True):
            @pl.when((key >= at) & (key < at + size))
            def _():
                pltpu.make_async_copy(source, out.at[key - at], out_sem.at[key]).start()

    @pl.loop(0, slots)
    def _(k):
        @pl.when(number[k] == 0)
        def _():
            send(zero, k)

    load_own.wait()

    @pl.loop(0, count)
    def _(i):
        p = i // 2
        load(i).wait()
        keep = lax.broadcasted_iota(jnp.int32, (1, width), 1) < counts_ref[p]
        own = jnp.where(keep, own_ref[...], jnp.zeros((modes, width), own_ref.dtype))
        product = jnp.dot(own, blocks[i], preferred_element_type=jnp.float32)
        left_ref[p, i % 2] = jnp.where(keep, product, 0.0).astype(jnp.bfloat16)
        key = keys[p]
        single = number[key] == 1

        @pl.when((i % 2 == 1) & single)
        def _():
            send(left_ref.at[p], key)

        @pl.when((i % 2 == 1) & jnp.logical_not(single))
        def _():
            fresh = seen[key] == 0

            @pl.when(fresh)
            def _():
                at_sum[key] = at_sum[slots]
                at_sum[slots] = at_sum[slots] + 1

            seen[key] = seen[key] + 1
            place = at_sum[key]

            @pl.loop(0, 2 * (modes // CHUNK))
            def _(r):
                t, rows = r % 2, pl.ds(pl.multiple_of(r // 2 * CHUNK, CHUNK), CHUNK)
                before = jnp.where(fresh, 0.0, sums[place, t, rows].astype(jnp.float32))
                sums[place, t, rows] = (before + left_ref[p, t, rows].astype(jnp.float32)).astype(jnp.bfloat16)

            @pl.when(seen[key] == number[key])
            def _():
                send(sums.at[place], key)

    @pl.loop(0, slots)
    def _(k):
        pltpu.make_async_copy(zero, outs[0].at[0], out_sem.at[k]).wait()


def in_hbm(value):
    return pltpu.with_memory_space_constraint(value, pltpu.HBM)


def left_products(own, coupling, partner, counts):
    pairs, blocks, width, _ = coupling.shape
    modes = own.shape[0]
    slots = SPAN_X + SPAN_Y
    sizes = [pairs] + [size for _, size in PARTS] + [SIDE] * 2
    out = pl.pallas_call(
        left_kernel,
        in_specs=[pl.BlockSpec(memory_space=pltpu.HBM)] * 4,
        out_specs=[pl.BlockSpec(memory_space=pltpu.VMEM)] * len(sizes),
        out_shape=[pltpu.VMEM((n, blocks, modes, width), jnp.bfloat16) for n in sizes],
        scratch_shapes=[
            pltpu.SMEM((pairs,), jnp.int32),
            pltpu.SMEM((pairs,), jnp.int32),
            pltpu.VMEM((modes, width), jnp.bfloat16),
            pltpu.VMEM((pairs * blocks, width, width), jnp.bfloat16),
            pltpu.VMEM((blocks, modes, width), jnp.bfloat16),
            pltpu.VMEM((pairs // 2, blocks, modes, width), jnp.bfloat16),
            pltpu.SMEM((pairs,), jnp.int32),
            pltpu.SMEM((slots,), jnp.int32),
            pltpu.SMEM((slots,), jnp.int32),
            pltpu.SMEM((slots + 1,), jnp.int32),
            pltpu.SemaphoreType.DMA((pairs * blocks + 3,)),
            pltpu.SemaphoreType.DMA((slots,)),
        ],
        compiler_params=pltpu.CompilerParams(vmem_limit_bytes=12 * 2**20),
        cost_estimate=pl.CostEstimate(flops=2 * pairs * blocks * modes * width * width,
                                      bytes_accessed=25 * 10**6, transcendentals=0),
    )(*map(in_hbm, (partner, counts, own, coupling)))
    return out[0], out[1:6], out[6], out[7]


def nt(a, b):
    return lax.dot_general(a, b, (((1,), (1,)), ((), ())), preferred_element_type=jnp.float32)


def pair_kernel(partner_ref, left_ref, *rest):
    (kept, near, far, low, high, ring_mine, ring_other, across), out_hbm = rest[:8], rest[8]
    panels, outs, panel_sem, out_sem = rest[9:]
    pairs, count = panels.shape[0], outs.shape[0]

    def save(i):
        return pltpu.make_async_copy(outs.at[i], out_hbm.at[i // 2, i % 2], out_sem.at[i])

    @pl.loop(0, pairs)
    def _(q):
        code = partner_ref[q]
        d1, d2 = offsets(code)
        dz, core, me = ring_offset(code)
        step = jnp.where((dz == 1) | (dz == 3), jnp.where((dz == 3) == (core == 0), 1, 2), jnp.where(dz == 2, 3, 0))
        along = code < SPAN_X
        for ref, index, chosen in (
            (kept, d1, along & (d2 == 0)),
            (near, d1, along & (d2 == 1)),
            (far, d1, along & (d2 == 3)),
            (low, d1, along & (d2 == 2) & (d1 < 2)),
            (high, d1 - 2, along & (d2 == 2) & (d1 >= 2)),
            (ring_mine, step, (code >= SPAN_X) & (dz != 2) & (core == me)),
            (ring_other, step, (code >= SPAN_X) & (dz != 2) & (core != me)),
            (across, jnp.where(core == me, 0, 1), (code >= SPAN_X) & (dz == 2)),
        ):
            @pl.when(chosen)
            def _():
                pltpu.make_async_copy(ref.at[index], panels.at[q], panel_sem.at[q]).start()

    @pl.loop(0, count)
    def _(i):
        p = i // 2

        @pl.when(i % 2 == 0)
        def _():
            pltpu.make_async_copy(kept.at[0], panels.at[p], panel_sem.at[p]).wait()

        outs[i] = nt(left_ref[p, i % 2], panels[p]).astype(jnp.bfloat16)
        save(i).start()

    @pl.loop(0, count)
    def _(i):
        save(i).wait()


def pair_products(left, sources, partner):
    pairs, blocks, modes, width = left.shape
    hbm, smem = pl.BlockSpec(memory_space=pltpu.HBM), pl.BlockSpec(memory_space=pltpu.SMEM)
    return pl.pallas_call(
        pair_kernel,
        in_specs=[smem, pl.BlockSpec(memory_space=pltpu.VMEM)] + [pl.BlockSpec(memory_space=pl.ANY)] * 8,
        out_specs=hbm,
        out_shape=jax.ShapeDtypeStruct((pairs, blocks, modes, modes), jnp.bfloat16),
        scratch_shapes=[
            pltpu.VMEM((pairs, modes, width), jnp.bfloat16),
            pltpu.VMEM((pairs * blocks, modes, modes), jnp.bfloat16),
            pltpu.SemaphoreType.DMA((pairs,)),
            pltpu.SemaphoreType.DMA((pairs * blocks,)),
        ],
        compiler_params=pltpu.CompilerParams(vmem_limit_bytes=14 * 2**20),
        cost_estimate=pl.CostEstimate(flops=2 * pairs * blocks * modes * width * modes,
                                      bytes_accessed=15 * 10**6, transcendentals=0),
    )(partner, left, *sources)


def partner_kernel(own_ref, sum_ref, *rest):
    last, out_ref = rest[:-1], rest[-1]

    @pl.loop(0, out_ref.shape[0])
    def _(t):
        total = sum_ref[t]
        for ref in last:
            total = total + ref[t].astype(jnp.float32)
        out_ref[t] = nt(own_ref[...], total.astype(jnp.bfloat16))


def partner_products(own, start, last):
    modes, _ = own.shape
    blocks = start.shape[0]
    return pl.pallas_call(
        partner_kernel,
        out_shape=jax.ShapeDtypeStruct((blocks, modes, modes), jnp.float32),
        compiler_params=pltpu.CompilerParams(vmem_limit_bytes=16 * 2**20),
    )(own, start, *last)


def permuted(value, move):
    pairs = []
    for n in range(SPAN_X * SPAN_Y):
        here = (n // SPAN_Y // SIDE, n // SPAN_Y % SIDE, n % SPAN_Y // 2, n % 2)
        x, y, z, c = move(*here)
        pairs.append((n, ((x % SIDE) * SIDE + y % SIDE) * SPAN_Y + (z % SIDE) * 2 + c))
    return lax.ppermute(value, ("sx", "sy"), pairs)


def first(value, by):
    return permuted(value, lambda x, y, z, c: (x + by, y, z, c) if c == 0 else (x, y + by, z, c))


def second(value, by):
    return permuted(value, lambda x, y, z, c: (x, y + by, z, c) if c == 0 else (x + by, y, z, c))


def turn(value, by):
    return permuted(value, lambda x, y, z, c: (x, y, z + (by if c == 0 else -by), c))


def swap(value):
    return permuted(value, lambda x, y, z, c: (x, y, z, 1 - c))


def added(*terms):
    return sum(v.astype(jnp.float32) for v in terms)


def rounded(*terms):
    return added(*terms).astype(jnp.bfloat16)


def after(value, *others):
    return lax.optimization_barrier((value,) + others)[0]


def body(panels, coupling, partner, counts):
    own = jnp.swapaxes(panels[0], 0, 1)
    barrier = lax.optimization_barrier

    moved = [first(own, -1), first(own, 2), first(own, 1)]
    ring1, ring2 = turn(own, 1), turn(own, -1)
    kept = jnp.stack([own] + moved)
    left, (up, down, pass_up, pass_down, here), z_other, z_mine = left_products(own, coupling, partner, counts)
    kept, ring1, ring2, up, down, z_other, own_z = barrier((kept, ring1, ring2, up, down, z_other, own))

    got = [first(up, 1), first(down, -1)]
    near, far = second(kept, -1), second(kept, 1)
    ring_mine = jnp.stack([own, ring1, ring2])
    pair_sum = swap(z_other)
    w = [rounded(z_mine[k], pair_sum[k]) for k in range(SIDE)]
    ring_other = swap(after(ring_mine, w))
    opposite, back = turn(after(w[3], ring_other), 1), turn(w[2], -1)
    got, near, far, ring_mine, ring_other, w, opposite, back = barrier(
        (got, near, far, ring_mine, ring_other, w, opposite, back)
    )
    got_up, got_down = got

    b_up, b_down = rounded(pass_up, got_up[:2]), rounded(pass_down, got_down[:2])
    across = jnp.stack([ring_mine[2], ring_other[1]])
    z_pass = rounded(w[1], opposite)
    b_up, b_down, near, far, across, z_pass = barrier((b_up, b_down, near, far, across, z_pass))
    low, high = second(near[:2], -1), second(far[2:], 1)
    across = turn(across, -1)
    last = [first(b_up, 1), first(b_down, -1)]
    last, low, high, across, z_pass = barrier((last, low, high, across, z_pass))
    last_up, last_down = last

    v = [
        rounded(here[0], got_down[2], last_up[0]),
        rounded(here[1], got_down[3], last_up[1]),
        rounded(here[2], got_up[2], last_down[0]),
        rounded(here[3], got_up[3], last_down[1]),
    ]
    v, z_pass = barrier((v, z_pass))
    z_last = turn(z_pass, 1)
    ends = [second(v[1], 1), second(v[3], -1), second(v[2], 2)]

    sources = [kept, near, far, low, high, ring_mine, ring_other, across]
    pair_blocks = pair_products(left, sources, after(partner, *v))
    pair_blocks, ends, z_last = barrier((pair_blocks, ends, z_last))
    partner_blocks = partner_products(own, added(v[0], w[0], back, z_last), ends)
    return (pair_blocks, partner_blocks[None])


def solution(mesh):
    placed = (
        P(("sx", "sy"), None, None),
        P(("sx", "sy"), None, None, None),
        P(("sx", "sy")),
        P(("sx", "sy")),
    )
    return jax.shard_map(
        body,
        mesh=mesh,
        in_specs=placed,
        out_specs=(P(("sx", "sy"), None, None, None), P(("sx", "sy"), None, None, None)),
        check_vma=False,
    )
```

```python
import jax
import jax.numpy as jnp
from jax import lax
from jax.experimental import pallas as pl
from jax.experimental.pallas import tpu as pltpu
from jax.sharding import PartitionSpec as P

SIDE = 4
SPAN_X, SPAN_Y = SIDE * SIDE, 2 * SIDE
PARTS = ((0, 4), (4, 4), (8, 2), (10, 2), (12, 4))
CHUNK = 80


def slot_of(d1, d2):
    low = d2 < 2
    return jnp.where(
        d1 == 0, 12 + d2,
        jnp.where(d1 == 1, jnp.where(low, 8 + d2, d2),
                  jnp.where(d1 == 2, jnp.where(low, d2, 2 + d2), jnp.where(low, 6 + d2, 8 + d2))))


def offsets(code):
    me = lax.axis_index("sx")
    dx = (code // SIDE - me // SIDE + SIDE) % SIDE
    dy = (code % SIDE - me % SIDE + SIDE) % SIDE
    swapped = lax.axis_index("sy") % 2 == 1
    return jnp.where(swapped, dy, dx), jnp.where(swapped, dx, dy)


def ring_offset(code):
    me = lax.axis_index("sy")
    other = code - SPAN_X
    return (other // 2 - me // 2 + SIDE) % SIDE, other % 2, me % 2


def left_kernel(partner_hbm, counts_hbm, own_hbm, coupling_hbm, left_ref, *rest):
    outs = rest[:7]
    partner_ref, counts_ref, own_ref, blocks, zero, sums = rest[7:13]
    keys, number, seen, at_sum, in_sem, out_sem = rest[13:]
    pairs, width = blocks.shape[0], blocks.shape[1]
    count, modes = 2 * pairs, own_ref.shape[0]
    slots = SPAN_X + SPAN_Y

    def load(i):
        return pltpu.make_async_copy(coupling_hbm.at[i // 2, i % 2],
                                     blocks.at[i // 2, :, pl.ds(pl.multiple_of(i % 2 * width, width), width)], in_sem.at[i])

    load_partner = pltpu.make_async_copy(partner_hbm, partner_ref, in_sem.at[count + 1])
    load_partner.start()
    load_counts = pltpu.make_async_copy(counts_hbm, counts_ref, in_sem.at[count + 2])
    load_counts.start()
    load_own = pltpu.make_async_copy(own_hbm, own_ref, in_sem.at[count])
    load_own.start()

    @pl.loop(0, count)
    def _(i):
        load(i).start()

    @pl.loop(0, slots)
    def _(k):
        number[k] = 0
        seen[k] = 0

    at_sum[slots] = 0
    load_partner.wait()
    load_counts.wait()

    @pl.loop(0, pairs)
    def _(p):
        code = partner_ref[p]
        d1, d2 = offsets(code)
        dz, core, me = ring_offset(code)
        step = jnp.where((dz == 1) | (dz == 3), jnp.where((dz == 1) == (core == 0), 1, 2), jnp.where(dz == 2, 3, 0))
        key = jnp.where(code < SPAN_X, slot_of(d1, d2), SPAN_X + step + jnp.where(core == me, SIDE, 0))
        keys[p] = key
        number[key] = number[key] + 1

    @pl.loop(0, 2 * (modes // CHUNK))
    def _(r):
        rows = pl.ds(pl.multiple_of(r // 2 * CHUNK, CHUNK), CHUNK)
        zero[r % 2, rows] = jnp.zeros((CHUNK, width), zero.dtype)

    def send(source, key):
        for out, (at, size) in zip(outs, PARTS + ((SPAN_X, SIDE), (SPAN_X + SIDE, SIDE)), strict=True):
            @pl.when((key >= at) & (key < at + size))
            def _():
                pltpu.make_async_copy(source, out.at[key - at], out_sem.at[key]).start()

    @pl.loop(0, slots)
    def _(k):
        @pl.when(number[k] == 0)
        def _():
            send(zero, k)

    load_own.wait()

    @pl.loop(0, pairs)
    def _(p):
        load(2 * p).wait()
        load(2 * p + 1).wait()
        keep = lax.broadcasted_iota(jnp.int32, (1, width), 1) < counts_ref[p]
        own = jnp.where(keep, own_ref[...], jnp.zeros((modes, width), own_ref.dtype))
        product = jnp.dot(own, blocks[p], preferred_element_type=jnp.float32)
        for t in range(2):
            left_ref[p, t] = jnp.where(keep, product[:, t * width:(t + 1) * width], 0.0).astype(jnp.bfloat16)
        key = keys[p]
        single = number[key] == 1

        @pl.when(single)
        def _():
            send(left_ref.at[p], key)

        @pl.when(jnp.logical_not(single))
        def _():
            fresh = seen[key] == 0

            @pl.when(fresh)
            def _():
                at_sum[key] = at_sum[slots]
                at_sum[slots] = at_sum[slots] + 1

            seen[key] = seen[key] + 1
            place = at_sum[key]

            @pl.loop(0, 2 * (modes // CHUNK))
            def _(r):
                t, rows = r % 2, pl.ds(pl.multiple_of(r // 2 * CHUNK, CHUNK), CHUNK)
                before = jnp.where(fresh, 0.0, sums[place, t, rows].astype(jnp.float32))
                sums[place, t, rows] = (before + left_ref[p, t, rows].astype(jnp.float32)).astype(jnp.bfloat16)

            @pl.when(seen[key] == number[key])
            def _():
                send(sums.at[place], key)

    @pl.loop(0, slots)
    def _(k):
        pltpu.make_async_copy(zero, outs[0].at[0], out_sem.at[k]).wait()


def in_hbm(value):
    return pltpu.with_memory_space_constraint(value, pltpu.HBM)


def left_products(own, coupling, partner, counts):
    pairs, blocks, width, _ = coupling.shape
    modes = own.shape[0]
    slots = SPAN_X + SPAN_Y
    sizes = [pairs] + [size for _, size in PARTS] + [SIDE] * 2
    hbm, vmem = pltpu.HBM, pltpu.VMEM
    spaces = [vmem, hbm, hbm, vmem, vmem, hbm, hbm, hbm]
    out = pl.pallas_call(
        left_kernel,
        in_specs=[pl.BlockSpec(memory_space=pltpu.HBM)] * 4,
        out_specs=[pl.BlockSpec(memory_space=space) for space in spaces],
        out_shape=[space((n, blocks, modes, width), jnp.bfloat16) for n, space in zip(sizes, spaces, strict=True)],
        scratch_shapes=[
            pltpu.SMEM((pairs,), jnp.int32),
            pltpu.SMEM((pairs,), jnp.int32),
            pltpu.VMEM((modes, width), jnp.bfloat16),
            pltpu.VMEM((pairs, width, blocks * width), jnp.bfloat16),
            pltpu.VMEM((blocks, modes, width), jnp.bfloat16),
            pltpu.VMEM((pairs // 2, blocks, modes, width), jnp.bfloat16),
            pltpu.SMEM((pairs,), jnp.int32),
            pltpu.SMEM((slots,), jnp.int32),
            pltpu.SMEM((slots,), jnp.int32),
            pltpu.SMEM((slots + 1,), jnp.int32),
            pltpu.SemaphoreType.DMA((pairs * blocks + 3,)),
            pltpu.SemaphoreType.DMA((slots,)),
        ],
        compiler_params=pltpu.CompilerParams(vmem_limit_bytes=12 * 2**20),
        cost_estimate=pl.CostEstimate(flops=2 * pairs * blocks * modes * width * width,
                                      bytes_accessed=25 * 10**6, transcendentals=0),
    )(*map(in_hbm, (partner, counts, own, coupling)))
    return out[0], out[1:6], out[6], out[7]


def nt(a, b):
    return lax.dot_general(a, b, (((1,), (1,)), ((), ())), preferred_element_type=jnp.float32)


def pair_kernel(partner_ref, left_ref, *rest):
    (kept, near, far, low, high, ring_mine, ring_other, across), out_hbm = rest[:8], rest[8]
    panels, outs, panel_sem, out_sem = rest[9:]
    pairs, count = panels.shape[0], outs.shape[0]

    def save(i):
        return pltpu.make_async_copy(outs.at[i], out_hbm.at[i // 2, i % 2], out_sem.at[i])

    @pl.loop(0, pairs)
    def _(q):
        code = partner_ref[q]
        d1, d2 = offsets(code)
        dz, core, me = ring_offset(code)
        step = jnp.where((dz == 1) | (dz == 3), jnp.where((dz == 3) == (core == 0), 1, 2), jnp.where(dz == 2, 3, 0))
        along = code < SPAN_X
        for ref, index, chosen in (
            (kept, d1, along & (d2 == 0)),
            (near, d1, along & (d2 == 1)),
            (far, d1, along & (d2 == 3)),
            (low, d1, along & (d2 == 2) & (d1 < 2)),
            (high, d1 - 2, along & (d2 == 2) & (d1 >= 2)),
            (ring_mine, step, (code >= SPAN_X) & (dz != 2) & (core == me)),
            (ring_other, step, (code >= SPAN_X) & (dz != 2) & (core != me)),
            (across, jnp.where(core == me, 0, 1), (code >= SPAN_X) & (dz == 2)),
        ):
            @pl.when(chosen)
            def _():
                pltpu.make_async_copy(ref.at[index], panels.at[q], panel_sem.at[q]).start()

    @pl.loop(0, count)
    def _(i):
        p = i // 2

        @pl.when(i % 2 == 0)
        def _():
            pltpu.make_async_copy(kept.at[0], panels.at[p], panel_sem.at[p]).wait()

        outs[i] = nt(left_ref[p, i % 2], panels[p]).astype(jnp.bfloat16)
        save(i).start()

    @pl.loop(0, count)
    def _(i):
        save(i).wait()


def pair_products(left, sources, partner):
    pairs, blocks, modes, width = left.shape
    hbm, smem = pl.BlockSpec(memory_space=pltpu.HBM), pl.BlockSpec(memory_space=pltpu.SMEM)
    return pl.pallas_call(
        pair_kernel,
        in_specs=[smem, pl.BlockSpec(memory_space=pltpu.VMEM)] + [pl.BlockSpec(memory_space=pl.ANY)] * 8,
        out_specs=hbm,
        out_shape=jax.ShapeDtypeStruct((pairs, blocks, modes, modes), jnp.bfloat16),
        scratch_shapes=[
            pltpu.VMEM((pairs, modes, width), jnp.bfloat16),
            pltpu.VMEM((pairs * blocks, modes, modes), jnp.bfloat16),
            pltpu.SemaphoreType.DMA((pairs,)),
            pltpu.SemaphoreType.DMA((pairs * blocks,)),
        ],
        compiler_params=pltpu.CompilerParams(vmem_limit_bytes=14 * 2**20),
        cost_estimate=pl.CostEstimate(flops=2 * pairs * blocks * modes * width * modes,
                                      bytes_accessed=15 * 10**6, transcendentals=0),
    )(partner, left, *sources)


def partner_kernel(own_ref, sum_ref, *rest):
    last, out_ref = rest[:-1], rest[-1]

    @pl.loop(0, out_ref.shape[0])
    def _(t):
        total = sum_ref[t]
        for ref in last:
            total = total + ref[t].astype(jnp.float32)
        out_ref[t] = nt(own_ref[...], total.astype(jnp.bfloat16))


def partner_products(own, start, last):
    modes, _ = own.shape
    blocks = start.shape[0]
    return pl.pallas_call(
        partner_kernel,
        out_shape=jax.ShapeDtypeStruct((blocks, modes, modes), jnp.float32),
        compiler_params=pltpu.CompilerParams(vmem_limit_bytes=16 * 2**20),
    )(own, start, *last)


def permuted(value, move):
    pairs = []
    for n in range(SPAN_X * SPAN_Y):
        here = (n // SPAN_Y // SIDE, n // SPAN_Y % SIDE, n % SPAN_Y // 2, n % 2)
        x, y, z, c = move(*here)
        pairs.append((n, ((x % SIDE) * SIDE + y % SIDE) * SPAN_Y + (z % SIDE) * 2 + c))
    return lax.ppermute(value, ("sx", "sy"), pairs)


def first(value, by):
    return permuted(value, lambda x, y, z, c: (x + by, y, z, c) if c == 0 else (x, y + by, z, c))


def second(value, by):
    return permuted(value, lambda x, y, z, c: (x, y + by, z, c) if c == 0 else (x + by, y, z, c))


def turn(value, by):
    return permuted(value, lambda x, y, z, c: (x, y, z + (by if c == 0 else -by), c))


def swap(value):
    return permuted(value, lambda x, y, z, c: (x, y, z, 1 - c))


def added(*terms):
    return sum(v.astype(jnp.float32) for v in terms)


def rounded(*terms):
    return added(*terms).astype(jnp.bfloat16)


def after(value, *others):
    return lax.optimization_barrier((value,) + others)[0]


def body(panels, coupling, partner, counts):
    own = jnp.swapaxes(panels[0], 0, 1)
    barrier = lax.optimization_barrier

    moved = [first(own, -1), first(own, 2), first(own, 1)]
    ring1, ring2 = turn(own, 1), turn(own, -1)
    kept = jnp.stack([own] + moved)
    left, (up, down, pass_up, pass_down, here), z_other, z_mine = left_products(own, coupling, partner, counts)
    kept, ring1, ring2, up, down, z_other, own_z = barrier((kept, ring1, ring2, up, down, z_other, own))

    got = [first(up, 1), first(down, -1)]
    near, far = second(kept, -1), second(kept, 1)
    ring_mine = jnp.stack([own, ring1, ring2])
    pair_sum = swap(z_other)
    w = [rounded(z_mine[k], pair_sum[k]) for k in range(SIDE)]
    ring_other = swap(after(ring_mine, w))
    opposite, back = turn(after(w[3], ring_other), 1), turn(w[2], -1)
    got, near, far, ring_mine, ring_other, w, opposite, back = barrier(
        (got, near, far, ring_mine, ring_other, w, opposite, back)
    )
    got_up, got_down = got

    b_up, b_down = rounded(pass_up, got_up[:2]), rounded(pass_down, got_down[:2])
    across = jnp.stack([ring_mine[2], ring_other[1]])
    z_pass = rounded(w[1], opposite)
    b_up, b_down, near, far, across, z_pass = barrier((b_up, b_down, near, far, across, z_pass))
    low, high = second(near[:2], -1), second(far[2:], 1)
    across = turn(across, -1)
    last = [first(b_up, 1), first(b_down, -1)]
    last, low, high, across, z_pass = barrier((last, low, high, across, z_pass))
    last_up, last_down = last

    v = [
        rounded(here[0], got_down[2], last_up[0]),
        rounded(here[1], got_down[3], last_up[1]),
        rounded(here[2], got_up[2], last_down[0]),
        rounded(here[3], got_up[3], last_down[1]),
    ]
    v, z_pass = barrier((v, z_pass))
    z_last = turn(z_pass, 1)
    ends = [second(v[1], 1), second(v[3], -1), second(v[2], 2)]

    sources = [kept, near, far, low, high, ring_mine, ring_other, across]
    pair_blocks = pair_products(left, sources, after(partner, *v))
    pair_blocks, ends, z_last = barrier((pair_blocks, ends, z_last))
    partner_blocks = partner_products(own, added(v[0], w[0], back, z_last), ends)
    return (pair_blocks, partner_blocks[None])


def solution(mesh):
    placed = (
        P(("sx", "sy"), None, None),
        P(("sx", "sy"), None, None, None),
        P(("sx", "sy")),
        P(("sx", "sy")),
    )
    return jax.shard_map(
        body,
        mesh=mesh,
        in_specs=placed,
        out_specs=(P(("sx", "sy"), None, None, None), P(("sx", "sy"), None, None, None)),
        check_vma=False,
    )
```

```python
import jax
import jax.numpy as jnp
from jax import lax
from jax.experimental import pallas as pl
from jax.experimental.pallas import tpu as pltpu
from jax.sharding import PartitionSpec as P

SIDE = 4
SPAN_X, SPAN_Y = SIDE * SIDE, 2 * SIDE
PARTS = ((0, 4), (4, 4), (8, 2), (10, 2), (12, 4))
CHUNK = 80


def slot_of(d1, d2):
    low = d2 < 2
    return jnp.where(
        d1 == 0, 12 + d2,
        jnp.where(d1 == 1, jnp.where(low, 8 + d2, d2),
                  jnp.where(d1 == 2, jnp.where(low, d2, 2 + d2), jnp.where(low, 6 + d2, 8 + d2))))


def offsets(code):
    me = lax.axis_index("sx")
    dx = (code // SIDE - me // SIDE + SIDE) % SIDE
    dy = (code % SIDE - me % SIDE + SIDE) % SIDE
    swapped = lax.axis_index("sy") % 2 == 1
    return jnp.where(swapped, dy, dx), jnp.where(swapped, dx, dy)


def ring_offset(code):
    me = lax.axis_index("sy")
    other = code - SPAN_X
    return (other // 2 - me // 2 + SIDE) % SIDE, other % 2, me % 2


def left_kernel(partner_hbm, counts_hbm, own_hbm, coupling_hbm, left_ref, *rest):
    outs = rest[:7]
    partner_ref, counts_ref, own_ref, blocks, zero, sums = rest[7:13]
    keys, number, seen, at_sum, in_sem, out_sem = rest[13:]
    pairs, width = blocks.shape[0], blocks.shape[1]
    count, modes = 2 * pairs, own_ref.shape[0]
    slots = SPAN_X + SPAN_Y

    def load(i):
        return pltpu.make_async_copy(coupling_hbm.at[i // 2, i % 2],
                                     blocks.at[i // 2, :, pl.ds(pl.multiple_of(i % 2 * width, width), width)], in_sem.at[i])

    load_partner = pltpu.make_async_copy(partner_hbm, partner_ref, in_sem.at[count + 1])
    load_partner.start()
    load_counts = pltpu.make_async_copy(counts_hbm, counts_ref, in_sem.at[count + 2])
    load_counts.start()
    load_own = pltpu.make_async_copy(own_hbm, own_ref, in_sem.at[count])
    load_own.start()

    @pl.loop(0, count)
    def _(i):
        load(i).start()

    @pl.loop(0, slots)
    def _(k):
        number[k] = 0
        seen[k] = 0

    at_sum[slots] = 0
    load_partner.wait()
    load_counts.wait()

    @pl.loop(0, pairs)
    def _(p):
        code = partner_ref[p]
        d1, d2 = offsets(code)
        dz, core, me = ring_offset(code)
        step = jnp.where((dz == 1) | (dz == 3), jnp.where((dz == 1) == (core == 0), 1, 2), jnp.where(dz == 2, 3, 0))
        key = jnp.where(code < SPAN_X, slot_of(d1, d2), SPAN_X + step + jnp.where(core == me, SIDE, 0))
        keys[p] = key
        number[key] = number[key] + 1

    @pl.loop(0, 2 * (modes // CHUNK))
    def _(r):
        rows = pl.ds(pl.multiple_of(r // 2 * CHUNK, CHUNK), CHUNK)
        zero[r % 2, rows] = jnp.zeros((CHUNK, width), zero.dtype)

    def send(source, key):
        for out, (at, size) in zip(outs, PARTS + ((SPAN_X, SIDE), (SPAN_X + SIDE, SIDE)), strict=True):
            @pl.when((key >= at) & (key < at + size))
            def _():
                pltpu.make_async_copy(source, out.at[key - at], out_sem.at[key]).start()

    @pl.loop(0, slots)
    def _(k):
        @pl.when(number[k] == 0)
        def _():
            send(zero, k)

    load_own.wait()

    @pl.loop(0, pairs)
    def _(p):
        load(2 * p).wait()
        load(2 * p + 1).wait()
        keep = lax.broadcasted_iota(jnp.int32, (1, width), 1) < counts_ref[p]
        own = jnp.where(keep, own_ref[...], jnp.zeros((modes, width), own_ref.dtype))
        product = jnp.dot(own, blocks[p], preferred_element_type=jnp.float32)
        for t in range(2):
            left_ref[p, t] = jnp.where(keep, product[:, t * width:(t + 1) * width], 0.0).astype(jnp.bfloat16)
        key = keys[p]
        single = number[key] == 1

        @pl.when(single)
        def _():
            send(left_ref.at[p], key)

        @pl.when(jnp.logical_not(single))
        def _():
            fresh = seen[key] == 0

            @pl.when(fresh)
            def _():
                at_sum[key] = at_sum[slots]
                at_sum[slots] = at_sum[slots] + 1

            seen[key] = seen[key] + 1
            place = at_sum[key]

            @pl.loop(0, 2 * (modes // CHUNK))
            def _(r):
                t, rows = r % 2, pl.ds(pl.multiple_of(r // 2 * CHUNK, CHUNK), CHUNK)
                before = jnp.where(fresh, 0.0, sums[place, t, rows].astype(jnp.float32))
                sums[place, t, rows] = (before + left_ref[p, t, rows].astype(jnp.float32)).astype(jnp.bfloat16)

            @pl.when(seen[key] == number[key])
            def _():
                send(sums.at[place], key)

    @pl.loop(0, slots)
    def _(k):
        pltpu.make_async_copy(zero, outs[0].at[0], out_sem.at[k]).wait()


def in_hbm(value):
    return pltpu.with_memory_space_constraint(value, pltpu.HBM)


def left_products(own, coupling, partner, counts):
    pairs, blocks, width, _ = coupling.shape
    modes = own.shape[0]
    slots = SPAN_X + SPAN_Y
    sizes = [pairs] + [size for _, size in PARTS] + [SIDE] * 2
    hbm, vmem = pltpu.HBM, pltpu.VMEM
    spaces = [vmem, hbm, hbm, vmem, vmem, hbm, hbm, hbm]
    out = pl.pallas_call(
        left_kernel,
        in_specs=[pl.BlockSpec(memory_space=pltpu.HBM)] * 4,
        out_specs=[pl.BlockSpec(memory_space=space) for space in spaces],
        out_shape=[space((n, blocks, modes, width), jnp.bfloat16) for n, space in zip(sizes, spaces, strict=True)],
        scratch_shapes=[
            pltpu.SMEM((pairs,), jnp.int32),
            pltpu.SMEM((pairs,), jnp.int32),
            pltpu.VMEM((modes, width), jnp.bfloat16),
            pltpu.VMEM((pairs, width, blocks * width), jnp.bfloat16),
            pltpu.VMEM((blocks, modes, width), jnp.bfloat16),
            pltpu.VMEM((pairs // 2, blocks, modes, width), jnp.bfloat16),
            pltpu.SMEM((pairs,), jnp.int32),
            pltpu.SMEM((slots,), jnp.int32),
            pltpu.SMEM((slots,), jnp.int32),
            pltpu.SMEM((slots + 1,), jnp.int32),
            pltpu.SemaphoreType.DMA((pairs * blocks + 3,)),
            pltpu.SemaphoreType.DMA((slots,)),
        ],
        compiler_params=pltpu.CompilerParams(vmem_limit_bytes=12 * 2**20),
        cost_estimate=pl.CostEstimate(flops=2 * pairs * blocks * modes * width * width,
                                      bytes_accessed=25 * 10**6, transcendentals=0),
    )(*map(in_hbm, (partner, counts, own, coupling)))
    return out[0], out[1:6], out[6], out[7]


def nt(a, b):
    return lax.dot_general(a, b, (((1,), (1,)), ((), ())), preferred_element_type=jnp.float32)


def pair_kernel(partner_ref, left_ref, *rest):
    (kept, near, far, low, high, ring_mine, ring_other, across), out_hbm = rest[:8], rest[8]
    panels, outs, panel_sem, out_sem = rest[9:]
    pairs, count = panels.shape[0], outs.shape[0]

    def save(i):
        return pltpu.make_async_copy(outs.at[i], out_hbm.at[i // 2, i % 2], out_sem.at[i])

    @pl.loop(0, pairs)
    def _(q):
        code = partner_ref[q]
        d1, d2 = offsets(code)
        dz, core, me = ring_offset(code)
        step = jnp.where((dz == 1) | (dz == 3), jnp.where((dz == 3) == (core == 0), 1, 2), jnp.where(dz == 2, 3, 0))
        along = code < SPAN_X
        for ref, index, chosen in (
            (kept, d1, along & (d2 == 0)),
            (near, d1, along & (d2 == 1)),
            (far, d1, along & (d2 == 3)),
            (low, d1, along & (d2 == 2) & (d1 < 2)),
            (high, d1 - 2, along & (d2 == 2) & (d1 >= 2)),
            (ring_mine, step, (code >= SPAN_X) & (dz != 2) & (core == me)),
            (ring_other, step, (code >= SPAN_X) & (dz != 2) & (core != me)),
            (across, jnp.where(core == me, 0, 1), (code >= SPAN_X) & (dz == 2)),
        ):
            @pl.when(chosen)
            def _():
                pltpu.make_async_copy(ref.at[index], panels.at[q], panel_sem.at[q]).start()

    @pl.loop(0, count)
    def _(i):
        p = i // 2

        @pl.when(i % 2 == 0)
        def _():
            pltpu.make_async_copy(kept.at[0], panels.at[p], panel_sem.at[p]).wait()

        outs[i] = nt(left_ref[p, i % 2], panels[p]).astype(jnp.bfloat16)
        save(i).start()

    @pl.loop(0, count)
    def _(i):
        save(i).wait()


def pair_products(left, sources, partner):
    pairs, blocks, modes, width = left.shape
    hbm, smem = pl.BlockSpec(memory_space=pltpu.HBM), pl.BlockSpec(memory_space=pltpu.SMEM)
    return pl.pallas_call(
        pair_kernel,
        in_specs=[smem, pl.BlockSpec(memory_space=pltpu.VMEM)] + [pl.BlockSpec(memory_space=pl.ANY)] * 8,
        out_specs=hbm,
        out_shape=jax.ShapeDtypeStruct((pairs, blocks, modes, modes), jnp.bfloat16),
        scratch_shapes=[
            pltpu.VMEM((pairs, modes, width), jnp.bfloat16),
            pltpu.VMEM((pairs * blocks, modes, modes), jnp.bfloat16),
            pltpu.SemaphoreType.DMA((pairs,)),
            pltpu.SemaphoreType.DMA((pairs * blocks,)),
        ],
        compiler_params=pltpu.CompilerParams(vmem_limit_bytes=14 * 2**20),
        cost_estimate=pl.CostEstimate(flops=2 * pairs * blocks * modes * width * modes,
                                      bytes_accessed=15 * 10**6, transcendentals=0),
    )(partner, left, *sources)


def partner_kernel(own_ref, sum_ref, *rest):
    last, out_ref = rest[:-1], rest[-1]

    @pl.loop(0, out_ref.shape[0])
    def _(t):
        total = sum_ref[t]
        for ref in last:
            total = total + ref[t].astype(jnp.float32)
        out_ref[t] = nt(own_ref[...], total.astype(jnp.bfloat16))


def partner_products(own, start, last):
    modes, _ = own.shape
    blocks = start.shape[0]
    return pl.pallas_call(
        partner_kernel,
        out_shape=jax.ShapeDtypeStruct((blocks, modes, modes), jnp.float32),
        compiler_params=pltpu.CompilerParams(vmem_limit_bytes=16 * 2**20),
    )(own, start, *last)


def permuted(value, move):
    pairs = []
    for n in range(SPAN_X * SPAN_Y):
        here = (n // SPAN_Y // SIDE, n // SPAN_Y % SIDE, n % SPAN_Y // 2, n % 2)
        x, y, z, c = move(*here)
        pairs.append((n, ((x % SIDE) * SIDE + y % SIDE) * SPAN_Y + (z % SIDE) * 2 + c))
    return lax.ppermute(value, ("sx", "sy"), pairs)


def first(value, by):
    return permuted(value, lambda x, y, z, c: (x + by, y, z, c) if c == 0 else (x, y + by, z, c))


def second(value, by):
    return permuted(value, lambda x, y, z, c: (x, y + by, z, c) if c == 0 else (x + by, y, z, c))


def turn(value, by):
    return permuted(value, lambda x, y, z, c: (x, y, z + (by if c == 0 else -by), c))


def swap(value):
    return permuted(value, lambda x, y, z, c: (x, y, z, 1 - c))


def added(*terms):
    return sum(v.astype(jnp.float32) for v in terms)


def rounded(*terms):
    return added(*terms).astype(jnp.bfloat16)


def after(value, *others):
    return lax.optimization_barrier((value,) + others)[0]


def body(panels, coupling, partner, counts):
    own = jnp.swapaxes(panels[0], 0, 1)
    barrier = lax.optimization_barrier

    moved = [first(own, -1), first(own, 2), first(own, 1)]
    ring1, ring2 = turn(own, 1), turn(own, -1)
    kept = jnp.stack([own] + moved)
    kept, ring1, ring2 = barrier((kept, ring1, ring2))
    near, far = second(kept, -1), second(kept, 1)
    left, (up, down, pass_up, pass_down, here), z_other, z_mine = left_products(
        own, coupling, partner, after(counts, kept)
    )

    got_up, got_down = first(up, 1), first(down, -1)
    ring_mine = jnp.stack([own, ring1, ring2])
    ring_other = swap(after(ring_mine, up))
    across = turn(jnp.stack([ring2, ring_other[1]]), -1)
    pair_sum = swap(after(z_other, near, far))
    b_up, b_down = rounded(pass_up, got_up[:2]), rounded(pass_down, got_down[:2])
    b_up, b_down, near, far, ring_mine, ring_other, across, pair_sum = barrier(
        (b_up, b_down, near, far, ring_mine, ring_other, across, pair_sum)
    )

    w = [rounded(z_mine[k], pair_sum[k]) for k in range(SIDE)]
    low, high = second(near[:2], -1), second(far[2:], 1)
    opposite = turn(w[3], 1)
    last = [first(b_up, 1), first(b_down, -1)]
    last, low, high, opposite = barrier((last, low, high, opposite))
    last_up, last_down = last

    v = [
        rounded(here[0], got_down[2], last_up[0]),
        rounded(here[1], got_down[3], last_up[1]),
        rounded(here[2], got_up[2], last_down[0]),
        rounded(here[3], got_up[3], last_down[1]),
    ]
    z_pass = rounded(w[1], opposite)
    v, z_pass, z_back = barrier((v, z_pass, w[2]))
    ends = [second(v[1], 1), second(v[3], -1), second(v[2], 2)]
    z_last, back = turn(z_pass, 1), turn(z_back, -1)

    sources = [kept, near, far, low, high, ring_mine, ring_other, across]
    pair_blocks = pair_products(left, sources, after(partner, *v))
    pair_blocks, ends = barrier((pair_blocks, ends))
    partner_blocks = partner_products(own, added(v[0], w[0], back, z_last), ends)
    return (pair_blocks, partner_blocks[None])


def solution(mesh):
    placed = (
        P(("sx", "sy"), None, None),
        P(("sx", "sy"), None, None, None),
        P(("sx", "sy")),
        P(("sx", "sy")),
    )
    return jax.shard_map(
        body,
        mesh=mesh,
        in_specs=placed,
        out_specs=(P(("sx", "sy"), None, None, None), P(("sx", "sy"), None, None, None)),
        check_vma=False,
    )
```

```python
import jax
import jax.numpy as jnp
from jax import lax
from jax.experimental import pallas as pl
from jax.experimental.pallas import tpu as pltpu
from jax.sharding import PartitionSpec as P

SIDE = 4
SPAN_X, SPAN_Y = SIDE * SIDE, 2 * SIDE
PARTS = ((0, 2), (2, 2), (4, 2), (6, 2), (8, 2), (10, 2), (12, 4))
RINGS = ((16, 2), (18, 2), (20, 4))
CHUNK = 80


def slot_of(d1, d2):
    low = d2 < 2
    return jnp.where(
        d1 == 0, 12 + d2,
        jnp.where(d1 == 1, jnp.where(low, 8 + d2, d2),
                  jnp.where(d1 == 2, jnp.where(low, d2, 2 + d2), jnp.where(low, 6 + d2, 8 + d2))))


def offsets(code):
    me = lax.axis_index("sx")
    dx = (code // SIDE - me // SIDE + SIDE) % SIDE
    dy = (code % SIDE - me % SIDE + SIDE) % SIDE
    swapped = lax.axis_index("sy") % 2 == 1
    return jnp.where(swapped, dy, dx), jnp.where(swapped, dx, dy)


def ring_offset(code):
    me = lax.axis_index("sy")
    other = code - SPAN_X
    return (other // 2 - me // 2 + SIDE) % SIDE, other % 2, me % 2


def left_kernel(partner_hbm, counts_hbm, own_hbm, coupling_hbm, left_ref, *rest):
    outs = rest[:10]
    partner_ref, counts_ref, own_ref, blocks, zero, sums = rest[10:16]
    keys, number, seen, at_sum, in_sem, out_sem = rest[16:]
    pairs, width = blocks.shape[0], blocks.shape[1]
    count, modes = 2 * pairs, own_ref.shape[0]
    slots = SPAN_X + SPAN_Y

    def load(i):
        return pltpu.make_async_copy(coupling_hbm.at[i // 2, i % 2],
                                     blocks.at[i // 2, :, pl.ds(pl.multiple_of(i % 2 * width, width), width)], in_sem.at[i])

    load_partner = pltpu.make_async_copy(partner_hbm, partner_ref, in_sem.at[count + 1])
    load_partner.start()
    load_counts = pltpu.make_async_copy(counts_hbm, counts_ref, in_sem.at[count + 2])
    load_counts.start()
    load_own = pltpu.make_async_copy(own_hbm, own_ref, in_sem.at[count])
    load_own.start()

    @pl.loop(0, count)
    def _(i):
        load(i).start()

    @pl.loop(0, slots)
    def _(k):
        number[k] = 0
        seen[k] = 0

    at_sum[slots] = 0
    load_partner.wait()
    load_counts.wait()

    @pl.loop(0, pairs)
    def _(p):
        code = partner_ref[p]
        d1, d2 = offsets(code)
        dz, core, me = ring_offset(code)
        step = jnp.where((dz == 1) | (dz == 3), jnp.where((dz == 1) == (core == 0), 1, 2), jnp.where(dz == 2, 3, 0))
        key = jnp.where(code < SPAN_X, slot_of(d1, d2), SPAN_X + step + jnp.where(core == me, SIDE, 0))
        keys[p] = key
        number[key] = number[key] + 1

    @pl.loop(0, 2 * (modes // CHUNK))
    def _(r):
        rows = pl.ds(pl.multiple_of(r // 2 * CHUNK, CHUNK), CHUNK)
        zero[r % 2, rows] = jnp.zeros((CHUNK, width), zero.dtype)

    def send(source, key):
        for out, (at, size) in zip(outs, PARTS + RINGS, strict=True):
            @pl.when((key >= at) & (key < at + size))
            def _():
                pltpu.make_async_copy(source, out.at[key - at], out_sem.at[key]).start()

    @pl.loop(0, slots)
    def _(k):
        @pl.when(number[k] == 0)
        def _():
            send(zero, k)

    load_own.wait()

    @pl.loop(0, pairs)
    def _(p):
        load(2 * p).wait()
        load(2 * p + 1).wait()
        keep = lax.broadcasted_iota(jnp.int32, (1, width), 1) < counts_ref[p]
        own = jnp.where(keep, own_ref[...], jnp.zeros((modes, width), own_ref.dtype))
        product = jnp.dot(own, blocks[p], preferred_element_type=jnp.float32)
        for t in range(2):
            left_ref[p, t] = jnp.where(keep, product[:, t * width:(t + 1) * width], 0.0).astype(jnp.bfloat16)
        key = keys[p]
        single = number[key] == 1

        @pl.when(single)
        def _():
            send(left_ref.at[p], key)

        @pl.when(jnp.logical_not(single))
        def _():
            fresh = seen[key] == 0

            @pl.when(fresh)
            def _():
                at_sum[key] = at_sum[slots]
                at_sum[slots] = at_sum[slots] + 1

            seen[key] = seen[key] + 1
            place = at_sum[key]

            @pl.loop(0, 2 * (modes // CHUNK))
            def _(r):
                t, rows = r % 2, pl.ds(pl.multiple_of(r // 2 * CHUNK, CHUNK), CHUNK)
                before = jnp.where(fresh, 0.0, sums[place, t, rows].astype(jnp.float32))
                sums[place, t, rows] = (before + left_ref[p, t, rows].astype(jnp.float32)).astype(jnp.bfloat16)

            @pl.when(seen[key] == number[key])
            def _():
                send(sums.at[place], key)

    @pl.loop(0, slots)
    def _(k):
        pltpu.make_async_copy(zero, outs[0].at[0], out_sem.at[k]).wait()


def in_hbm(value):
    return pltpu.with_memory_space_constraint(value, pltpu.HBM)


def left_products(own, coupling, partner, counts):
    pairs, blocks, width, _ = coupling.shape
    modes = own.shape[0]
    slots = SPAN_X + SPAN_Y
    sizes = [pairs] + [size for _, size in PARTS + RINGS]
    hbm, vmem = pltpu.HBM, pltpu.VMEM
    spaces = [vmem] + [hbm] * 4 + [vmem] * 2 + [hbm] * 4
    out = pl.pallas_call(
        left_kernel,
        in_specs=[pl.BlockSpec(memory_space=pltpu.HBM)] * 4,
        out_specs=[pl.BlockSpec(memory_space=space) for space in spaces],
        out_shape=[space((n, blocks, modes, width), jnp.bfloat16) for n, space in zip(sizes, spaces, strict=True)],
        scratch_shapes=[
            pltpu.SMEM((pairs,), jnp.int32),
            pltpu.SMEM((pairs,), jnp.int32),
            pltpu.VMEM((modes, width), jnp.bfloat16),
            pltpu.VMEM((pairs, width, blocks * width), jnp.bfloat16),
            pltpu.VMEM((blocks, modes, width), jnp.bfloat16),
            pltpu.VMEM((pairs // 2, blocks, modes, width), jnp.bfloat16),
            pltpu.SMEM((pairs,), jnp.int32),
            pltpu.SMEM((slots,), jnp.int32),
            pltpu.SMEM((slots,), jnp.int32),
            pltpu.SMEM((slots + 1,), jnp.int32),
            pltpu.SemaphoreType.DMA((pairs * blocks + 3,)),
            pltpu.SemaphoreType.DMA((slots,)),
        ],
        compiler_params=pltpu.CompilerParams(vmem_limit_bytes=12 * 2**20),
        cost_estimate=pl.CostEstimate(flops=2 * pairs * blocks * modes * width * width,
                                      bytes_accessed=25 * 10**6, transcendentals=0),
    )(*map(in_hbm, (partner, counts, own, coupling)))
    return out[0], out[1:8], out[8:11]


def nt(a, b):
    return lax.dot_general(a, b, (((1,), (1,)), ((), ())), preferred_element_type=jnp.float32)


def pair_kernel(partner_ref, left_ref, *rest):
    (kept, near, far, low, high, ring_mine, ring_other, across), out_hbm = rest[:8], rest[8]
    panels, outs, panel_sem, out_sem = rest[9:]
    pairs, count = panels.shape[0], outs.shape[0]

    def save(i):
        return pltpu.make_async_copy(outs.at[i], out_hbm.at[i // 2, i % 2], out_sem.at[i])

    @pl.loop(0, pairs)
    def _(q):
        code = partner_ref[q]
        d1, d2 = offsets(code)
        dz, core, me = ring_offset(code)
        step = jnp.where((dz == 1) | (dz == 3), jnp.where((dz == 3) == (core == 0), 1, 2), jnp.where(dz == 2, 3, 0))
        along = code < SPAN_X
        for ref, index, chosen in (
            (kept, d1, along & (d2 == 0)),
            (near, d1, along & (d2 == 1)),
            (far, d1, along & (d2 == 3)),
            (low, d1, along & (d2 == 2) & (d1 < 2)),
            (high, d1 - 2, along & (d2 == 2) & (d1 >= 2)),
            (ring_mine, step, (code >= SPAN_X) & (dz != 2) & (core == me)),
            (ring_other, step, (code >= SPAN_X) & (dz != 2) & (core != me)),
            (across, jnp.where(core == me, 0, 1), (code >= SPAN_X) & (dz == 2)),
        ):
            @pl.when(chosen)
            def _():
                pltpu.make_async_copy(ref.at[index], panels.at[q], panel_sem.at[q]).start()

    @pl.loop(0, count)
    def _(i):
        p = i // 2

        @pl.when(i % 2 == 0)
        def _():
            pltpu.make_async_copy(kept.at[0], panels.at[p], panel_sem.at[p]).wait()

        outs[i] = nt(left_ref[p, i % 2], panels[p]).astype(jnp.bfloat16)
        save(i).start()

    @pl.loop(0, count)
    def _(i):
        save(i).wait()


def pair_products(left, sources, partner):
    pairs, blocks, modes, width = left.shape
    hbm, smem = pl.BlockSpec(memory_space=pltpu.HBM), pl.BlockSpec(memory_space=pltpu.SMEM)
    return pl.pallas_call(
        pair_kernel,
        in_specs=[smem, pl.BlockSpec(memory_space=pltpu.VMEM)] + [pl.BlockSpec(memory_space=pl.ANY)] * 8,
        out_specs=hbm,
        out_shape=jax.ShapeDtypeStruct((pairs, blocks, modes, modes), jnp.bfloat16),
        scratch_shapes=[
            pltpu.VMEM((pairs, modes, width), jnp.bfloat16),
            pltpu.VMEM((pairs * blocks, modes, modes), jnp.bfloat16),
            pltpu.SemaphoreType.DMA((pairs,)),
            pltpu.SemaphoreType.DMA((pairs * blocks,)),
        ],
        compiler_params=pltpu.CompilerParams(vmem_limit_bytes=14 * 2**20),
        cost_estimate=pl.CostEstimate(flops=2 * pairs * blocks * modes * width * modes,
                                      bytes_accessed=15 * 10**6, transcendentals=0),
    )(partner, left, *sources)


def partner_kernel(own_ref, sum_ref, *rest):
    last, out_ref = rest[:-1], rest[-1]

    @pl.loop(0, out_ref.shape[0])
    def _(t):
        total = sum_ref[t]
        for ref in last:
            total = total + ref[t].astype(jnp.float32)
        out_ref[t] = nt(own_ref[...], total.astype(jnp.bfloat16))


def partner_products(own, start, last):
    modes, _ = own.shape
    blocks = start.shape[0]
    return pl.pallas_call(
        partner_kernel,
        out_shape=jax.ShapeDtypeStruct((blocks, modes, modes), jnp.float32),
        compiler_params=pltpu.CompilerParams(vmem_limit_bytes=16 * 2**20),
    )(own, start, *last)


def permuted(value, move):
    pairs = []
    for n in range(SPAN_X * SPAN_Y):
        here = (n // SPAN_Y // SIDE, n // SPAN_Y % SIDE, n % SPAN_Y // 2, n % 2)
        x, y, z, c = move(*here)
        pairs.append((n, ((x % SIDE) * SIDE + y % SIDE) * SPAN_Y + (z % SIDE) * 2 + c))
    return lax.ppermute(value, ("sx", "sy"), pairs)


def first(value, by):
    return permuted(value, lambda x, y, z, c: (x + by, y, z, c) if c == 0 else (x, y + by, z, c))


def second(value, by):
    return permuted(value, lambda x, y, z, c: (x, y + by, z, c) if c == 0 else (x + by, y, z, c))


def turn(value, by):
    return permuted(value, lambda x, y, z, c: (x, y, z + (by if c == 0 else -by), c))


def swap(value):
    return permuted(value, lambda x, y, z, c: (x, y, z, 1 - c))


def added(*terms):
    return sum(v.astype(jnp.float32) for v in terms)


def rounded(*terms):
    return added(*terms).astype(jnp.bfloat16)


def after(value, *others):
    return lax.optimization_barrier((value,) + others)[0]


def body(panels, coupling, partner, counts):
    own = jnp.swapaxes(panels[0], 0, 1)
    barrier = lax.optimization_barrier

    moved = [first(own, -1), first(own, 2), first(own, 1)]
    ring1, ring2 = turn(own, 1), turn(own, -1)
    kept = jnp.stack([own] + moved)
    kept, ring1, ring2 = barrier((kept, ring1, ring2))
    near, far = second(kept, -1), second(kept, 1)
    left, (up, up_end, down, down_end, pass_up, pass_down, here), (z_near, z_far, z_mine) = left_products(
        own, coupling, partner, after(counts, kept)
    )

    got_up, got_down = first(up, 1), first(down, -1)
    up_end, down_end, z_far, near, far = barrier((up_end, down_end, z_far, near, far))
    end_up, end_down = first(up_end, 1), first(down_end, -1)
    last_up, last_down = first(rounded(pass_up, got_up), 1), first(rounded(pass_down, got_down), -1)

    ring_mine = jnp.stack([own, ring1, ring2])
    ring_other = swap(after(ring_mine, up))
    far_sum = swap(z_far)
    across = turn(jnp.stack([ring2, ring_other[1]]), -1)
    near_sum = swap(after(z_near, ring_other))
    w = [rounded(z_mine[k], (near_sum, far_sum)[k // 2][k % 2]) for k in range(SIDE)]

    near, far, w3, end_up, end_down = barrier((near, far, w[3], end_up, end_down))
    low, high = second(near[:2], -1), second(far[2:], 1)
    opposite = turn(w3, 1)
    last_up, last_down, low, high, opposite, across, ring_other, w = barrier(
        (last_up, last_down, low, high, opposite, across, ring_other, w)
    )

    v = [
        rounded(here[0], end_down[0], last_up[0]),
        rounded(here[1], end_down[1], last_up[1]),
        rounded(here[2], end_up[0], last_down[0]),
        rounded(here[3], end_up[1], last_down[1]),
    ]
    z_pass = rounded(w[1], opposite)
    v, z_pass, z_back = barrier((v, z_pass, w[2]))
    ends = [second(v[1], 1), second(v[3], -1), second(v[2], 2)]
    z_last, back = turn(z_pass, 1), turn(z_back, -1)

    sources = [kept, near, far, low, high, ring_mine, ring_other, across]
    pair_blocks = pair_products(left, sources, after(partner, *v))
    pair_blocks, ends = barrier((pair_blocks, ends))
    partner_blocks = partner_products(own, added(v[0], w[0], back, z_last), ends)
    return (pair_blocks, partner_blocks[None])


def solution(mesh):
    placed = (
        P(("sx", "sy"), None, None),
        P(("sx", "sy"), None, None, None),
        P(("sx", "sy")),
        P(("sx", "sy")),
    )
    return jax.shard_map(
        body,
        mesh=mesh,
        in_specs=placed,
        out_specs=(P(("sx", "sy"), None, None, None), P(("sx", "sy"), None, None, None)),
        check_vma=False,
    )
```

```python
import jax
import jax.numpy as jnp
from jax import lax
from jax.experimental import pallas as pl
from jax.experimental.pallas import tpu as pltpu
from jax.sharding import PartitionSpec as P

SIDE = 4
SPAN_X, SPAN_Y = SIDE * SIDE, 2 * SIDE
PARTS = ((0, 2), (2, 2), (4, 2), (6, 2), (8, 2), (10, 2), (12, 4))
RINGS = ((16, 2), (18, 2), (20, 4))
CHUNK = 80


def slot_of(d1, d2):
    low = d2 < 2
    return jnp.where(
        d1 == 0, 12 + d2,
        jnp.where(d1 == 1, jnp.where(low, 8 + d2, d2),
                  jnp.where(d1 == 2, jnp.where(low, d2, 2 + d2), jnp.where(low, 6 + d2, 8 + d2))))


def offsets(code):
    me = lax.axis_index("sx")
    dx = (code // SIDE - me // SIDE + SIDE) % SIDE
    dy = (code % SIDE - me % SIDE + SIDE) % SIDE
    swapped = lax.axis_index("sy") % 2 == 1
    return jnp.where(swapped, dy, dx), jnp.where(swapped, dx, dy)


def ring_offset(code):
    me = lax.axis_index("sy")
    other = code - SPAN_X
    return (other // 2 - me // 2 + SIDE) % SIDE, other % 2, me % 2


def left_kernel(partner_hbm, counts_hbm, own_hbm, coupling_hbm, left_ref, *rest):
    outs = rest[:10]
    partner_ref, counts_ref, own_ref, blocks, zero, sums = rest[10:16]
    keys, number, seen, at_sum, in_sem, out_sem = rest[16:]
    pairs, width = blocks.shape[0], blocks.shape[1]
    count, modes = 2 * pairs, own_ref.shape[0]
    slots = SPAN_X + SPAN_Y

    def load(i):
        return pltpu.make_async_copy(coupling_hbm.at[i // 2, i % 2],
                                     blocks.at[i // 2, :, pl.ds(pl.multiple_of(i % 2 * width, width), width)], in_sem.at[i])

    load_partner = pltpu.make_async_copy(partner_hbm, partner_ref, in_sem.at[count + 1])
    load_partner.start()
    load_counts = pltpu.make_async_copy(counts_hbm, counts_ref, in_sem.at[count + 2])
    load_counts.start()
    load_own = pltpu.make_async_copy(own_hbm, own_ref, in_sem.at[count])
    load_own.start()

    @pl.loop(0, count)
    def _(i):
        load(i).start()

    @pl.loop(0, slots)
    def _(k):
        number[k] = 0
        seen[k] = 0

    at_sum[slots] = 0
    load_partner.wait()
    load_counts.wait()

    @pl.loop(0, pairs)
    def _(p):
        code = partner_ref[p]
        d1, d2 = offsets(code)
        dz, core, me = ring_offset(code)
        step = jnp.where((dz == 1) | (dz == 3), jnp.where((dz == 1) == (core == 0), 1, 2), jnp.where(dz == 2, 3, 0))
        key = jnp.where(code < SPAN_X, slot_of(d1, d2), SPAN_X + step + jnp.where(core == me, SIDE, 0))
        keys[p] = key
        number[key] = number[key] + 1

    @pl.loop(0, 2 * (modes // CHUNK))
    def _(r):
        rows = pl.ds(pl.multiple_of(r // 2 * CHUNK, CHUNK), CHUNK)
        zero[r % 2, rows] = jnp.zeros((CHUNK, width), zero.dtype)

    def send(source, key):
        for out, (at, size) in zip(outs, PARTS + RINGS, strict=True):
            @pl.when((key >= at) & (key < at + size))
            def _():
                pltpu.make_async_copy(source, out.at[key - at], out_sem.at[key]).start()

    @pl.loop(0, slots)
    def _(k):
        @pl.when(number[k] == 0)
        def _():
            send(zero, k)

    load_own.wait()

    @pl.loop(0, pairs)
    def _(p):
        load(2 * p).wait()
        load(2 * p + 1).wait()
        keep = lax.broadcasted_iota(jnp.int32, (1, width), 1) < counts_ref[p]
        own = jnp.where(keep, own_ref[...], jnp.zeros((modes, width), own_ref.dtype))
        product = jnp.dot(own, blocks[p], preferred_element_type=jnp.float32)
        for t in range(2):
            left_ref[p, t] = jnp.where(keep, product[:, t * width:(t + 1) * width], 0.0).astype(jnp.bfloat16)
        key = keys[p]
        single = number[key] == 1

        @pl.when(single)
        def _():
            send(left_ref.at[p], key)

        @pl.when(jnp.logical_not(single))
        def _():
            fresh = seen[key] == 0

            @pl.when(fresh)
            def _():
                at_sum[key] = at_sum[slots]
                at_sum[slots] = at_sum[slots] + 1

            seen[key] = seen[key] + 1
            place = at_sum[key]

            @pl.loop(0, 2 * (modes // CHUNK))
            def _(r):
                t, rows = r % 2, pl.ds(pl.multiple_of(r // 2 * CHUNK, CHUNK), CHUNK)
                before = jnp.where(fresh, 0.0, sums[place, t, rows].astype(jnp.float32))
                sums[place, t, rows] = (before + left_ref[p, t, rows].astype(jnp.float32)).astype(jnp.bfloat16)

            @pl.when(seen[key] == number[key])
            def _():
                send(sums.at[place], key)

    @pl.loop(0, slots)
    def _(k):
        pltpu.make_async_copy(zero, outs[0].at[0], out_sem.at[k]).wait()


def in_hbm(value):
    return pltpu.with_memory_space_constraint(value, pltpu.HBM)


def left_products(own, coupling, partner, counts):
    pairs, blocks, width, _ = coupling.shape
    modes = own.shape[0]
    slots = SPAN_X + SPAN_Y
    sizes = [pairs] + [size for _, size in PARTS + RINGS]
    hbm, vmem = pltpu.HBM, pltpu.VMEM
    spaces = [vmem] + [hbm] * 4 + [vmem] * 2 + [hbm] * 4
    out = pl.pallas_call(
        left_kernel,
        in_specs=[pl.BlockSpec(memory_space=pltpu.HBM)] * 4,
        out_specs=[pl.BlockSpec(memory_space=space) for space in spaces],
        out_shape=[space((n, blocks, modes, width), jnp.bfloat16) for n, space in zip(sizes, spaces, strict=True)],
        scratch_shapes=[
            pltpu.SMEM((pairs,), jnp.int32),
            pltpu.SMEM((pairs,), jnp.int32),
            pltpu.VMEM((modes, width), jnp.bfloat16),
            pltpu.VMEM((pairs, width, blocks * width), jnp.bfloat16),
            pltpu.VMEM((blocks, modes, width), jnp.bfloat16),
            pltpu.VMEM((pairs // 2, blocks, modes, width), jnp.bfloat16),
            pltpu.SMEM((pairs,), jnp.int32),
            pltpu.SMEM((slots,), jnp.int32),
            pltpu.SMEM((slots,), jnp.int32),
            pltpu.SMEM((slots + 1,), jnp.int32),
            pltpu.SemaphoreType.DMA((pairs * blocks + 3,)),
            pltpu.SemaphoreType.DMA((slots,)),
        ],
        compiler_params=pltpu.CompilerParams(vmem_limit_bytes=12 * 2**20),
        cost_estimate=pl.CostEstimate(flops=2 * pairs * blocks * modes * width * width,
                                      bytes_accessed=25 * 10**6, transcendentals=0),
    )(*map(in_hbm, (partner, counts, own, coupling)))
    return out[0], out[1:8], out[8:11]


def nt(a, b):
    return lax.dot_general(a, b, (((1,), (1,)), ((), ())), preferred_element_type=jnp.float32)


def pair_kernel(partner_ref, left_ref, *rest):
    (kept, near, far, low, high, ring_mine, ring_other, across), out_hbm = rest[:8], rest[8]
    panels, outs, panel_sem, out_sem = rest[9:]
    pairs, count = panels.shape[0], outs.shape[0]

    def save(i):
        return pltpu.make_async_copy(outs.at[i], out_hbm.at[i // 2, i % 2], out_sem.at[i])

    @pl.loop(0, pairs)
    def _(q):
        code = partner_ref[q]
        d1, d2 = offsets(code)
        dz, core, me = ring_offset(code)
        step = jnp.where((dz == 1) | (dz == 3), jnp.where((dz == 3) == (core == 0), 1, 2), jnp.where(dz == 2, 3, 0))
        along = code < SPAN_X
        for ref, index, chosen in (
            (kept, d1, along & (d2 == 0)),
            (near, d1, along & (d2 == 1)),
            (far, d1, along & (d2 == 3)),
            (low, d1, along & (d2 == 2) & (d1 < 2)),
            (high, d1 - 2, along & (d2 == 2) & (d1 >= 2)),
            (ring_mine, step, (code >= SPAN_X) & (dz != 2) & (core == me)),
            (ring_other, step, (code >= SPAN_X) & (dz != 2) & (core != me)),
            (across, jnp.where(core == me, 0, 1), (code >= SPAN_X) & (dz == 2)),
        ):
            @pl.when(chosen)
            def _():
                pltpu.make_async_copy(ref.at[index], panels.at[q], panel_sem.at[q]).start()

    @pl.loop(0, count)
    def _(i):
        p = i // 2

        @pl.when(i % 2 == 0)
        def _():
            pltpu.make_async_copy(kept.at[0], panels.at[p], panel_sem.at[p]).wait()

        outs[i] = nt(left_ref[p, i % 2], panels[p]).astype(jnp.bfloat16)
        save(i).start()

    @pl.loop(0, count)
    def _(i):
        save(i).wait()


def pair_products(left, sources, partner):
    pairs, blocks, modes, width = left.shape
    hbm, smem = pl.BlockSpec(memory_space=pltpu.HBM), pl.BlockSpec(memory_space=pltpu.SMEM)
    return pl.pallas_call(
        pair_kernel,
        in_specs=[smem, pl.BlockSpec(memory_space=pltpu.VMEM)] + [pl.BlockSpec(memory_space=pl.ANY)] * 8,
        out_specs=hbm,
        out_shape=jax.ShapeDtypeStruct((pairs, blocks, modes, modes), jnp.bfloat16),
        scratch_shapes=[
            pltpu.VMEM((pairs, modes, width), jnp.bfloat16),
            pltpu.VMEM((pairs * blocks, modes, modes), jnp.bfloat16),
            pltpu.SemaphoreType.DMA((pairs,)),
            pltpu.SemaphoreType.DMA((pairs * blocks,)),
        ],
        compiler_params=pltpu.CompilerParams(vmem_limit_bytes=14 * 2**20),
        cost_estimate=pl.CostEstimate(flops=2 * pairs * blocks * modes * width * modes,
                                      bytes_accessed=15 * 10**6, transcendentals=0),
    )(partner, left, *sources)


def partner_kernel(own_ref, sum_ref, *rest):
    last, out_ref = rest[:-1], rest[-1]

    @pl.loop(0, out_ref.shape[0])
    def _(t):
        total = sum_ref[t]
        for ref in last:
            total = total + ref[t].astype(jnp.float32)
        out_ref[t] = nt(own_ref[...], total.astype(jnp.bfloat16))


def partner_products(own, start, last):
    modes, _ = own.shape
    blocks = start.shape[0]
    return pl.pallas_call(
        partner_kernel,
        out_shape=jax.ShapeDtypeStruct((blocks, modes, modes), jnp.float32),
        compiler_params=pltpu.CompilerParams(vmem_limit_bytes=16 * 2**20),
    )(own, start, *last)


def permuted(value, move):
    pairs = []
    for n in range(SPAN_X * SPAN_Y):
        here = (n // SPAN_Y // SIDE, n // SPAN_Y % SIDE, n % SPAN_Y // 2, n % 2)
        x, y, z, c = move(*here)
        pairs.append((n, ((x % SIDE) * SIDE + y % SIDE) * SPAN_Y + (z % SIDE) * 2 + c))
    return lax.ppermute(value, ("sx", "sy"), pairs)


def first(value, by):
    return permuted(value, lambda x, y, z, c: (x + by, y, z, c) if c == 0 else (x, y + by, z, c))


def second(value, by):
    return permuted(value, lambda x, y, z, c: (x, y + by, z, c) if c == 0 else (x + by, y, z, c))


def turn(value, by):
    return permuted(value, lambda x, y, z, c: (x, y, z + (by if c == 0 else -by), c))


def swap(value):
    return permuted(value, lambda x, y, z, c: (x, y, z, 1 - c))


def added(*terms):
    return sum(v.astype(jnp.float32) for v in terms)


def rounded(*terms):
    return added(*terms).astype(jnp.bfloat16)


def after(value, *others):
    return lax.optimization_barrier((value,) + others)[0]


def body(panels, coupling, partner, counts):
    own = jnp.swapaxes(panels[0], 0, 1)
    barrier = lax.optimization_barrier

    moved = [first(own, -1), first(own, 2), first(own, 1)]
    ring1, ring2 = turn(own, 1), turn(own, -1)
    kept = jnp.stack([own] + moved)
    kept = barrier(kept)
    near, far = second(kept, -1), second(kept, 1)
    left, (up, up_end, down, down_end, pass_up, pass_down, here), (z_near, z_far, z_mine) = left_products(
        own, coupling, partner, after(counts, kept)
    )

    got_up, got_down = first(up, 1), first(down, -1)
    up_end, down_end, z_far, near, far = barrier((up_end, down_end, z_far, near, far))
    end_up, end_down = first(up_end, 1), first(down_end, -1)
    last_up, last_down = first(rounded(pass_up, got_up), 1), first(rounded(pass_down, got_down), -1)

    ring_mine = jnp.stack([own, ring1, ring2])
    ring_other = swap(after(ring_mine, up))
    far_sum = swap(z_far)
    across = turn(jnp.stack([ring2, ring_other[1]]), -1)
    near_sum = swap(after(z_near, ring_other))
    w = [rounded(z_mine[k], (near_sum, far_sum)[k // 2][k % 2]) for k in range(SIDE)]

    near, far, w3, end_up, end_down = barrier((near, far, w[3], end_up, end_down))
    low, high = second(near[:2], -1), second(far[2:], 1)
    opposite = turn(w3, 1)
    low, high, opposite, across, ring_other, w = barrier((low, high, opposite, across, ring_other, w))
    z_last, back = turn(rounded(w[1], opposite), 1), turn(w[2], -1)

    v = [
        rounded(here[0], end_down[0], last_up[0]),
        rounded(here[1], end_down[1], last_up[1]),
        rounded(here[2], end_up[0], last_down[0]),
        rounded(here[3], end_up[1], last_down[1]),
    ]
    ends = [second(v[1], 1), second(v[3], -1), second(v[2], 2)]

    sources = [kept, near, far, low, high, ring_mine, ring_other, across]
    pair_blocks = pair_products(left, sources, after(partner, *v, z_last, back))
    pair_blocks, ends = barrier((pair_blocks, ends))
    partner_blocks = partner_products(own, added(v[0], w[0], back, z_last), ends)
    return (pair_blocks, partner_blocks[None])


def solution(mesh):
    placed = (
        P(("sx", "sy"), None, None),
        P(("sx", "sy"), None, None, None),
        P(("sx", "sy")),
        P(("sx", "sy")),
    )
    return jax.shard_map(
        body,
        mesh=mesh,
        in_specs=placed,
        out_specs=(P(("sx", "sy"), None, None, None), P(("sx", "sy"), None, None, None)),
        check_vma=False,
    )
```

```python
import jax
import jax.numpy as jnp
from jax import lax
from jax.experimental import pallas as pl
from jax.experimental.pallas import tpu as pltpu
from jax.sharding import PartitionSpec as P

SIDE = 4
SPAN_X, SPAN_Y = SIDE * SIDE, 2 * SIDE
PARTS = ((0, 2), (2, 2), (4, 2), (6, 2), (8, 2), (10, 2), (12, 4))
RINGS = ((16, 2), (18, 2), (20, 4))
CHUNK = 80


def slot_of(d1, d2):
    low = d2 < 2
    return jnp.where(
        d1 == 0, 12 + d2,
        jnp.where(d1 == 1, jnp.where(low, 8 + d2, d2),
                  jnp.where(d1 == 2, jnp.where(low, d2, 2 + d2), jnp.where(low, 6 + d2, 8 + d2))))


def offsets(code):
    me = lax.axis_index("sx")
    dx = (code // SIDE - me // SIDE + SIDE) % SIDE
    dy = (code % SIDE - me % SIDE + SIDE) % SIDE
    swapped = lax.axis_index("sy") % 2 == 1
    return jnp.where(swapped, dy, dx), jnp.where(swapped, dx, dy)


def ring_offset(code):
    me = lax.axis_index("sy")
    other = code - SPAN_X
    return (other // 2 - me // 2 + SIDE) % SIDE, other % 2, me % 2


def left_kernel(partner_hbm, counts_hbm, own_hbm, coupling_hbm, left_ref, *rest):
    outs = rest[:10]
    partner_ref, counts_ref, own_ref, blocks, zero, sums = rest[10:16]
    keys, number, seen, at_sum, in_sem, out_sem = rest[16:]
    pairs, width = blocks.shape[0], blocks.shape[1]
    count, modes = 2 * pairs, own_ref.shape[0]
    slots = SPAN_X + SPAN_Y

    def load(i):
        return pltpu.make_async_copy(coupling_hbm.at[i // 2, i % 2],
                                     blocks.at[i // 2, :, pl.ds(pl.multiple_of(i % 2 * width, width), width)], in_sem.at[i])

    load_partner = pltpu.make_async_copy(partner_hbm, partner_ref, in_sem.at[count + 1])
    load_partner.start()
    load_counts = pltpu.make_async_copy(counts_hbm, counts_ref, in_sem.at[count + 2])
    load_counts.start()
    load_own = pltpu.make_async_copy(own_hbm, own_ref, in_sem.at[count])
    load_own.start()

    @pl.loop(0, count)
    def _(i):
        load(i).start()

    @pl.loop(0, slots)
    def _(k):
        number[k] = 0
        seen[k] = 0

    at_sum[slots] = 0
    load_partner.wait()
    load_counts.wait()

    @pl.loop(0, pairs)
    def _(p):
        code = partner_ref[p]
        d1, d2 = offsets(code)
        dz, core, me = ring_offset(code)
        step = jnp.where((dz == 1) | (dz == 3), jnp.where((dz == 1) == (core == 0), 1, 2), jnp.where(dz == 2, 3, 0))
        key = jnp.where(code < SPAN_X, slot_of(d1, d2), SPAN_X + step + jnp.where(core == me, SIDE, 0))
        keys[p] = key
        number[key] = number[key] + 1

    @pl.loop(0, 2 * (modes // CHUNK))
    def _(r):
        rows = pl.ds(pl.multiple_of(r // 2 * CHUNK, CHUNK), CHUNK)
        zero[r % 2, rows] = jnp.zeros((CHUNK, width), zero.dtype)

    def send(source, key):
        for out, (at, size) in zip(outs, PARTS + RINGS, strict=True):
            @pl.when((key >= at) & (key < at + size))
            def _():
                pltpu.make_async_copy(source, out.at[key - at], out_sem.at[key]).start()

    @pl.loop(0, slots)
    def _(k):
        @pl.when(number[k] == 0)
        def _():
            send(zero, k)

    load_own.wait()

    @pl.loop(0, pairs)
    def _(p):
        load(2 * p).wait()
        load(2 * p + 1).wait()
        keep = lax.broadcasted_iota(jnp.int32, (1, width), 1) < counts_ref[p]
        own = jnp.where(keep, own_ref[...], jnp.zeros((modes, width), own_ref.dtype))
        product = jnp.dot(own, blocks[p], preferred_element_type=jnp.float32)
        for t in range(2):
            left_ref[p, t] = jnp.where(keep, product[:, t * width:(t + 1) * width], 0.0).astype(jnp.bfloat16)
        key = keys[p]
        single = number[key] == 1

        @pl.when(single)
        def _():
            send(left_ref.at[p], key)

        @pl.when(jnp.logical_not(single))
        def _():
            fresh = seen[key] == 0

            @pl.when(fresh)
            def _():
                at_sum[key] = at_sum[slots]
                at_sum[slots] = at_sum[slots] + 1

            seen[key] = seen[key] + 1
            place = at_sum[key]

            @pl.loop(0, 2 * (modes // CHUNK))
            def _(r):
                t, rows = r % 2, pl.ds(pl.multiple_of(r // 2 * CHUNK, CHUNK), CHUNK)
                before = jnp.where(fresh, 0.0, sums[place, t, rows].astype(jnp.float32))
                sums[place, t, rows] = (before + left_ref[p, t, rows].astype(jnp.float32)).astype(jnp.bfloat16)

            @pl.when(seen[key] == number[key])
            def _():
                send(sums.at[place], key)

    @pl.loop(0, slots)
    def _(k):
        pltpu.make_async_copy(zero, outs[0].at[0], out_sem.at[k]).wait()


def in_hbm(value):
    return pltpu.with_memory_space_constraint(value, pltpu.HBM)


def left_products(own, coupling, partner, counts):
    pairs, blocks, width, _ = coupling.shape
    modes = own.shape[0]
    slots = SPAN_X + SPAN_Y
    sizes = [pairs] + [size for _, size in PARTS + RINGS]
    hbm, vmem = pltpu.HBM, pltpu.VMEM
    spaces = [vmem] + [hbm] * 4 + [vmem] * 2 + [hbm] * 4
    out = pl.pallas_call(
        left_kernel,
        in_specs=[pl.BlockSpec(memory_space=pltpu.HBM)] * 4,
        out_specs=[pl.BlockSpec(memory_space=space) for space in spaces],
        out_shape=[space((n, blocks, modes, width), jnp.bfloat16) for n, space in zip(sizes, spaces, strict=True)],
        scratch_shapes=[
            pltpu.SMEM((pairs,), jnp.int32),
            pltpu.SMEM((pairs,), jnp.int32),
            pltpu.VMEM((modes, width), jnp.bfloat16),
            pltpu.VMEM((pairs, width, blocks * width), jnp.bfloat16),
            pltpu.VMEM((blocks, modes, width), jnp.bfloat16),
            pltpu.VMEM((pairs // 2, blocks, modes, width), jnp.bfloat16),
            pltpu.SMEM((pairs,), jnp.int32),
            pltpu.SMEM((slots,), jnp.int32),
            pltpu.SMEM((slots,), jnp.int32),
            pltpu.SMEM((slots + 1,), jnp.int32),
            pltpu.SemaphoreType.DMA((pairs * blocks + 3,)),
            pltpu.SemaphoreType.DMA((slots,)),
        ],
        compiler_params=pltpu.CompilerParams(vmem_limit_bytes=12 * 2**20),
        cost_estimate=pl.CostEstimate(flops=2 * pairs * blocks * modes * width * width,
                                      bytes_accessed=25 * 10**6, transcendentals=0),
    )(*map(in_hbm, (partner, counts, own, coupling)))
    return out[0], out[1:8], out[8:11]


def nt(a, b):
    return lax.dot_general(a, b, (((1,), (1,)), ((), ())), preferred_element_type=jnp.float32)


def pair_kernel(partner_ref, left_ref, *rest):
    (kept, near, far, low, high, ring_mine, ring_other, across), out_hbm = rest[:8], rest[8]
    panels, outs, panel_sem, out_sem = rest[9:]
    pairs, count = panels.shape[0], outs.shape[0]

    def save(i):
        return pltpu.make_async_copy(outs.at[i], out_hbm.at[i // 2, i % 2], out_sem.at[i])

    @pl.loop(0, pairs)
    def _(q):
        code = partner_ref[q]
        d1, d2 = offsets(code)
        dz, core, me = ring_offset(code)
        step = jnp.where((dz == 1) | (dz == 3), jnp.where((dz == 3) == (core == 0), 1, 2), jnp.where(dz == 2, 3, 0))
        along = code < SPAN_X
        for ref, index, chosen in (
            (kept, d1, along & (d2 == 0)),
            (near, d1, along & (d2 == 1)),
            (far, d1, along & (d2 == 3)),
            (low, d1, along & (d2 == 2) & (d1 < 2)),
            (high, d1 - 2, along & (d2 == 2) & (d1 >= 2)),
            (ring_mine, step, (code >= SPAN_X) & (dz != 2) & (core == me)),
            (ring_other, step, (code >= SPAN_X) & (dz != 2) & (core != me)),
            (across, jnp.where(core == me, 0, 1), (code >= SPAN_X) & (dz == 2)),
        ):
            @pl.when(chosen)
            def _():
                pltpu.make_async_copy(ref.at[index], panels.at[q], panel_sem.at[q]).start()

    @pl.loop(0, count)
    def _(i):
        p = i // 2

        @pl.when(i % 2 == 0)
        def _():
            pltpu.make_async_copy(kept.at[0], panels.at[p], panel_sem.at[p]).wait()

        outs[i] = nt(left_ref[p, i % 2], panels[p]).astype(jnp.bfloat16)
        save(i).start()

    @pl.loop(0, count)
    def _(i):
        save(i).wait()


def pair_products(left, sources, partner):
    pairs, blocks, modes, width = left.shape
    hbm, smem = pl.BlockSpec(memory_space=pltpu.HBM), pl.BlockSpec(memory_space=pltpu.SMEM)
    return pl.pallas_call(
        pair_kernel,
        in_specs=[smem, pl.BlockSpec(memory_space=pltpu.VMEM)] + [pl.BlockSpec(memory_space=pl.ANY)] * 8,
        out_specs=hbm,
        out_shape=jax.ShapeDtypeStruct((pairs, blocks, modes, modes), jnp.bfloat16),
        scratch_shapes=[
            pltpu.VMEM((pairs, modes, width), jnp.bfloat16),
            pltpu.VMEM((pairs * blocks, modes, modes), jnp.bfloat16),
            pltpu.SemaphoreType.DMA((pairs,)),
            pltpu.SemaphoreType.DMA((pairs * blocks,)),
        ],
        compiler_params=pltpu.CompilerParams(vmem_limit_bytes=14 * 2**20),
        cost_estimate=pl.CostEstimate(flops=2 * pairs * blocks * modes * width * modes,
                                      bytes_accessed=15 * 10**6, transcendentals=0),
    )(partner, left, *sources)


def partner_kernel(own_ref, sum_ref, *rest):
    last, out_ref = rest[:-1], rest[-1]

    @pl.loop(0, out_ref.shape[0])
    def _(t):
        total = sum_ref[t]
        for ref in last:
            total = total + ref[t].astype(jnp.float32)
        out_ref[t] = nt(own_ref[...], total.astype(jnp.bfloat16))


def partner_products(own, start, last):
    modes, _ = own.shape
    blocks = start.shape[0]
    return pl.pallas_call(
        partner_kernel,
        out_shape=jax.ShapeDtypeStruct((blocks, modes, modes), jnp.float32),
        compiler_params=pltpu.CompilerParams(vmem_limit_bytes=16 * 2**20),
    )(own, start, *last)


def permuted(value, move):
    pairs = []
    for n in range(SPAN_X * SPAN_Y):
        here = (n // SPAN_Y // SIDE, n // SPAN_Y % SIDE, n % SPAN_Y // 2, n % 2)
        x, y, z, c = move(*here)
        pairs.append((n, ((x % SIDE) * SIDE + y % SIDE) * SPAN_Y + (z % SIDE) * 2 + c))
    return lax.ppermute(value, ("sx", "sy"), pairs)


def first(value, by):
    return permuted(value, lambda x, y, z, c: (x + by, y, z, c) if c == 0 else (x, y + by, z, c))


def second(value, by):
    return permuted(value, lambda x, y, z, c: (x, y + by, z, c) if c == 0 else (x + by, y, z, c))


def turn(value, by):
    return permuted(value, lambda x, y, z, c: (x, y, z + (by if c == 0 else -by), c))


def swap(value):
    return permuted(value, lambda x, y, z, c: (x, y, z, 1 - c))


def added(*terms):
    return sum(v.astype(jnp.float32) for v in terms)


def rounded(*terms):
    return added(*terms).astype(jnp.bfloat16)


def after(value, *others):
    return lax.optimization_barrier((value,) + others)[0]


def body(panels, coupling, partner, counts):
    own = jnp.swapaxes(panels[0], 0, 1)
    barrier = lax.optimization_barrier

    moved = [first(own, -1), first(own, 2), first(own, 1)]
    ring1, ring2 = turn(own, 1), turn(own, -1)
    kept = jnp.stack([own] + moved)
    kept = barrier(kept)
    near, far = second(kept, -1), second(kept, 1)
    left, (up, up_end, down, down_end, pass_up, pass_down, here), (z_near, z_far, z_mine) = left_products(
        own, coupling, partner, after(counts, kept)
    )

    got_up, got_down = first(up, 1), first(down, -1)
    up_end, down_end, z_far, near, far = barrier((up_end, down_end, z_far, near, far))
    end_up, end_down = first(up_end, 1), first(down_end, -1)
    last_up, last_down = first(rounded(pass_up, got_up), 1), first(rounded(pass_down, got_down), -1)

    ring_mine = jnp.stack([own, ring1, ring2])
    ring_other = swap(after(ring_mine, up))
    far_sum = swap(z_far)
    across = turn(jnp.stack([ring2, ring_other[1]]), -1)
    near_sum = swap(after(z_near, ring_other))
    w = [rounded(z_mine[k], (near_sum, far_sum)[k // 2][k % 2]) for k in range(SIDE)]

    near, far, w3, end_up, end_down = barrier((near, far, w[3], end_up, end_down))
    low, high = second(near[:2], -1), second(far[2:], 1)
    opposite = turn(w3, 1)
    low, high, opposite, across, ring_other, w = barrier((low, high, opposite, across, ring_other, w))
    z_last = turn(rounded(w[1], opposite), 1)

    v = [
        rounded(here[0], end_down[0], last_up[0]),
        rounded(here[1], end_down[1], last_up[1]),
        rounded(here[2], end_up[0], last_down[0]),
        rounded(here[3], end_up[1], last_down[1]),
    ]
    v, w2 = barrier((v, w[2]))
    back = turn(w2, -1)
    ends = [second(v[1], 1), second(v[3], -1), second(v[2], 2)]

    sources = [kept, near, far, low, high, ring_mine, ring_other, across]
    pair_blocks = pair_products(left, sources, after(partner, *v, z_last))
    pair_blocks, ends = barrier((pair_blocks, ends))
    partner_blocks = partner_products(own, added(v[0], w[0], back, z_last), ends)
    return (pair_blocks, partner_blocks[None])


def solution(mesh):
    placed = (
        P(("sx", "sy"), None, None),
        P(("sx", "sy"), None, None, None),
        P(("sx", "sy")),
        P(("sx", "sy")),
    )
    return jax.shard_map(
        body,
        mesh=mesh,
        in_specs=placed,
        out_specs=(P(("sx", "sy"), None, None, None), P(("sx", "sy"), None, None, None)),
        check_vma=False,
    )
```

```python
import jax
import jax.numpy as jnp
from jax import lax
from jax.experimental import pallas as pl
from jax.experimental.pallas import tpu as pltpu
from jax.sharding import PartitionSpec as P

SIDE = 4
SPAN_X, SPAN_Y = SIDE * SIDE, 2 * SIDE
PARTS = ((0, 2), (2, 2), (4, 2), (6, 2), (8, 2), (10, 2), (12, 4))
RINGS = ((16, 2), (18, 2), (20, 4))
CHUNK = 80


def slot_of(d1, d2):
    low = d2 < 2
    return jnp.where(
        d1 == 0, 12 + d2,
        jnp.where(d1 == 1, jnp.where(low, 8 + d2, d2),
                  jnp.where(d1 == 2, jnp.where(low, d2, 2 + d2), jnp.where(low, 6 + d2, 8 + d2))))


def offsets(code):
    me = lax.axis_index("sx")
    dx = (code // SIDE - me // SIDE + SIDE) % SIDE
    dy = (code % SIDE - me % SIDE + SIDE) % SIDE
    swapped = lax.axis_index("sy") % 2 == 1
    return jnp.where(swapped, dy, dx), jnp.where(swapped, dx, dy)


def ring_offset(code):
    me = lax.axis_index("sy")
    other = code - SPAN_X
    return (other // 2 - me // 2 + SIDE) % SIDE, other % 2, me % 2


def left_kernel(partner_hbm, counts_hbm, own_hbm, coupling_hbm, left_ref, *rest):
    outs = rest[:10]
    partner_ref, counts_ref, own_ref, blocks, zero, sums = rest[10:16]
    keys, number, seen, at_sum, in_sem, out_sem = rest[16:]
    pairs, width = blocks.shape[0], blocks.shape[1]
    count, modes = 2 * pairs, own_ref.shape[0]
    slots = SPAN_X + SPAN_Y

    def load(i):
        return pltpu.make_async_copy(coupling_hbm.at[i // 2, i % 2],
                                     blocks.at[i // 2, :, pl.ds(pl.multiple_of(i % 2 * width, width), width)], in_sem.at[i])

    load_partner = pltpu.make_async_copy(partner_hbm, partner_ref, in_sem.at[count + 1])
    load_partner.start()
    load_counts = pltpu.make_async_copy(counts_hbm, counts_ref, in_sem.at[count + 2])
    load_counts.start()
    load_own = pltpu.make_async_copy(own_hbm, own_ref, in_sem.at[count])
    load_own.start()

    @pl.loop(0, count)
    def _(i):
        load(i).start()

    @pl.loop(0, slots)
    def _(k):
        number[k] = 0
        seen[k] = 0

    at_sum[slots] = 0
    load_partner.wait()
    load_counts.wait()

    @pl.loop(0, pairs)
    def _(p):
        code = partner_ref[p]
        d1, d2 = offsets(code)
        dz, core, me = ring_offset(code)
        step = jnp.where((dz == 1) | (dz == 3), jnp.where((dz == 1) == (core == 0), 1, 2), jnp.where(dz == 2, 3, 0))
        key = jnp.where(code < SPAN_X, slot_of(d1, d2), SPAN_X + step + jnp.where(core == me, SIDE, 0))
        keys[p] = key
        number[key] = number[key] + 1

    @pl.loop(0, 2 * (modes // CHUNK))
    def _(r):
        rows = pl.ds(pl.multiple_of(r // 2 * CHUNK, CHUNK), CHUNK)
        zero[r % 2, rows] = jnp.zeros((CHUNK, width), zero.dtype)

    def send(source, key):
        for out, (at, size) in zip(outs, PARTS + RINGS, strict=True):
            @pl.when((key >= at) & (key < at + size))
            def _():
                pltpu.make_async_copy(source, out.at[key - at], out_sem.at[key]).start()

    @pl.loop(0, slots)
    def _(k):
        @pl.when(number[k] == 0)
        def _():
            send(zero, k)

    load_own.wait()

    @pl.loop(0, pairs)
    def _(p):
        load(2 * p).wait()
        load(2 * p + 1).wait()
        keep = lax.broadcasted_iota(jnp.int32, (1, width), 1) < counts_ref[p]
        own = jnp.where(keep, own_ref[...], jnp.zeros((modes, width), own_ref.dtype))
        product = jnp.dot(own, blocks[p], preferred_element_type=jnp.float32)
        for t in range(2):
            left_ref[p, t] = jnp.where(keep, product[:, t * width:(t + 1) * width], 0.0).astype(jnp.bfloat16)
        key = keys[p]
        single = number[key] == 1

        @pl.when(single)
        def _():
            send(left_ref.at[p], key)

        @pl.when(jnp.logical_not(single))
        def _():
            fresh = seen[key] == 0

            @pl.when(fresh)
            def _():
                at_sum[key] = at_sum[slots]
                at_sum[slots] = at_sum[slots] + 1

            seen[key] = seen[key] + 1
            place = at_sum[key]

            @pl.loop(0, 2 * (modes // CHUNK))
            def _(r):
                t, rows = r % 2, pl.ds(pl.multiple_of(r // 2 * CHUNK, CHUNK), CHUNK)
                before = jnp.where(fresh, 0.0, sums[place, t, rows].astype(jnp.float32))
                sums[place, t, rows] = (before + left_ref[p, t, rows].astype(jnp.float32)).astype(jnp.bfloat16)

            @pl.when(seen[key] == number[key])
            def _():
                send(sums.at[place], key)

    @pl.loop(0, slots)
    def _(k):
        pltpu.make_async_copy(zero, outs[0].at[0], out_sem.at[k]).wait()


def in_hbm(value):
    return pltpu.with_memory_space_constraint(value, pltpu.HBM)


def left_products(own, coupling, partner, counts):
    pairs, blocks, width, _ = coupling.shape
    modes = own.shape[0]
    slots = SPAN_X + SPAN_Y
    sizes = [pairs] + [size for _, size in PARTS + RINGS]
    hbm, vmem = pltpu.HBM, pltpu.VMEM
    spaces = [vmem] + [hbm] * 4 + [vmem] * 2 + [hbm] * 4
    out = pl.pallas_call(
        left_kernel,
        in_specs=[pl.BlockSpec(memory_space=pltpu.HBM)] * 4,
        out_specs=[pl.BlockSpec(memory_space=space) for space in spaces],
        out_shape=[space((n, blocks, modes, width), jnp.bfloat16) for n, space in zip(sizes, spaces, strict=True)],
        scratch_shapes=[
            pltpu.SMEM((pairs,), jnp.int32),
            pltpu.SMEM((pairs,), jnp.int32),
            pltpu.VMEM((modes, width), jnp.bfloat16),
            pltpu.VMEM((pairs, width, blocks * width), jnp.bfloat16),
            pltpu.VMEM((blocks, modes, width), jnp.bfloat16),
            pltpu.VMEM((pairs // 2, blocks, modes, width), jnp.bfloat16),
            pltpu.SMEM((pairs,), jnp.int32),
            pltpu.SMEM((slots,), jnp.int32),
            pltpu.SMEM((slots,), jnp.int32),
            pltpu.SMEM((slots + 1,), jnp.int32),
            pltpu.SemaphoreType.DMA((pairs * blocks + 3,)),
            pltpu.SemaphoreType.DMA((slots,)),
        ],
        compiler_params=pltpu.CompilerParams(vmem_limit_bytes=12 * 2**20),
        cost_estimate=pl.CostEstimate(flops=2 * pairs * blocks * modes * width * width,
                                      bytes_accessed=25 * 10**6, transcendentals=0),
    )(*map(in_hbm, (partner, counts, own, coupling)))
    return out[0], out[1:8], out[8:11]


def nt(a, b):
    return lax.dot_general(a, b, (((1,), (1,)), ((), ())), preferred_element_type=jnp.float32)


def pair_kernel(partner_ref, left_ref, *rest):
    (kept, near, far, low, high, ring_mine, ring_other, across), out_hbm = rest[:8], rest[8]
    panels, outs, panel_sem, out_sem = rest[9:]
    pairs, count = panels.shape[0], outs.shape[0]

    def save(i):
        return pltpu.make_async_copy(outs.at[i], out_hbm.at[i // 2, i % 2], out_sem.at[i])

    @pl.loop(0, pairs)
    def _(q):
        code = partner_ref[q]
        d1, d2 = offsets(code)
        dz, core, me = ring_offset(code)
        step = jnp.where((dz == 1) | (dz == 3), jnp.where((dz == 3) == (core == 0), 1, 2), jnp.where(dz == 2, 3, 0))
        along = code < SPAN_X
        for ref, index, chosen in (
            (kept, d1, along & (d2 == 0)),
            (near, d1, along & (d2 == 1)),
            (far, d1, along & (d2 == 3)),
            (low, d1, along & (d2 == 2) & (d1 < 2)),
            (high, d1 - 2, along & (d2 == 2) & (d1 >= 2)),
            (ring_mine, step, (code >= SPAN_X) & (dz != 2) & (core == me)),
            (ring_other, step, (code >= SPAN_X) & (dz != 2) & (core != me)),
            (across, jnp.where(core == me, 0, 1), (code >= SPAN_X) & (dz == 2)),
        ):
            @pl.when(chosen)
            def _():
                pltpu.make_async_copy(ref.at[index], panels.at[q], panel_sem.at[q]).start()

    @pl.loop(0, pairs)
    def _(p):
        pltpu.make_async_copy(kept.at[0], panels.at[p], panel_sem.at[p]).wait()
        modes, width = panels.shape[1:]
        product = nt(left_ref[p].reshape(2 * modes, width), panels[p])
        for t in range(2):
            outs[2 * p + t] = product[t * modes:(t + 1) * modes].astype(jnp.bfloat16)
            save(2 * p + t).start()

    @pl.loop(0, count)
    def _(i):
        save(i).wait()


def pair_products(left, sources, partner):
    pairs, blocks, modes, width = left.shape
    hbm, smem = pl.BlockSpec(memory_space=pltpu.HBM), pl.BlockSpec(memory_space=pltpu.SMEM)
    return pl.pallas_call(
        pair_kernel,
        in_specs=[smem, pl.BlockSpec(memory_space=pltpu.VMEM)] + [pl.BlockSpec(memory_space=pl.ANY)] * 8,
        out_specs=hbm,
        out_shape=jax.ShapeDtypeStruct((pairs, blocks, modes, modes), jnp.bfloat16),
        scratch_shapes=[
            pltpu.VMEM((pairs, modes, width), jnp.bfloat16),
            pltpu.VMEM((pairs * blocks, modes, modes), jnp.bfloat16),
            pltpu.SemaphoreType.DMA((pairs,)),
            pltpu.SemaphoreType.DMA((pairs * blocks,)),
        ],
        compiler_params=pltpu.CompilerParams(vmem_limit_bytes=14 * 2**20),
        cost_estimate=pl.CostEstimate(flops=2 * pairs * blocks * modes * width * modes,
                                      bytes_accessed=15 * 10**6, transcendentals=0),
    )(partner, left, *sources)


def partner_kernel(own_ref, sum_ref, *rest):
    last, out_ref = rest[:-1], rest[-1]

    @pl.loop(0, out_ref.shape[0])
    def _(t):
        total = sum_ref[t]
        for ref in last:
            total = total + ref[t].astype(jnp.float32)
        out_ref[t] = nt(own_ref[...], total.astype(jnp.bfloat16))


def partner_products(own, start, last):
    modes, _ = own.shape
    blocks = start.shape[0]
    return pl.pallas_call(
        partner_kernel,
        out_shape=jax.ShapeDtypeStruct((blocks, modes, modes), jnp.float32),
        compiler_params=pltpu.CompilerParams(vmem_limit_bytes=16 * 2**20),
    )(own, start, *last)


def permuted(value, move):
    pairs = []
    for n in range(SPAN_X * SPAN_Y):
        here = (n // SPAN_Y // SIDE, n // SPAN_Y % SIDE, n % SPAN_Y // 2, n % 2)
        x, y, z, c = move(*here)
        pairs.append((n, ((x % SIDE) * SIDE + y % SIDE) * SPAN_Y + (z % SIDE) * 2 + c))
    return lax.ppermute(value, ("sx", "sy"), pairs)


def first(value, by):
    return permuted(value, lambda x, y, z, c: (x + by, y, z, c) if c == 0 else (x, y + by, z, c))


def second(value, by):
    return permuted(value, lambda x, y, z, c: (x, y + by, z, c) if c == 0 else (x + by, y, z, c))


def turn(value, by):
    return permuted(value, lambda x, y, z, c: (x, y, z + (by if c == 0 else -by), c))


def swap(value):
    return permuted(value, lambda x, y, z, c: (x, y, z, 1 - c))


def added(*terms):
    return sum(v.astype(jnp.float32) for v in terms)


def rounded(*terms):
    return added(*terms).astype(jnp.bfloat16)


def after(value, *others):
    return lax.optimization_barrier((value,) + others)[0]


def body(panels, coupling, partner, counts):
    own = jnp.swapaxes(panels[0], 0, 1)
    barrier = lax.optimization_barrier

    moved = [first(own, -1), first(own, 2), first(own, 1)]
    ring1, ring2 = turn(own, 1), turn(own, -1)
    kept = jnp.stack([own] + moved)
    kept = barrier(kept)
    near, far = second(kept, -1), second(kept, 1)
    left, (up, up_end, down, down_end, pass_up, pass_down, here), (z_near, z_far, z_mine) = left_products(
        own, coupling, partner, after(counts, kept)
    )

    got_up, got_down = first(up, 1), first(down, -1)
    up_end, down_end, z_far, near, far = barrier((up_end, down_end, z_far, near, far))
    end_up, end_down = first(up_end, 1), first(down_end, -1)
    last_up, last_down = first(rounded(pass_up, got_up), 1), first(rounded(pass_down, got_down), -1)

    ring_mine = jnp.stack([own, ring1, ring2])
    ring_other = swap(after(ring_mine, up))
    far_sum = swap(z_far)
    across = turn(jnp.stack([ring2, ring_other[1]]), -1)
    near_sum = swap(after(z_near, ring_other))
    w = [rounded(z_mine[k], (near_sum, far_sum)[k // 2][k % 2]) for k in range(SIDE)]

    near, far, w3, end_up, end_down = barrier((near, far, w[3], end_up, end_down))
    low, high = second(near[:2], -1), second(far[2:], 1)
    opposite = turn(w3, 1)
    low, high, opposite, across, ring_other, w = barrier((low, high, opposite, across, ring_other, w))
    z_last = turn(rounded(w[1], opposite), 1)

    v = [
        rounded(here[0], end_down[0], last_up[0]),
        rounded(here[1], end_down[1], last_up[1]),
        rounded(here[2], end_up[0], last_down[0]),
        rounded(here[3], end_up[1], last_down[1]),
    ]
    v, w2 = barrier((v, w[2]))
    back = turn(w2, -1)
    ends = [second(v[1], 1), second(v[3], -1), second(v[2], 2)]

    sources = [kept, near, far, low, high, ring_mine, ring_other, across]
    pair_blocks = pair_products(left, sources, after(partner, *v, z_last))
    pair_blocks, ends = barrier((pair_blocks, ends))
    partner_blocks = partner_products(own, added(v[0], w[0], back, z_last), ends)
    return (pair_blocks, partner_blocks[None])


def solution(mesh):
    placed = (
        P(("sx", "sy"), None, None),
        P(("sx", "sy"), None, None, None),
        P(("sx", "sy")),
        P(("sx", "sy")),
    )
    return jax.shard_map(
        body,
        mesh=mesh,
        in_specs=placed,
        out_specs=(P(("sx", "sy"), None, None, None), P(("sx", "sy"), None, None, None)),
        check_vma=False,
    )
```

```python
import jax
import jax.numpy as jnp
from jax import lax
from jax.experimental import pallas as pl
from jax.experimental.pallas import tpu as pltpu
from jax.sharding import PartitionSpec as P

SIDE = 4
SPAN_X, SPAN_Y = SIDE * SIDE, 2 * SIDE
PARTS = ((0, 2), (2, 2), (4, 2), (6, 2), (8, 2), (10, 2), (12, 4))
RINGS = ((16, 2), (18, 2), (20, 4))
CHUNK = 80


def slot_of(d1, d2):
    low = d2 < 2
    return jnp.where(
        d1 == 0, 12 + d2,
        jnp.where(d1 == 1, jnp.where(low, 8 + d2, d2),
                  jnp.where(d1 == 2, jnp.where(low, d2, 2 + d2), jnp.where(low, 6 + d2, 8 + d2))))


def offsets(code):
    me = lax.axis_index("sx")
    dx = (code // SIDE - me // SIDE + SIDE) % SIDE
    dy = (code % SIDE - me % SIDE + SIDE) % SIDE
    swapped = lax.axis_index("sy") % 2 == 1
    return jnp.where(swapped, dy, dx), jnp.where(swapped, dx, dy)


def ring_offset(code):
    me = lax.axis_index("sy")
    other = code - SPAN_X
    return (other // 2 - me // 2 + SIDE) % SIDE, other % 2, me % 2


def left_kernel(partner_hbm, counts_hbm, own_hbm, coupling_hbm, left_ref, *rest):
    outs = rest[:10]
    partner_ref, counts_ref, own_ref, blocks, zero, sums = rest[10:16]
    keys, number, seen, at_sum, in_sem, out_sem = rest[16:]
    pairs, width = blocks.shape[0], blocks.shape[1]
    count, modes = 2 * pairs, own_ref.shape[0]
    slots = SPAN_X + SPAN_Y

    def load(i):
        return pltpu.make_async_copy(coupling_hbm.at[i // 2, i % 2],
                                     blocks.at[i // 2, :, pl.ds(pl.multiple_of(i % 2 * width, width), width)], in_sem.at[i])

    load_partner = pltpu.make_async_copy(partner_hbm, partner_ref, in_sem.at[count + 1])
    load_partner.start()
    load_counts = pltpu.make_async_copy(counts_hbm, counts_ref, in_sem.at[count + 2])
    load_counts.start()
    load_own = pltpu.make_async_copy(own_hbm, own_ref, in_sem.at[count])
    load_own.start()

    @pl.loop(0, count)
    def _(i):
        load(i).start()

    @pl.loop(0, slots)
    def _(k):
        number[k] = 0
        seen[k] = 0

    at_sum[slots] = 0
    load_partner.wait()
    load_counts.wait()

    @pl.loop(0, pairs)
    def _(p):
        code = partner_ref[p]
        d1, d2 = offsets(code)
        dz, core, me = ring_offset(code)
        step = jnp.where((dz == 1) | (dz == 3), jnp.where((dz == 1) == (core == 0), 1, 2), jnp.where(dz == 2, 3, 0))
        key = jnp.where(code < SPAN_X, slot_of(d1, d2), SPAN_X + step + jnp.where(core == me, SIDE, 0))
        keys[p] = key
        number[key] = number[key] + 1

    @pl.loop(0, 2 * (modes // CHUNK))
    def _(r):
        rows = pl.ds(pl.multiple_of(r // 2 * CHUNK, CHUNK), CHUNK)
        zero[r % 2, rows] = jnp.zeros((CHUNK, width), zero.dtype)

    def send(source, key):
        for out, (at, size) in zip(outs, PARTS + RINGS, strict=True):
            @pl.when((key >= at) & (key < at + size))
            def _():
                pltpu.make_async_copy(source, out.at[key - at], out_sem.at[key]).start()

    @pl.loop(0, slots)
    def _(k):
        @pl.when(number[k] == 0)
        def _():
            send(zero, k)

    load_own.wait()

    @pl.loop(0, pairs)
    def _(p):
        load(2 * p).wait()
        load(2 * p + 1).wait()
        keep = lax.broadcasted_iota(jnp.int32, (1, width), 1) < counts_ref[p]
        own = jnp.where(keep, own_ref[...], jnp.zeros((modes, width), own_ref.dtype))
        product = jnp.dot(own, blocks[p], preferred_element_type=jnp.float32)
        for t in range(2):
            left_ref[p, t] = jnp.where(keep, product[:, t * width:(t + 1) * width], 0.0).astype(jnp.bfloat16)
        key = keys[p]
        single = number[key] == 1

        @pl.when(single)
        def _():
            send(left_ref.at[p], key)

        @pl.when(jnp.logical_not(single))
        def _():
            fresh = seen[key] == 0

            @pl.when(fresh)
            def _():
                at_sum[key] = at_sum[slots]
                at_sum[slots] = at_sum[slots] + 1

            seen[key] = seen[key] + 1
            place = at_sum[key]

            @pl.loop(0, 2 * (modes // CHUNK))
            def _(r):
                t, rows = r % 2, pl.ds(pl.multiple_of(r // 2 * CHUNK, CHUNK), CHUNK)
                before = jnp.where(fresh, 0.0, sums[place, t, rows].astype(jnp.float32))
                sums[place, t, rows] = (before + left_ref[p, t, rows].astype(jnp.float32)).astype(jnp.bfloat16)

            @pl.when(seen[key] == number[key])
            def _():
                send(sums.at[place], key)

    @pl.loop(0, slots)
    def _(k):
        pltpu.make_async_copy(zero, outs[0].at[0], out_sem.at[k]).wait()


def in_hbm(value):
    return pltpu.with_memory_space_constraint(value, pltpu.HBM)


def left_products(own, coupling, partner, counts):
    pairs, blocks, width, _ = coupling.shape
    modes = own.shape[0]
    slots = SPAN_X + SPAN_Y
    sizes = [pairs] + [size for _, size in PARTS + RINGS]
    hbm, vmem = pltpu.HBM, pltpu.VMEM
    spaces = [vmem] + [hbm] * 4 + [vmem] * 2 + [hbm] * 4
    out = pl.pallas_call(
        left_kernel,
        in_specs=[pl.BlockSpec(memory_space=pltpu.HBM)] * 4,
        out_specs=[pl.BlockSpec(memory_space=space) for space in spaces],
        out_shape=[space((n, blocks, modes, width), jnp.bfloat16) for n, space in zip(sizes, spaces, strict=True)],
        scratch_shapes=[
            pltpu.SMEM((pairs,), jnp.int32),
            pltpu.SMEM((pairs,), jnp.int32),
            pltpu.VMEM((modes, width), jnp.bfloat16),
            pltpu.VMEM((pairs, width, blocks * width), jnp.bfloat16),
            pltpu.VMEM((blocks, modes, width), jnp.bfloat16),
            pltpu.VMEM((pairs // 2, blocks, modes, width), jnp.bfloat16),
            pltpu.SMEM((pairs,), jnp.int32),
            pltpu.SMEM((slots,), jnp.int32),
            pltpu.SMEM((slots,), jnp.int32),
            pltpu.SMEM((slots + 1,), jnp.int32),
            pltpu.SemaphoreType.DMA((pairs * blocks + 3,)),
            pltpu.SemaphoreType.DMA((slots,)),
        ],
        compiler_params=pltpu.CompilerParams(vmem_limit_bytes=12 * 2**20),
        cost_estimate=pl.CostEstimate(flops=2 * pairs * blocks * modes * width * width,
                                      bytes_accessed=25 * 10**6, transcendentals=0),
    )(*map(in_hbm, (partner, counts, own, coupling)))
    return out[0], out[1:8], out[8:11]


def nt(a, b):
    return lax.dot_general(a, b, (((1,), (1,)), ((), ())), preferred_element_type=jnp.float32)


def pair_kernel(partner_ref, left_ref, *rest):
    (kept, near, far, low, high, ring_mine, ring_other, across), out_hbm = rest[:8], rest[8]
    panels, outs, panel_sem, out_sem = rest[9:]
    pairs, count = panels.shape[0], outs.shape[0]

    def save(i):
        return pltpu.make_async_copy(outs.at[i], out_hbm.at[i // 2, i % 2], out_sem.at[i])

    @pl.loop(0, pairs)
    def _(q):
        code = partner_ref[q]
        d1, d2 = offsets(code)
        dz, core, me = ring_offset(code)
        step = jnp.where((dz == 1) | (dz == 3), jnp.where((dz == 3) == (core == 0), 1, 2), jnp.where(dz == 2, 3, 0))
        along = code < SPAN_X
        for ref, index, chosen in (
            (kept, d1, along & (d2 == 0)),
            (near, d1, along & (d2 == 1)),
            (far, d1, along & (d2 == 3)),
            (low, d1, along & (d2 == 2) & (d1 < 2)),
            (high, d1 - 2, along & (d2 == 2) & (d1 >= 2)),
            (ring_mine, step, (code >= SPAN_X) & (dz != 2) & (core == me)),
            (ring_other, step, (code >= SPAN_X) & (dz != 2) & (core != me)),
            (across, jnp.where(core == me, 0, 1), (code >= SPAN_X) & (dz == 2)),
        ):
            @pl.when(chosen)
            def _():
                pltpu.make_async_copy(ref.at[index], panels.at[q], panel_sem.at[q]).start()

    @pl.loop(0, pairs)
    def _(p):
        pltpu.make_async_copy(kept.at[0], panels.at[p], panel_sem.at[p]).wait()
        modes, width = panels.shape[1:]
        product = nt(left_ref[p].reshape(2 * modes, width), panels[p])
        for t in range(2):
            outs[2 * p + t] = product[t * modes:(t + 1) * modes].astype(jnp.bfloat16)
            save(2 * p + t).start()

    @pl.loop(0, count)
    def _(i):
        save(i).wait()


def pair_products(left, sources, partner):
    pairs, blocks, modes, width = left.shape
    hbm, smem = pl.BlockSpec(memory_space=pltpu.HBM), pl.BlockSpec(memory_space=pltpu.SMEM)
    return pl.pallas_call(
        pair_kernel,
        in_specs=[smem, pl.BlockSpec(memory_space=pltpu.VMEM)] + [pl.BlockSpec(memory_space=pl.ANY)] * 8,
        out_specs=hbm,
        out_shape=jax.ShapeDtypeStruct((pairs, blocks, modes, modes), jnp.bfloat16),
        scratch_shapes=[
            pltpu.VMEM((pairs, modes, width), jnp.bfloat16),
            pltpu.VMEM((pairs * blocks, modes, modes), jnp.bfloat16),
            pltpu.SemaphoreType.DMA((pairs,)),
            pltpu.SemaphoreType.DMA((pairs * blocks,)),
        ],
        compiler_params=pltpu.CompilerParams(vmem_limit_bytes=14 * 2**20),
        cost_estimate=pl.CostEstimate(flops=2 * pairs * blocks * modes * width * modes,
                                      bytes_accessed=15 * 10**6, transcendentals=0),
    )(partner, left, *sources)


def partner_kernel(own_ref, sum_ref, *rest):
    last, out_ref = rest[:-1], rest[-1]

    @pl.loop(0, out_ref.shape[0])
    def _(t):
        total = sum_ref[t]
        for ref in last:
            total = total + ref[t].astype(jnp.float32)
        out_ref[t] = nt(own_ref[...], total.astype(jnp.bfloat16))


def partner_products(own, start, last):
    modes, _ = own.shape
    blocks = start.shape[0]
    return pl.pallas_call(
        partner_kernel,
        out_shape=jax.ShapeDtypeStruct((blocks, modes, modes), jnp.float32),
        compiler_params=pltpu.CompilerParams(vmem_limit_bytes=16 * 2**20),
    )(own, start, *last)


def permuted(value, move):
    pairs = []
    for n in range(SPAN_X * SPAN_Y):
        here = (n // SPAN_Y // SIDE, n // SPAN_Y % SIDE, n % SPAN_Y // 2, n % 2)
        x, y, z, c = move(*here)
        pairs.append((n, ((x % SIDE) * SIDE + y % SIDE) * SPAN_Y + (z % SIDE) * 2 + c))
    return lax.ppermute(value, ("sx", "sy"), pairs)


def first(value, by):
    return permuted(value, lambda x, y, z, c: (x + by, y, z, c) if c == 0 else (x, y + by, z, c))


def second(value, by):
    return permuted(value, lambda x, y, z, c: (x, y + by, z, c) if c == 0 else (x + by, y, z, c))


def turn(value, by):
    return permuted(value, lambda x, y, z, c: (x, y, z + (by if c == 0 else -by), c))


def swap(value):
    return permuted(value, lambda x, y, z, c: (x, y, z, 1 - c))


def added(*terms):
    return sum(v.astype(jnp.float32) for v in terms)


def rounded(*terms):
    return added(*terms).astype(jnp.bfloat16)


def after(value, *others):
    return lax.optimization_barrier((value,) + others)[0]


def body(panels, coupling, partner, counts):
    own = jnp.swapaxes(panels[0], 0, 1)
    barrier = lax.optimization_barrier

    moved = [first(own, -1), first(own, 2), first(own, 1)]
    ring1, ring2 = turn(own, 1), turn(own, -1)
    kept = jnp.stack([own] + moved)
    kept = barrier(kept)
    near, far = second(kept, -1), second(kept, 1)
    left, (up, up_end, down, down_end, pass_up, pass_down, here), (z_near, z_far, z_mine) = left_products(
        own, coupling, partner, after(counts, kept)
    )

    got_up, got_down = first(up, 1), first(down, -1)
    up_end, down_end, z_far, near, far = barrier((up_end, down_end, z_far, near, far))
    end_up, end_down = first(up_end, 1), first(down_end, -1)
    last_up, last_down = first(rounded(pass_up, got_up), 1), first(rounded(pass_down, got_down), -1)

    ring_mine = jnp.stack([own, ring1, ring2])
    ring_other = swap(after(ring_mine, up))
    far_sum = swap(z_far)
    across = turn(jnp.stack([ring2, ring_other[1]]), -1)
    near_sum = swap(after(z_near, ring_other))
    w = [rounded(z_mine[k], (near_sum, far_sum)[k // 2][k % 2]) for k in range(SIDE)]

    near, far, w3, end_up, end_down = barrier((near, far, w[3], end_up, end_down))
    low, high = second(near[:2], -1), second(far[2:], 1)
    opposite = turn(w3, 1)
    low, high, opposite, across, ring_other, w = barrier((low, high, opposite, across, ring_other, w))
    z_last = turn(rounded(w[1], opposite), 1)

    v = [
        rounded(here[0], end_down[0], last_up[0]),
        rounded(here[1], end_down[1], last_up[1]),
        rounded(here[2], end_up[0], last_down[0]),
        rounded(here[3], end_up[1], last_down[1]),
    ]
    v, w2 = barrier((v, w[2]))
    back = turn(after(w2, z_last), -1)
    ends = [second(v[1], 1), second(v[3], -1), second(v[2], 2)]

    sources = [kept, near, far, low, high, ring_mine, ring_other, across]
    pair_blocks = pair_products(left, sources, after(partner, *v, z_last))
    pair_blocks, ends = barrier((pair_blocks, ends))
    partner_blocks = partner_products(own, added(v[0], w[0], back, z_last), ends)
    return (pair_blocks, partner_blocks[None])


def solution(mesh):
    placed = (
        P(("sx", "sy"), None, None),
        P(("sx", "sy"), None, None, None),
        P(("sx", "sy")),
        P(("sx", "sy")),
    )
    return jax.shard_map(
        body,
        mesh=mesh,
        in_specs=placed,
        out_specs=(P(("sx", "sy"), None, None, None), P(("sx", "sy"), None, None, None)),
        check_vma=False,
    )
```
